32 devices in a mesh: group: 16 (over z, y, core), head: 2 (over x).
Axes of the slice: x: 2, y: 2, z: 4, core: 2. Of those that a mesh axis runs over, the one named last changes fastest.
Arguments:
- kv_pool: bfloat16 [512, 128, 2048], P('group', None, 'head'), may hold values from -6 to 6
- lengths: int32 [256], replicated, may hold values from 1 to 256, as said below
- prefill_of: int32 [256], replicated, may hold values from 0 to 15, as said below
- decode_of: int32 [256], replicated, may hold values from 0 to 15, as said below
- row_request: int32 [256], replicated, may hold values from 0 to 255, as said below
- queries: bfloat16 [256, 8192], P('group', 'head'), may hold values from -6 to 6
- out_weight: bfloat16 [8192, 8192], P('head', 'group'), may hold values from -0.0625 to 0.0625
Outputs:
- received: bfloat16 [512, 128, 2048], P('group', None, 'head')
- output: bfloat16 [256, 8192], P('head', 'group')
The draws below stay inside these ranges and needn't reach their ends.
Inputs may be any that keep to these rules, and one draw needn't show every extreme that they name: `lengths`: every prefill group has a request of 256 tokens. `prefill_of`: each prefill group holds exactly 16 requests. `decode_of`: no two requests of one prefill group have the same decode group; every decode group receives at least one request. `row_request`: row b's request has decode group b // 16.
All inputs are finite; a program needn't handle non-finite values.
Results may differ from the reference program's by a relative error of at most 0.009.
Values may be sent and summed in bfloat16 or wider, within the bound.
No kernel may reach another device: no remote copies, remote signals or barrier semaphores. Data moves between devices by JAX's collectives and lax.ppermute only.
A program may use at most 128 MiB of HBM per device.

```python
import math
import jax
import jax.numpy as jnp
from jax import lax

D = 8192
QH = 64
KVH = 8
HD = 128
PAGE = 128
MAX_PAGES = 2
REQ_DEV = 16
ROWS_DEV = 16
REQS = 256
PAGES = 512
ROWS = 256
N_GROUP = 16


def layout(key):
    groups = N_GROUP
    request_total = REQ_DEV * groups
    target = jax.random.randint(jax.random.fold_in(key, 11), (), 0, groups)
    row_keys = jax.random.split(jax.random.fold_in(key, 12), groups)
    shuffles = jax.vmap(lambda one_key: jax.random.permutation(one_key, groups))(row_keys).astype(jnp.int32)
    column = jnp.arange(groups, dtype=jnp.int32)[None, :]
    own_group = jnp.arange(groups, dtype=jnp.int32)[:, None]
    ranking = jnp.where(column == own_group, -2, jnp.where(column == target, -1, shuffles))
    destination = jnp.argsort(ranking, axis=1, stable=True)[:, :REQ_DEV].astype(jnp.int32)
    longest = MAX_PAGES * PAGE
    drawn_lengths = jax.random.randint(jax.random.fold_in(key, 13), (groups, REQ_DEV), 1, longest + 1)
    drawn_lengths = jnp.where(destination == target, longest, drawn_lengths).astype(jnp.int32)
    shuffle = jax.random.permutation(jax.random.fold_in(key, 14), request_total).astype(jnp.int32)
    source = jnp.repeat(jnp.arange(groups, dtype=jnp.int32), REQ_DEV)
    lengths = jnp.zeros((request_total,), jnp.int32).at[shuffle].set(drawn_lengths.reshape(-1))
    prefill = jnp.zeros((request_total,), jnp.int32).at[shuffle].set(source)
    decode = jnp.zeros((request_total,), jnp.int32).at[shuffle].set(destination.reshape(-1))
    row_total = ROWS_DEV * groups
    row_group = jnp.arange(row_total, dtype=jnp.int32) // ROWS_DEV
    member = decode[None, :] == row_group[:, None]
    members = jnp.sum(member.astype(jnp.int32), axis=1)
    chosen_rank = jax.random.randint(jax.random.fold_in(key, 15), (row_total,), 0, members)
    running = jnp.cumsum(member.astype(jnp.int32), axis=1)
    ordinal = jnp.arange(request_total, dtype=jnp.int32)[None, :]
    chosen = jnp.sum(jnp.where(member & (running == chosen_rank[:, None] + 1), ordinal, 0), axis=1)
    return (lengths, prefill, decode, chosen.astype(jnp.int32))


def draw_lengths(key, part):
    tables = layout(key)
    return tables[0]


def draw_prefill_of(key, part):
    tables = layout(key)
    return tables[1]


def draw_decode_of(key, part):
    tables = layout(key)
    return tables[2]


def draw_row_request(key, part):
    tables = layout(key)
    return tables[3]


def draw_kv_pool(key, part):
    key = jax.random.fold_in(key, 31)
    values_drawn = jax.random.truncated_normal(key, -6.0, 6.0, (PAGES, PAGE, KVH * 2 * HD), jnp.float32)
    return values_drawn.astype(jnp.bfloat16)


def draw_queries(key, part):
    key = jax.random.fold_in(key, 32)
    values_drawn = jax.random.truncated_normal(key, -6.0, 6.0, (ROWS, QH * HD), jnp.float32)
    return values_drawn.astype(jnp.bfloat16)


def level_of(stream_key, shape, pieces, low, top_value):
    factor_of = 1.0
    for dim, blocks in pieces:
        draws = jax.random.uniform(jax.random.fold_in(jax.random.fold_in(stream_key, 6), dim), (blocks,), jnp.float32, low / len(pieces), top_value / len(pieces))
        factor_of = factor_of * jnp.repeat(jnp.exp(draws), shape[dim] // blocks).reshape((-1,) + (1,) * (len(shape) - 1 - dim))
    return factor_of


def scatter_about(key, shape, width, limit, cuts=(), kind=jnp.bfloat16):
    drawn = jax.random.normal(key, shape, jnp.float32) * width
    if len(cuts) > 0:
        drawn = level_of(key, shape, cuts, -0.22, 0.18) * drawn
    return jnp.clip(drawn, min=-limit, max=limit).astype(kind)


def setup_inputs(seed: int = 0) -> dict:
    streams_of = jax.random.split(jax.random.key(seed), 8)
    return {
        "kv_pool": draw_kv_pool(jax.random.fold_in(streams_of[7], 71), 0),
        "lengths": draw_lengths(jax.random.fold_in(streams_of[7], 71), 0),
        "prefill_of": draw_prefill_of(jax.random.fold_in(streams_of[7], 71), 0),
        "decode_of": draw_decode_of(jax.random.fold_in(streams_of[7], 71), 0),
        "row_request": draw_row_request(jax.random.fold_in(streams_of[7], 71), 0),
        "queries": draw_queries(jax.random.fold_in(streams_of[7], 71), 0),
        "out_weight": scatter_about(streams_of[6], (QH * HD, D), (QH * HD) ** -0.5, 0.0625, ((0, 2), (1, 16))),
    }


def reference(kv_pool, lengths, prefill_of, decode_of, row_request, queries, out_weight):
    groups = N_GROUP
    per_group = REQ_DEV * MAX_PAGES
    page_count = ((lengths + PAGE - 1) // PAGE).astype(jnp.int32)
    ordinal = jnp.arange(REQS, dtype=jnp.int32)
    same_group = (prefill_of[None, :] == prefill_of[:, None]) & (ordinal[None, :] < ordinal[:, None])
    page_start = lax.optimization_barrier(jnp.sum(jnp.where(same_group, page_count[None, :], 0), axis=1)).astype(jnp.int32)
    request_id = jnp.zeros((groups, groups), jnp.int32).at[decode_of, prefill_of].set(ordinal)
    present = jnp.zeros((groups, groups), jnp.int32).at[decode_of, prefill_of].set(1)
    slot_index = jnp.arange(MAX_PAGES, dtype=jnp.int32)
    sources = jnp.arange(groups, dtype=jnp.int32)
    page_index = sources[None, :, None] * per_group + page_start[request_id][:, :, None] + slot_index[None, None, :]
    filled = (present[:, :, None] == 1) & (slot_index[None, None, :] < page_count[request_id][:, :, None])
    page_index = jnp.where(filled, page_index, 0).astype(jnp.int32)
    received = jnp.where(filled[..., None, None], kv_pool[page_index], jnp.zeros((), kv_pool.dtype))
    received = received.reshape(groups * groups * MAX_PAGES, PAGE, KVH * 2 * HD)
    scaling = 1.0 / math.sqrt(HD)

    def one_row(row_args):
        request, query = row_args
        pages_of_row = prefill_of[request] * per_group + page_start[request] + slot_index
        pages_of_row = jnp.minimum(pages_of_row, PAGES - 1).astype(jnp.int32)
        cache = kv_pool[pages_of_row].reshape(MAX_PAGES * PAGE, KVH, 2, HD).astype(jnp.float32)
        query_heads = query.reshape(KVH, QH // KVH, HD).astype(jnp.float32)
        score = jnp.einsum('hgd,thd->hgt', query_heads, cache[:, :, 0, :]) * scaling
        live_tokens = jnp.arange(MAX_PAGES * PAGE, dtype=jnp.int32) < lengths[request]
        masked = jnp.where(live_tokens, score, -1e+30)
        highest = lax.optimization_barrier(jnp.max(masked, axis=-1, keepdims=True))
        weights = jnp.where(live_tokens, jnp.exp(masked - highest), 0.0)
        totals = lax.optimization_barrier(jnp.sum(weights, axis=-1))
        rounded = lax.optimization_barrier(weights.astype(jnp.bfloat16)).astype(jnp.float32)
        mixture = jnp.einsum('hgt,thd->hgd', rounded, cache[:, :, 1, :]) / totals[..., None]
        return mixture.reshape(QH * HD).astype(jnp.bfloat16)
    attended = lax.map(one_row, (row_request, queries))
    output = jnp.dot(attended, out_weight, preferred_element_type=jnp.float32).astype(jnp.bfloat16)
    return (received, output)
```

```python
import functools
import itertools
import math

import jax
import jax.numpy as jnp
from jax import lax
from jax.experimental import pallas as pl
from jax.experimental.pallas import tpu as pltpu
from jax.sharding import PartitionSpec as P

HD = 128
MAX_PAGES = 2
CAPACITY = 32
ROW_UNROLL = 4
VMEM_LIMIT = 48 * 1024 * 1024


def factors(groups):
    if groups % 4 == 0:
        return (groups // 4, 2, 2)
    return (groups,)


def strides(dims):
    return tuple(math.prod(dims[i + 1 :]) for i in range(len(dims)))


def shifted(index, offset, dims):
    result = 0
    for size, stride, ahead in zip(dims, strides(dims), offset):
        result = result + lax.rem(index // stride % size + ahead + size, size) * stride
    return result


def shifted_static(index, offset, dims):
    result = 0
    for size, stride, ahead in zip(dims, strides(dims), offset):
        result += (index // stride % size + ahead) % size * stride
    return result


def send_by(array, offset, dims):
    groups = math.prod(dims)
    pairs = [(s, shifted_static(s, offset, dims)) for s in range(groups)]
    return lax.ppermute(array, "group", pairs)


def gather_shards(shard, dims):
    held = {(0,) * len(dims): shard}
    for axis, size in enumerate(dims):
        incoming = {}
        for ahead in range(1, size):
            step = tuple(ahead if i == axis else 0 for i in range(len(dims)))
            for offset, array in held.items():
                place = tuple(a + b for a, b in zip(offset, step))
                incoming[place] = send_by(array, step, dims)
        held.update(incoming)
    return held


def offset_rank(offset, dims):
    return sum(o * s for o, s in zip(offset, strides(dims)))


def behind_rank(me, other, dims):
    rank = 0
    for size, stride in zip(dims, strides(dims)):
        rank = rank + lax.rem(me // stride % size - other // stride % size + size, size) * stride
    return rank


def prepare_kernel(dims, offsets, lengths, prefill_of, decode_of, pool, received, *rest):
    sends = rest[: len(offsets)]
    zero_page, start_of, count_of, zero_sem, sems = rest[len(offsets) :]
    me = lax.axis_index("group")
    page_size = pool.shape[1]
    for d in range(math.prod(dims)):
        start_of[d] = 0
        count_of[d] = 0
    start_of[math.prod(dims)] = 0
    count_of[math.prod(dims)] = 0
    zero_page[...] = jnp.zeros_like(zero_page)

    def visit(r, running):
        mine = prefill_of[r] == me
        count = (lengths[r] + page_size - 1) // page_size
        place = jnp.where(mine, decode_of[r], math.prod(dims))
        start_of[place] = running
        count_of[place] = count
        return running + jnp.where(mine, count, 0)

    lax.fori_loop(0, lengths.shape[0], visit, jnp.int32(0), unroll=8)

    def fill(target, page, start, count, sem):
        @pl.when(page < count)
        def _():
            pltpu.make_async_copy(pool.at[start + page], target, sem).start()

        @pl.when(page >= count)
        def _():
            pltpu.make_async_copy(zero_page, target, sem).start()

    own = start_of[me], count_of[me]
    for page in range(MAX_PAGES):
        fill(received.at[me * MAX_PAGES + page], page, *own, zero_sem.at[page])
    for i, offset in enumerate(offsets):
        to = shifted(me, offset, dims)
        start, count = start_of[to], count_of[to]
        for page in range(MAX_PAGES):
            fill(sends[i].at[page], page, start, count, sems.at[i, page])
    for page in range(MAX_PAGES):
        pltpu.make_async_copy(zero_page, received.at[page], zero_sem.at[page]).wait()
    for i in range(len(offsets)):
        for page in range(MAX_PAGES):
            pltpu.make_async_copy(zero_page, sends[i].at[page], sems.at[i, page]).wait()


def prepare(dims, offsets, lengths, prefill_of, decode_of, pool):
    groups = math.prod(dims)
    page = pool.shape[1:]
    block = jax.ShapeDtypeStruct((MAX_PAGES,) + page, pool.dtype)
    outs = [jax.ShapeDtypeStruct((groups * MAX_PAGES,) + page, pool.dtype)] + [block] * len(offsets)
    smem = pl.BlockSpec(memory_space=pltpu.SMEM)
    hbm = pl.BlockSpec(memory_space=pl.ANY)
    return pl.pallas_call(
        functools.partial(prepare_kernel, dims, offsets),
        out_shape=outs,
        in_specs=[smem, smem, smem, hbm],
        out_specs=[hbm] * len(outs),
        scratch_shapes=[
            pltpu.VMEM(page, pool.dtype),
            pltpu.SMEM((groups + 1,), jnp.int32),
            pltpu.SMEM((groups + 1,), jnp.int32),
            pltpu.SemaphoreType.DMA((MAX_PAGES,)),
            pltpu.SemaphoreType.DMA((len(offsets), MAX_PAGES)),
        ],
        compiler_params=pltpu.CompilerParams(vmem_limit_bytes=VMEM_LIMIT),
        cost_estimate=pl.CostEstimate(flops=0, bytes_accessed=4 * pool.size, transcendentals=0),
        name="outgoing_pages",
    )(lengths, prefill_of, decode_of, pool)


def place_kernel(dims, offsets, received_in, *rest):
    blocks = rest[: len(offsets)]
    received, sems = rest[len(offsets) :]
    me = lax.axis_index("group")
    copies = []
    for i, offset in enumerate(offsets):
        source = shifted(me, tuple(-o for o in offset), dims)
        copies.append(
            pltpu.make_async_copy(
                blocks[i], received.at[pl.ds(source * MAX_PAGES, MAX_PAGES)], sems.at[i]
            )
        )
        copies[-1].start()
    for copy in copies:
        copy.wait()


def place(dims, offsets, received, blocks):
    hbm = pl.BlockSpec(memory_space=pl.ANY)
    return pl.pallas_call(
        functools.partial(place_kernel, dims, offsets),
        out_shape=jax.ShapeDtypeStruct(received.shape, received.dtype),
        in_specs=[hbm] * (1 + len(blocks)),
        out_specs=hbm,
        scratch_shapes=[pltpu.SemaphoreType.DMA((len(blocks),))],
        input_output_aliases={0: 0},
        compiler_params=pltpu.CompilerParams(vmem_limit_bytes=VMEM_LIMIT),
        cost_estimate=pl.CostEstimate(
            flops=0, bytes_accessed=4 * sum(b.size for b in blocks), transcendentals=0
        ),
        name="place_pages",
    )(received, *blocks)


def attend_kernel(dims, offsets, lengths, prefill_of, row_request, pool, *rest):
    shards = rest[: len(offsets)]
    out, queries, start_of, mine_rows, sems = rest[len(offsets) :]
    me = lax.axis_index("group")
    page_total, page_size, width = pool.shape
    row_local, query_heads = queries.shape[1:3]
    row_total = row_request.shape[0]
    kv_heads = width // (2 * HD)
    share = query_heads // kv_heads
    copies = []
    for i, offset in enumerate(offsets):
        copies.append(
            pltpu.make_async_copy(shards[i], queries.at[offset_rank(offset, dims)], sems.at[i])
        )
        copies[-1].start()
    out[...] = jnp.zeros_like(out)

    def visit(r, running):
        start_of[r] = running
        count = (lengths[r] + page_size - 1) // page_size
        return running + jnp.where(prefill_of[r] == me, count, 0)

    lax.fori_loop(0, lengths.shape[0], visit, jnp.int32(0), unroll=8)
    for i in range(ROW_UNROLL):
        mine_rows[i] = 0

    def collect(b, held):
        mine_rows[held] = b
        return held + jnp.where(prefill_of[row_request[b]] == me, 1, 0)

    row_count = lax.fori_loop(0, row_total, collect, jnp.int32(0), unroll=8)
    for i in range(ROW_UNROLL):
        mine_rows[row_count + i] = 0
    for copy in copies:
        copy.wait()
    scaling = 1.0 / math.sqrt(HD)

    def one_row(place):
        row = mine_rows[place]
        request = row_request[row]
        first = jnp.minimum(start_of[request], page_total - 1)
        second = jnp.minimum(first + 1, page_total - 1)
        length = lengths[request]
        from_rank = behind_rank(me, row // row_local, dims)
        query = queries[from_rank, lax.rem(row, row_local)]
        scores = []
        for h in range(kv_heads):
            columns = slice(2 * h * HD, (2 * h + 1) * HD)
            keys = jnp.concatenate([pool[first, :, columns], pool[second, :, columns]], axis=0)
            every = lax.dot_general(
                query, keys, (((1,), (1,)), ((), ())), preferred_element_type=jnp.float32
            )
            scores.append(every[h * share : (h + 1) * share])
        score = jnp.concatenate(scores, axis=0) * scaling
        token = lax.broadcasted_iota(jnp.int32, score.shape, 1)
        live = token < length
        masked = jnp.where(live, score, -1e30)
        highest = jnp.max(masked, axis=1, keepdims=True)
        weights = jnp.where(live, jnp.exp(masked - highest), 0.0)
        totals = jnp.sum(weights, axis=1, keepdims=True)
        rounded = weights.astype(jnp.bfloat16)
        mixtures = []
        for h in range(kv_heads):
            columns = slice((2 * h + 1) * HD, (2 * h + 2) * HD)
            values = jnp.concatenate([pool[first, :, columns], pool[second, :, columns]], axis=0)
            every = jnp.dot(rounded, values, preferred_element_type=jnp.float32)
            mixtures.append(every[h * share : (h + 1) * share])
        mixture = jnp.concatenate(mixtures, axis=0) / totals
        return mixture.astype(jnp.bfloat16)

    @pl.loop(0, (row_count + ROW_UNROLL - 1) // ROW_UNROLL)
    def _(step):
        for i in range(ROW_UNROLL):
            out[step * ROW_UNROLL + i] = one_row(step * ROW_UNROLL + i)


def attend(dims, shards, lengths, prefill_of, row_request, pool):
    offsets = list(shards)
    row_local, query_heads, _ = shards[offsets[0]].shape
    row_total = row_request.shape[0]
    smem = pl.BlockSpec(memory_space=pltpu.SMEM)
    vmem = pl.BlockSpec(memory_space=pltpu.VMEM)
    hbm = pl.BlockSpec(memory_space=pl.ANY)
    return pl.pallas_call(
        functools.partial(attend_kernel, dims, offsets),
        out_shape=jax.ShapeDtypeStruct((row_total + ROW_UNROLL, query_heads, HD), jnp.bfloat16),
        in_specs=[smem, smem, smem, vmem] + [hbm] * len(offsets),
        out_specs=vmem,
        scratch_shapes=[
            pltpu.VMEM((len(offsets), row_local, query_heads, HD), jnp.bfloat16),
            pltpu.SMEM((lengths.shape[0],), jnp.int32),
            pltpu.SMEM((row_total + ROW_UNROLL,), jnp.int32),
            pltpu.SemaphoreType.DMA((len(offsets),)),
        ],
        compiler_params=pltpu.CompilerParams(vmem_limit_bytes=VMEM_LIMIT),
        cost_estimate=pl.CostEstimate(
            flops=1 << 33, bytes_accessed=2 * pool.size, transcendentals=1 << 20
        ),
        name="attend_local_rows",
    )(lengths, prefill_of, row_request, pool, *(shards[o] for o in offsets))


def local(dims, kv_pool, lengths, prefill_of, decode_of, row_request, queries, out_weight):
    groups = math.prod(dims)
    me = lax.axis_index("group")
    row_local, query_width = queries.shape
    row_total = row_request.shape[0]
    query_heads = query_width // HD
    offsets = [o for o in itertools.product(*(range(n) for n in dims)) if any(o)]

    received, *sends = prepare(dims, offsets, lengths, prefill_of, decode_of, kv_pool)
    arrived = [send_by(block, offset, dims) for block, offset in zip(sends, offsets)]

    shards = gather_shards(queries.reshape(row_local, query_heads, HD), dims)
    rows = attend(dims, shards, lengths, prefill_of, row_request, kv_pool)
    rows = rows.reshape(rows.shape[0], query_width)

    row_home = prefill_of[row_request]
    ordinal = jnp.arange(row_total, dtype=jnp.int32)
    earlier = (row_home[None, :] == row_home[:, None]) & (ordinal[None, :] < ordinal[:, None])
    row_rank = jnp.sum(earlier.astype(jnp.int32), axis=1)
    home_slot = behind_rank(me, row_home, dims) * CAPACITY

    def gather_round(done):
        gathered = gather_shards(lax.dynamic_slice_in_dim(rows, done, CAPACITY), dims)
        stacked = jnp.concatenate(
            [gathered[o] for o in sorted(gathered, key=lambda o: offset_rank(o, dims))], axis=0
        )
        inside = (row_rank >= done) & (row_rank < done + CAPACITY)
        slot = jnp.where(inside, home_slot + row_rank - done, -1)
        chosen = slot[:, None] == jnp.arange(stacked.shape[0], dtype=jnp.int32)[None, :]
        return jnp.dot(
            chosen.astype(jnp.bfloat16), stacked, preferred_element_type=jnp.float32
        ).astype(jnp.bfloat16)

    most = jnp.max(row_rank) + 1
    attended = gather_round(jnp.int32(0))
    _, attended = lax.while_loop(
        lambda state: state[0] < most,
        lambda state: (state[0] + CAPACITY, state[1] + gather_round(state[0])),
        (jnp.int32(CAPACITY), attended),
    )
    product = jnp.dot(attended, out_weight, preferred_element_type=jnp.float32)

    heads = lax.axis_size("head")
    my_head = lax.axis_index("head")
    share = row_total // heads
    output = lax.dynamic_slice_in_dim(product, my_head * share, share)
    for ahead in range(1, heads):
        theirs = lax.dynamic_slice_in_dim(product, lax.rem(my_head + ahead, heads) * share, share)
        pairs = [(h, (h + ahead) % heads) for h in range(heads)]
        output = output + lax.ppermute(theirs.astype(jnp.bfloat16), "head", pairs).astype(jnp.float32)

    received = place(dims, offsets, received, arrived)
    return (received, output.astype(jnp.bfloat16))


def solution(mesh):
    in_specs = (
        P("group", None, "head"),
        P(),
        P(),
        P(),
        P(),
        P("group", "head"),
        P("head", "group"),
    )
    out_specs = (P("group", None, "head"), P("head", "group"))
    body = functools.partial(local, factors(mesh.shape["group"]))
    return jax.shard_map(body, mesh=mesh, in_specs=in_specs, out_specs=out_specs, check_vma=False)
```

```python
import functools
import itertools
import math

import jax
import jax.numpy as jnp
from jax import lax
from jax.experimental import pallas as pl
from jax.experimental.pallas import tpu as pltpu
from jax.sharding import PartitionSpec as P

HD = 128
MAX_PAGES = 2
CAPACITY = 32
ROW_UNROLL = 4
VMEM_LIMIT = 48 * 1024 * 1024


def factors(groups):
    if groups % 4 == 0:
        return (groups // 4, 2, 2)
    return (groups,)


def strides(dims):
    return tuple(math.prod(dims[i + 1 :]) for i in range(len(dims)))


def shifted(index, offset, dims):
    result = 0
    for size, stride, ahead in zip(dims, strides(dims), offset):
        result = result + lax.rem(index // stride % size + ahead + size, size) * stride
    return result


def shifted_static(index, offset, dims):
    result = 0
    for size, stride, ahead in zip(dims, strides(dims), offset):
        result += (index // stride % size + ahead) % size * stride
    return result


def send_by(array, offset, dims):
    groups = math.prod(dims)
    pairs = [(s, shifted_static(s, offset, dims)) for s in range(groups)]
    return lax.ppermute(array, "group", pairs)


def along(axis, step, dims):
    return tuple(step if i == axis else 0 for i in range(len(dims)))


def relay(array, axis, step, dims):
    groups, size, stride = math.prod(dims), dims[axis], strides(dims)[axis]
    pairs = [(s, s + step * stride) for s in range(groups) if 0 <= s // stride % size + step < size]
    return lax.ppermute(array, "group", pairs)


def gather_shards(shard, dims):
    held = {(0,) * len(dims): shard}
    me = lax.axis_index("group")
    for axis, size in enumerate(dims):
        digit = me // strides(dims)[axis] % size
        incoming = {}
        for offset, array in held.items():
            if size == 2:
                passed = {1: send_by(array, along(axis, 1, dims), dims)}
            else:
                up, down = [array], [array]
                for _ in range(1, size):
                    up.append(relay(up[-1], axis, 1, dims))
                    down.append(relay(down[-1], axis, -1, dims))
                passed = {k: jnp.where(digit >= k, up[k], down[size - k]) for k in range(1, size)}
            for k, moved in passed.items():
                incoming[tuple(a + b for a, b in zip(offset, along(axis, k, dims)))] = moved
        held.update(incoming)
    return held


def offset_rank(offset, dims):
    return sum(o * s for o, s in zip(offset, strides(dims)))


def behind_rank(me, other, dims):
    rank = 0
    for size, stride in zip(dims, strides(dims)):
        rank = rank + lax.rem(me // stride % size - other // stride % size + size, size) * stride
    return rank


def prepare_kernel(groups, lengths, prefill_of, decode_of, pool, sends, held, zero_page, start_of, count_of, in_sems, out_sem):
    me = lax.axis_index("group")
    page_total, page_size, _ = pool.shape
    loads = [pltpu.make_async_copy(pool.at[p], held.at[p], in_sems.at[p]) for p in range(page_total)]
    for load in loads:
        load.start()
    for d in range(groups + 1):
        start_of[d] = 0
        count_of[d] = 0
    zero_page[...] = jnp.zeros_like(zero_page)

    def visit(r, running):
        mine = prefill_of[r] == me
        count = (lengths[r] + page_size - 1) // page_size
        to = jnp.where(mine, decode_of[r], groups)
        start_of[to] = running
        count_of[to] = count
        return running + jnp.where(mine, count, 0)

    lax.fori_loop(0, lengths.shape[0], visit, jnp.int32(0), unroll=8)
    for load in loads:
        load.wait()

    def store(d, page, do):
        target = sends.at[d, page]

        @pl.when(page < count_of[d])
        def _():
            do(pltpu.make_async_copy(held.at[start_of[d] + page], target, out_sem))

        @pl.when(page >= count_of[d])
        def _():
            do(pltpu.make_async_copy(zero_page, target, out_sem))

    for d in range(groups):
        for page in range(MAX_PAGES):
            store(d, page, lambda copy: copy.start())
    for d in range(groups):
        for page in range(MAX_PAGES):
            store(d, page, lambda copy: copy.wait())


def prepare(groups, lengths, prefill_of, decode_of, pool):
    page = pool.shape[1:]
    smem = pl.BlockSpec(memory_space=pltpu.SMEM)
    hbm = pl.BlockSpec(memory_space=pl.ANY)
    return pl.pallas_call(
        functools.partial(prepare_kernel, groups),
        out_shape=jax.ShapeDtypeStruct((groups, MAX_PAGES) + page, pool.dtype),
        in_specs=[smem, smem, smem, hbm],
        out_specs=hbm,
        scratch_shapes=[
            pltpu.VMEM(pool.shape, pool.dtype),
            pltpu.VMEM(page, pool.dtype),
            pltpu.SMEM((groups + 1,), jnp.int32),
            pltpu.SMEM((groups + 1,), jnp.int32),
            pltpu.SemaphoreType.DMA((pool.shape[0],)),
            pltpu.SemaphoreType.DMA,
        ],
        compiler_params=pltpu.CompilerParams(vmem_limit_bytes=VMEM_LIMIT),
        cost_estimate=pl.CostEstimate(flops=0, bytes_accessed=4 * pool.size, transcendentals=0),
        name="outgoing_pages",
    )(lengths, prefill_of, decode_of, pool)


def hand_on_kernel(blocks, arrived, after, received, held, in_sems, out_sems):
    step = arrived.shape[0] // blocks
    loads, stores = [], []
    for i in range(blocks):
        part = pl.ds(i * step, step)
        loads.append(pltpu.make_async_copy(arrived.at[part], held.at[part], in_sems.at[i]))
        stores.append(pltpu.make_async_copy(held.at[part], received.at[part], out_sems.at[i]))
        loads[-1].start()
    for load, store in zip(loads, stores):
        load.wait()
        store.start()
    for store in stores:
        store.wait()


def hand_on(arrived, after):
    hbm = pl.BlockSpec(memory_space=pl.ANY)
    blocks = math.gcd(arrived.shape[0], 16)
    return pl.pallas_call(
        functools.partial(hand_on_kernel, blocks),
        out_shape=jax.ShapeDtypeStruct(arrived.shape, arrived.dtype),
        in_specs=[hbm, hbm],
        out_specs=hbm,
        scratch_shapes=[
            pltpu.VMEM(arrived.shape, arrived.dtype),
            pltpu.SemaphoreType.DMA((blocks,)),
            pltpu.SemaphoreType.DMA((blocks,)),
        ],
        compiler_params=pltpu.CompilerParams(vmem_limit_bytes=VMEM_LIMIT),
        cost_estimate=pl.CostEstimate(flops=0, bytes_accessed=4 * arrived.size, transcendentals=0),
        name="place_pages",
    )(arrived, after)


def attend_kernel(dims, offsets, lengths, prefill_of, row_request, pool, after, *rest):
    shards = rest[: len(offsets)]
    out, queries, start_of, mine_rows, sems = rest[len(offsets) :]
    me = lax.axis_index("group")
    page_total, page_size, width = pool.shape
    row_local, query_heads = queries.shape[1:3]
    row_total = row_request.shape[0]
    kv_heads = width // (2 * HD)
    share = query_heads // kv_heads
    copies = []
    for i, offset in enumerate(offsets):
        copies.append(
            pltpu.make_async_copy(shards[i], queries.at[offset_rank(offset, dims)], sems.at[i])
        )
        copies[-1].start()
    out[...] = jnp.zeros_like(out)

    def visit(r, running):
        start_of[r] = running
        count = (lengths[r] + page_size - 1) // page_size
        return running + jnp.where(prefill_of[r] == me, count, 0)

    lax.fori_loop(0, lengths.shape[0], visit, jnp.int32(0), unroll=8)
    for i in range(ROW_UNROLL):
        mine_rows[i] = 0

    def collect(b, held):
        mine_rows[held] = b
        return held + jnp.where(prefill_of[row_request[b]] == me, 1, 0)

    row_count = lax.fori_loop(0, row_total, collect, jnp.int32(0), unroll=8)
    for i in range(ROW_UNROLL):
        mine_rows[row_count + i] = 0
    for copy in copies:
        copy.wait()
    scaling = 1.0 / math.sqrt(HD)

    def one_row(place):
        row = mine_rows[place]
        request = row_request[row]
        first = jnp.minimum(start_of[request], page_total - 1)
        second = jnp.minimum(first + 1, page_total - 1)
        length = lengths[request]
        from_rank = behind_rank(me, row // row_local, dims)
        query = queries[from_rank, lax.rem(row, row_local)]
        scores = []
        for h in range(kv_heads):
            columns = slice(2 * h * HD, (2 * h + 1) * HD)
            keys = jnp.concatenate([pool[first, :, columns], pool[second, :, columns]], axis=0)
            every = lax.dot_general(
                query, keys, (((1,), (1,)), ((), ())), preferred_element_type=jnp.float32
            )
            scores.append(every[h * share : (h + 1) * share])
        score = jnp.concatenate(scores, axis=0) * scaling
        token = lax.broadcasted_iota(jnp.int32, score.shape, 1)
        live = token < length
        masked = jnp.where(live, score, -1e30)
        highest = jnp.max(masked, axis=1, keepdims=True)
        weights = jnp.where(live, jnp.exp(masked - highest), 0.0)
        totals = jnp.sum(weights, axis=1, keepdims=True)
        rounded = weights.astype(jnp.bfloat16)
        mixtures = []
        for h in range(kv_heads):
            columns = slice((2 * h + 1) * HD, (2 * h + 2) * HD)
            values = jnp.concatenate([pool[first, :, columns], pool[second, :, columns]], axis=0)
            every = jnp.dot(rounded, values, preferred_element_type=jnp.float32)
            mixtures.append(every[h * share : (h + 1) * share])
        mixture = jnp.concatenate(mixtures, axis=0) / totals
        return mixture.astype(jnp.bfloat16)

    @pl.loop(0, (row_count + ROW_UNROLL - 1) // ROW_UNROLL)
    def _(step):
        for i in range(ROW_UNROLL):
            out[step * ROW_UNROLL + i] = one_row(step * ROW_UNROLL + i)


def attend(dims, shards, lengths, prefill_of, row_request, pool, after):
    offsets = list(shards)
    row_local, query_heads, _ = shards[offsets[0]].shape
    row_total = row_request.shape[0]
    smem = pl.BlockSpec(memory_space=pltpu.SMEM)
    vmem = pl.BlockSpec(memory_space=pltpu.VMEM)
    hbm = pl.BlockSpec(memory_space=pl.ANY)
    return pl.pallas_call(
        functools.partial(attend_kernel, dims, offsets),
        out_shape=jax.ShapeDtypeStruct((row_total + ROW_UNROLL, query_heads, HD), jnp.bfloat16),
        in_specs=[smem, smem, smem, vmem, hbm] + [hbm] * len(offsets),
        out_specs=vmem,
        scratch_shapes=[
            pltpu.VMEM((len(offsets), row_local, query_heads, HD), jnp.bfloat16),
            pltpu.SMEM((lengths.shape[0],), jnp.int32),
            pltpu.SMEM((row_total + ROW_UNROLL,), jnp.int32),
            pltpu.SemaphoreType.DMA((len(offsets),)),
        ],
        compiler_params=pltpu.CompilerParams(vmem_limit_bytes=VMEM_LIMIT),
        cost_estimate=pl.CostEstimate(
            flops=1 << 33, bytes_accessed=2 * pool.size, transcendentals=1 << 20
        ),
        name="attend_local_rows",
    )(lengths, prefill_of, row_request, pool, after, *(shards[o] for o in offsets))


def project(attended, out_weight):
    product = jnp.dot(attended, out_weight, preferred_element_type=jnp.float32)
    heads = lax.axis_size("head")
    my_head = lax.axis_index("head")
    share = attended.shape[0] // heads
    output = lax.dynamic_slice_in_dim(product, my_head * share, share)
    for ahead in range(1, heads):
        theirs = lax.dynamic_slice_in_dim(product, lax.rem(my_head + ahead, heads) * share, share)
        pairs = [(h, (h + ahead) % heads) for h in range(heads)]
        output = output + lax.ppermute(theirs.astype(jnp.bfloat16), "head", pairs).astype(jnp.float32)
    return output.astype(jnp.bfloat16)


def local(dims, kv_pool, lengths, prefill_of, decode_of, row_request, queries, out_weight):
    groups = math.prod(dims)
    me = lax.axis_index("group")
    row_local, query_width = queries.shape
    row_total = row_request.shape[0]

    outgoing = prepare(groups, lengths, prefill_of, decode_of, kv_pool)
    incoming = lax.all_to_all(outgoing, "group", split_axis=0, concat_axis=0, tiled=True)

    shards = gather_shards(queries.reshape(row_local, query_width // HD, HD), dims)
    rows = attend(dims, shards, lengths, prefill_of, row_request, kv_pool, outgoing)

    row_home = prefill_of[row_request]
    ordinal = jnp.arange(row_total, dtype=jnp.int32)
    earlier = (row_home[None, :] == row_home[:, None]) & (ordinal[None, :] < ordinal[:, None])
    row_rank = jnp.sum(earlier.astype(jnp.int32), axis=1)
    home_slot = behind_rank(me, row_home, dims) * CAPACITY

    def gather_round(done):
        part = lax.dynamic_slice_in_dim(rows, done, CAPACITY).reshape(CAPACITY, query_width)
        gathered = gather_shards(part, dims)
        stacked = jnp.concatenate(
            [gathered[o] for o in sorted(gathered, key=lambda o: offset_rank(o, dims))], axis=0
        )
        inside = (row_rank >= done) & (row_rank < done + CAPACITY)
        slot = jnp.where(inside, home_slot + row_rank - done, -1)
        chosen = slot[:, None] == jnp.arange(stacked.shape[0], dtype=jnp.int32)[None, :]
        return jnp.dot(
            chosen.astype(jnp.bfloat16), stacked, preferred_element_type=jnp.float32
        ).astype(jnp.bfloat16)

    most = jnp.max(row_rank) + 1
    attended = gather_round(jnp.int32(0))
    output = project(attended, out_weight)

    def further_rounds(attended, output):
        _, attended = lax.while_loop(
            lambda state: state[0] < most,
            lambda state: (state[0] + CAPACITY, state[1] + gather_round(state[0])),
            (jnp.int32(CAPACITY), attended),
        )
        return project(attended, out_weight)

    received = hand_on(incoming.reshape((groups * MAX_PAGES,) + kv_pool.shape[1:]), output)
    output = lax.cond(most > CAPACITY, further_rounds, lambda attended, output: output, attended, output)
    return (received, output)


def solution(mesh):
    in_specs = (
        P("group", None, "head"),
        P(),
        P(),
        P(),
        P(),
        P("group", "head"),
        P("head", "group"),
    )
    out_specs = (P("group", None, "head"), P("head", "group"))
    body = functools.partial(local, factors(mesh.shape["group"]))
    return jax.shard_map(body, mesh=mesh, in_specs=in_specs, out_specs=out_specs, check_vma=False)
```

```python
import functools
import itertools
import math

import jax
import jax.numpy as jnp
from jax import lax
from jax.experimental import pallas as pl
from jax.experimental.pallas import tpu as pltpu
from jax.sharding import PartitionSpec as P

HD = 128
MAX_PAGES = 2
WAVE = 3
ROW_UNROLL = 4
VMEM_LIMIT = 48 * 1024 * 1024


def factors(groups):
    if groups % 4 == 0:
        return (groups // 4, 2, 2)
    return (groups,)


def strides(dims):
    return tuple(math.prod(dims[i + 1 :]) for i in range(len(dims)))


def shifted(index, offset, dims):
    result = 0
    for size, stride, ahead in zip(dims, strides(dims), offset):
        result = result + lax.rem(index // stride % size + ahead + size, size) * stride
    return result


def shifted_static(index, offset, dims):
    result = 0
    for size, stride, ahead in zip(dims, strides(dims), offset):
        result += (index // stride % size + ahead) % size * stride
    return result


def send_by(array, offset, dims):
    groups = math.prod(dims)
    pairs = [(s, shifted_static(s, offset, dims)) for s in range(groups)]
    return lax.ppermute(array, "group", pairs)


def offset_rank(offset, dims):
    return sum(o * s for o, s in zip(offset, strides(dims)))


def behind_rank(me, other, dims):
    rank = 0
    for size, stride in zip(dims, strides(dims)):
        rank = rank + lax.rem(me // stride % size - other // stride % size + size, size) * stride
    return rank


def behind(me, offset, dims):
    return shifted(me, tuple(-o for o in offset), dims)


def gather_shards(shard, dims):
    held = {(0,) * len(dims): shard}
    for axis, size in enumerate(dims):
        incoming = {}
        for ahead in range(1, size):
            step = tuple(ahead if i == axis else 0 for i in range(len(dims)))
            for offset, array in held.items():
                incoming[tuple(a + b for a, b in zip(offset, step))] = send_by(array, step, dims)
        held.update(incoming)
    return held


def prepare_kernel(dims, offsets, lengths, prefill_of, decode_of, pool, received, *rest):
    sends = rest[: len(offsets)]
    held, zero_page, start_of, count_of, in_sems, out_sem = rest[len(offsets) :]
    groups = math.prod(dims)
    me = lax.axis_index("group")
    page_total, page_size, _ = pool.shape
    loads = [pltpu.make_async_copy(pool.at[p], held.at[p], in_sems.at[p]) for p in range(page_total)]
    for load in loads:
        load.start()
    for d in range(groups + 1):
        start_of[d] = 0
        count_of[d] = 0
    zero_page[...] = jnp.zeros_like(zero_page)

    def visit(r, running):
        mine = prefill_of[r] == me
        count = (lengths[r] + page_size - 1) // page_size
        to = jnp.where(mine, decode_of[r], groups)
        start_of[to] = running
        count_of[to] = count
        return running + jnp.where(mine, count, 0)

    lax.fori_loop(0, lengths.shape[0], visit, jnp.int32(0), unroll=8)
    for load in loads:
        load.wait()

    def store(start, count, page, target, do):
        @pl.when(page < count)
        def _():
            do(pltpu.make_async_copy(held.at[start + page], target, out_sem))

        @pl.when(page >= count)
        def _():
            do(pltpu.make_async_copy(zero_page, target, out_sem))

    def every(do):
        for send, offset in zip(sends, offsets):
            to = shifted(me, offset, dims)
            for page in range(MAX_PAGES):
                store(start_of[to], count_of[to], page, send.at[page], do)
        for page in range(MAX_PAGES):
            store(start_of[me], count_of[me], page, received.at[me * MAX_PAGES + page], do)

    every(lambda copy: copy.start())
    every(lambda copy: copy.wait())


def prepare(dims, offsets, lengths, prefill_of, decode_of, pool):
    groups = math.prod(dims)
    page = pool.shape[1:]
    smem = pl.BlockSpec(memory_space=pltpu.SMEM)
    hbm = pl.BlockSpec(memory_space=pl.ANY)
    block = jax.ShapeDtypeStruct((MAX_PAGES,) + page, pool.dtype)
    outs = [jax.ShapeDtypeStruct((groups * MAX_PAGES,) + page, pool.dtype)] + [block] * len(offsets)
    return pl.pallas_call(
        functools.partial(prepare_kernel, dims, offsets),
        out_shape=outs,
        in_specs=[smem, smem, smem, hbm],
        out_specs=[hbm] * len(outs),
        scratch_shapes=[
            pltpu.VMEM(pool.shape, pool.dtype),
            pltpu.VMEM(page, pool.dtype),
            pltpu.SMEM((groups + 1,), jnp.int32),
            pltpu.SMEM((groups + 1,), jnp.int32),
            pltpu.SemaphoreType.DMA((pool.shape[0],)),
            pltpu.SemaphoreType.DMA,
        ],
        compiler_params=pltpu.CompilerParams(vmem_limit_bytes=VMEM_LIMIT),
        cost_estimate=pl.CostEstimate(flops=0, bytes_accessed=4 * pool.size, transcendentals=0),
        name="outgoing_pages",
    )(lengths, prefill_of, decode_of, pool)


def attend_row(query, pages, length):
    first, second = pages
    kv_heads = first.shape[1] // (2 * HD)
    share = query.shape[0] // kv_heads
    scores = []
    for h in range(kv_heads):
        columns = slice(2 * h * HD, (2 * h + 1) * HD)
        keys = jnp.concatenate([first[:, columns], second[:, columns]], axis=0)
        every = lax.dot_general(
            query, keys, (((1,), (1,)), ((), ())), preferred_element_type=jnp.float32
        )
        scores.append(every[h * share : (h + 1) * share])
    score = jnp.concatenate(scores, axis=0) * (1.0 / math.sqrt(HD))
    live = lax.broadcasted_iota(jnp.int32, score.shape, 1) < length
    masked = jnp.where(live, score, -1e30)
    highest = jnp.max(masked, axis=1, keepdims=True)
    weights = jnp.where(live, jnp.exp(masked - highest), 0.0)
    totals = jnp.sum(weights, axis=1, keepdims=True)
    rounded = weights.astype(jnp.bfloat16)
    mixtures = []
    for h in range(kv_heads):
        columns = slice((2 * h + 1) * HD, (2 * h + 2) * HD)
        values = jnp.concatenate([first[:, columns], second[:, columns]], axis=0)
        every = jnp.dot(rounded, values, preferred_element_type=jnp.float32)
        mixtures.append(every[h * share : (h + 1) * share])
    return jnp.concatenate(mixtures, axis=0) / totals


def settle_kernel(dims, offsets, own, last, lengths, prefill_of, row_request, queries, rows_in, received_in, *rest):
    blocks = rest[: len(offsets)]
    received, out, rows, held, list_row, list_block, list_length, in_sems, out_sems = rest[len(offsets) :]
    me = lax.axis_index("group")
    row_local, query_heads, _ = queries.shape
    mine = pl.ds(me * MAX_PAGES, MAX_PAGES)
    places = [pl.ds(behind(me, offset, dims) * MAX_PAGES, MAX_PAGES) for offset in offsets]
    sources = list(blocks) + ([received_in.at[mine]] if own else [])
    ranks = [offset_rank(offset, dims) for offset in offsets] + ([0] if own else [])
    loads = [pltpu.make_async_copy(s, held.at[i], in_sems.at[i]) for i, s in enumerate(sources)]
    stores = [
        pltpu.make_async_copy(held.at[i], received.at[place], out_sems.at[i]) for i, place in enumerate(places)
    ]
    for load in loads:
        load.start()

    found = jnp.int32(0)
    for b in range(row_local):
        request = row_request[me * row_local + b]
        rank = behind_rank(me, prefill_of[request], dims)
        block, match = jnp.int32(0), jnp.int32(0)
        for i, here in enumerate(ranks):
            block = jnp.where(rank == here, i, block)
            match = jnp.where(rank == here, 1, match)
        list_row[found] = b
        list_block[found] = block
        list_length[found] = lengths[request]
        found = found + match
    for i in range(ROW_UNROLL):
        list_row[found + i] = row_local
        list_block[found + i] = 0
        list_length[found + i] = 1
    rows[:row_local] = rows_in[...]
    for load in loads:
        load.wait()
    for store in stores:
        store.start()

    @pl.loop(0, (found + ROW_UNROLL - 1) // ROW_UNROLL)
    def _(step):
        results = []
        for i in range(ROW_UNROLL):
            at = step * ROW_UNROLL + i
            query = queries[jnp.minimum(list_row[at], row_local - 1)]
            pages = [held[list_block[at], page] for page in range(MAX_PAGES)]
            results.append(attend_row(query, pages, list_length[at]))
        for i, result in enumerate(results):
            rows[list_row[step * ROW_UNROLL + i]] = result

    if last:
        for h in range(query_heads):
            out[:, h * HD : (h + 1) * HD] = rows[:row_local, h, :].astype(out.dtype)
    else:
        out[...] = rows[:row_local]
    for store in stores:
        store.wait()


def settle(dims, offsets, own, last, tables, queries, rows, received, blocks):
    row_local, query_heads, _ = queries.shape
    smem = pl.BlockSpec(memory_space=pltpu.SMEM)
    vmem = pl.BlockSpec(memory_space=pltpu.VMEM)
    hbm = pl.BlockSpec(memory_space=pl.ANY)
    count = len(blocks) + (1 if own else 0)
    if last:
        out = jax.ShapeDtypeStruct((row_local, query_heads * HD), jnp.bfloat16)
    else:
        out = jax.ShapeDtypeStruct(rows.shape, rows.dtype)
    return pl.pallas_call(
        functools.partial(settle_kernel, dims, offsets, own, last),
        out_shape=[jax.ShapeDtypeStruct(received.shape, received.dtype), out],
        in_specs=[smem, smem, smem, vmem, vmem, hbm] + [hbm] * len(blocks),
        out_specs=[hbm, vmem],
        scratch_shapes=[
            pltpu.VMEM((row_local + 1, query_heads, HD), jnp.float32),
            pltpu.VMEM((count, MAX_PAGES) + received.shape[1:], received.dtype),
            pltpu.SMEM((row_local + ROW_UNROLL,), jnp.int32),
            pltpu.SMEM((row_local + ROW_UNROLL,), jnp.int32),
            pltpu.SMEM((row_local + ROW_UNROLL,), jnp.int32),
            pltpu.SemaphoreType.DMA((count,)),
            pltpu.SemaphoreType.DMA((count,)),
        ],
        input_output_aliases={5: 0},
        compiler_params=pltpu.CompilerParams(vmem_limit_bytes=VMEM_LIMIT),
        cost_estimate=pl.CostEstimate(
            flops=1 << 30, bytes_accessed=4 * sum(b.size for b in blocks), transcendentals=1 << 18
        ),
        name="settle_pages",
    )(*tables, queries, rows, received, *blocks)


def project_kernel(dims, offsets, out_weight, *rest):
    shards = rest[: len(offsets)]
    own, *theirs = rest[len(offsets) : -3]
    attended, product, sems = rest[-3:]
    me = lax.axis_index("group")
    heads = lax.axis_size("head")
    my_head = lax.axis_index("head")
    row_local = shards[0].shape[0]
    share = own.shape[0]
    copies = []
    for i, offset in enumerate(offsets):
        place = pl.ds(behind(me, offset, dims) * row_local, row_local)
        copies.append(pltpu.make_async_copy(shards[i], attended.at[place], sems.at[i]))
        copies[-1].start()
    for copy in copies:
        copy.wait()
    product[...] = jnp.dot(attended[...], out_weight[...], preferred_element_type=jnp.float32)
    own[...] = product[pl.ds(pl.multiple_of(my_head * share, share), share)]
    for ahead, target in enumerate(theirs, 1):
        start = pl.multiple_of(lax.rem(my_head + ahead, heads) * share, share)
        target[...] = product[pl.ds(start, share)].astype(target.dtype)


def project(dims, gathered, out_weight, heads):
    offsets = list(gathered)
    shards = [gathered[o] for o in offsets]
    row_local, width = shards[0].shape
    row_total = row_local * len(shards)
    share, columns = row_total // heads, out_weight.shape[1]
    vmem = pl.BlockSpec(memory_space=pltpu.VMEM)
    hbm = pl.BlockSpec(memory_space=pl.ANY)
    theirs = jax.ShapeDtypeStruct((share, columns), jnp.bfloat16)
    return pl.pallas_call(
        functools.partial(project_kernel, dims, offsets),
        out_shape=[jax.ShapeDtypeStruct((share, columns), jnp.float32)] + [theirs] * (heads - 1),
        in_specs=[vmem] + [hbm] * len(shards),
        out_specs=[vmem] * heads,
        scratch_shapes=[
            pltpu.VMEM((row_total, width), jnp.bfloat16),
            pltpu.VMEM((row_total, columns), jnp.float32),
            pltpu.SemaphoreType.DMA((len(shards),)),
        ],
        compiler_params=pltpu.CompilerParams(vmem_limit_bytes=VMEM_LIMIT),
        cost_estimate=pl.CostEstimate(
            flops=2 * row_total * width * columns, bytes_accessed=2 * out_weight.size, transcendentals=0
        ),
        name="project_rows",
    )(out_weight, *shards)


def local(dims, kv_pool, lengths, prefill_of, decode_of, row_request, queries, out_weight):
    row_local, query_width = queries.shape
    query_heads = queries.reshape(row_local, query_width // HD, HD)
    heads = lax.axis_size("head")

    far, near = range(dims[0]), list(itertools.product(*(range(n) for n in dims[1:])))
    offsets = [(z,) + n for n in near for z in far if z or any(n)]
    received, *sends = prepare(dims, offsets, lengths, prefill_of, decode_of, kv_pool)
    arrived = [send_by(block, offset, dims) for block, offset in zip(sends, offsets)]
    rows = jnp.zeros(query_heads.shape, jnp.float32)
    tables = (lengths, prefill_of, row_request)
    for first in range(0, len(offsets), WAVE):
        wave = slice(first, first + WAVE)
        last = first + WAVE >= len(offsets)
        received, rows = settle(
            dims, offsets[wave], first == 0, last, tables, query_heads, rows, received, arrived[wave]
        )

    own, *theirs = project(dims, gather_shards(rows, dims), out_weight, heads)
    for ahead, part in enumerate(theirs, 1):
        pairs = [(h, (h + ahead) % heads) for h in range(heads)]
        own = own + lax.ppermute(part, "head", pairs).astype(jnp.float32)
    return (received, own.astype(jnp.bfloat16))


def solution(mesh):
    in_specs = (
        P("group", None, "head"),
        P(),
        P(),
        P(),
        P(),
        P("group", "head"),
        P("head", "group"),
    )
    out_specs = (P("group", None, "head"), P("head", "group"))
    body = functools.partial(local, factors(mesh.shape["group"]))
    return jax.shard_map(body, mesh=mesh, in_specs=in_specs, out_specs=out_specs, check_vma=False)
```

```python
import functools
import math

import jax
import jax.numpy as jnp
from jax import lax
from jax.experimental import pallas as pl
from jax.experimental.pallas import tpu as pltpu
from jax.sharding import PartitionSpec as P

HD = 128
MAX_PAGES = 2
WAVE = 3
ROW_UNROLL = 4
EARLY = 4
DEPTH = 512
VMEM_LIMIT = 48 * 1024 * 1024


def partner(me, code):
    return me ^ code


def send_by(array, code):
    groups = lax.axis_size("group")
    return lax.ppermute(array, "group", [(s, partner(s, code)) for s in range(groups)])


def page_codes(groups):
    near = min(4, groups)
    far = groups // near
    order = [z * near + n for n in range(near) for z in list(range(far // 2, far)) + list(range(far // 2)) if z * near + n]
    tail = order[-far:]
    return order[:-far] + tail[far // 2 :] + tail[: far // 2]


def gather_shards(shard):
    groups = lax.axis_size("group")
    held = {0: shard}
    near = min(4, groups)
    for codes in (range(groups - near, 0, -near), (2,), (1,)):
        incoming = {}
        for step in codes:
            for code, array in held.items():
                incoming[code | step] = send_by(array, step)
        held.update(incoming)
    return held


def prepare_kernel(codes, own, lengths_hbm, prefill_hbm, decode_hbm, pool, *rest):
    aliased = 0 if own else 1
    received, *sends = rest[aliased : aliased + 1 + len(codes)]
    lengths, prefill_of, decode_of, held, zero_page, start_of, count_of, table_sem, in_sems, out_sem = rest[
        aliased + 1 + len(codes) :
    ]
    me = lax.axis_index("group")
    groups = lax.axis_size("group")
    page_size = pool.shape[1]
    tables = [
        pltpu.make_async_copy(source, target, table_sem.at[i])
        for i, (source, target) in enumerate(
            [(lengths_hbm, lengths), (prefill_hbm, prefill_of), (decode_hbm, decode_of)]
        )
    ]
    for table in tables:
        table.start()
    for d in range(groups + 1):
        start_of[d] = 0
        count_of[d] = 0
    zero_page[...] = jnp.zeros_like(zero_page)
    for table in tables:
        table.wait()

    def visit(r, running):
        mine = prefill_of[r] == me
        count = (lengths[r] + page_size - 1) // page_size
        to = jnp.where(mine, decode_of[r], groups)
        start_of[to] = running
        count_of[to] = count
        return running + jnp.where(mine, count, 0)

    lax.fori_loop(0, lengths.shape[0], visit, jnp.int32(0), unroll=8)
    targets = [(partner(me, code), send, 0) for code, send in zip(codes, sends)]
    if own:
        targets.append((me, received, me * MAX_PAGES))

    def each(do):
        for i, (to, target, base) in enumerate(targets):
            for page in range(MAX_PAGES):
                there = page < count_of[to]
                source = pool.at[jnp.where(there, start_of[to] + page, 0)]
                buffer, place = held.at[i, page], target.at[base + page]
                do(there, (source, buffer, in_sems.at[i, page]), (buffer, place, out_sem), (zero_page, place, out_sem))

    def fetch(there, load, store, blank):
        @pl.when(there)
        def _():
            pltpu.make_async_copy(*load).start()

        @pl.when(jnp.logical_not(there))
        def _():
            pltpu.make_async_copy(*blank).start()

    def forward(there, load, store, blank):
        @pl.when(there)
        def _():
            pltpu.make_async_copy(*load).wait()
            pltpu.make_async_copy(*store).start()

    def finish(there, load, store, blank):
        pltpu.make_async_copy(*blank).wait()

    each(fetch)
    each(forward)
    each(finish)


def prepare(codes, lengths, prefill_of, decode_of, pool, received=None):
    own = received is None
    groups = lax.axis_size("group")
    page = pool.shape[1:]
    blocks = len(codes) + (1 if own else 0)
    hbm = pl.BlockSpec(memory_space=pl.ANY)
    block = jax.ShapeDtypeStruct((MAX_PAGES,) + page, pool.dtype)
    outs = [jax.ShapeDtypeStruct((groups * MAX_PAGES,) + page, pool.dtype)] + [block] * len(codes)
    operands = [lengths, prefill_of, decode_of, pool] + ([] if own else [received])
    table = pltpu.SMEM(lengths.shape, jnp.int32)
    return pl.pallas_call(
        functools.partial(prepare_kernel, codes, own),
        out_shape=outs,
        in_specs=[hbm] * len(operands),
        out_specs=[hbm] * len(outs),
        scratch_shapes=[
            table,
            table,
            table,
            pltpu.VMEM((blocks, MAX_PAGES) + page, pool.dtype),
            pltpu.VMEM(page, pool.dtype),
            pltpu.SMEM((groups + 1,), jnp.int32),
            pltpu.SMEM((groups + 1,), jnp.int32),
            pltpu.SemaphoreType.DMA((3,)),
            pltpu.SemaphoreType.DMA((blocks, MAX_PAGES)),
            pltpu.SemaphoreType.DMA,
        ],
        input_output_aliases={} if own else {4: 0},
        compiler_params=pltpu.CompilerParams(vmem_limit_bytes=VMEM_LIMIT),
        cost_estimate=pl.CostEstimate(
            flops=0, bytes_accessed=4 * blocks * MAX_PAGES * math.prod(page), transcendentals=0
        ),
        name="outgoing_pages",
    )(*operands)


def attend_row(query, pages, length):
    first, second = pages
    kv_heads = first.shape[1] // (2 * HD)
    share = query.shape[0] // kv_heads
    scores = []
    for h in range(kv_heads):
        columns = slice(2 * h * HD, (2 * h + 1) * HD)
        keys = jnp.concatenate([first[:, columns], second[:, columns]], axis=0)
        every = lax.dot_general(
            query, keys, (((1,), (1,)), ((), ())), preferred_element_type=jnp.float32
        )
        scores.append(every[h * share : (h + 1) * share])
    score = jnp.concatenate(scores, axis=0) * (1.0 / math.sqrt(HD))
    live = lax.broadcasted_iota(jnp.int32, score.shape, 1) < length
    masked = jnp.where(live, score, -1e30)
    highest = jnp.max(masked, axis=1, keepdims=True)
    weights = jnp.where(live, jnp.exp(masked - highest), 0.0)
    totals = jnp.sum(weights, axis=1, keepdims=True)
    rounded = weights.astype(jnp.bfloat16)
    mixtures = []
    for h in range(kv_heads):
        columns = slice((2 * h + 1) * HD, (2 * h + 2) * HD)
        values = jnp.concatenate([first[:, columns], second[:, columns]], axis=0)
        every = jnp.dot(rounded, values, preferred_element_type=jnp.float32)
        mixtures.append(every[h * share : (h + 1) * share])
    return jnp.concatenate(mixtures, axis=0) / totals


def settle_kernel(codes, own, last, lengths, prefill_of, row_request, queries, rows_in, received_in, *rest):
    blocks = rest[: len(codes)]
    received, out, rows, held, list_row, list_block, list_length, in_sems, out_sems = rest[len(codes) :]
    me = lax.axis_index("group")
    row_local, query_heads, _ = queries.shape
    mine = pl.ds(me * MAX_PAGES, MAX_PAGES)
    places = [pl.ds(partner(me, code) * MAX_PAGES, MAX_PAGES) for code in codes]
    sources = list(blocks) + ([received_in.at[mine]] if own else [])
    kinds = list(codes) + ([0] if own else [])
    loads = [pltpu.make_async_copy(s, held.at[i], in_sems.at[i]) for i, s in enumerate(sources)]
    stores = [
        pltpu.make_async_copy(held.at[i], received.at[place], out_sems.at[i]) for i, place in enumerate(places)
    ]
    for load in loads:
        load.start()

    found = jnp.int32(0)
    for b in range(row_local):
        request = row_request[me * row_local + b]
        kind = partner(me, prefill_of[request])
        block, match = jnp.int32(0), jnp.int32(0)
        for i, here in enumerate(kinds):
            block = jnp.where(kind == here, i, block)
            match = jnp.where(kind == here, 1, match)
        list_row[found] = b
        list_block[found] = block
        list_length[found] = lengths[request]
        found = found + match
    for i in range(ROW_UNROLL):
        list_row[found + i] = row_local
        list_block[found + i] = 0
        list_length[found + i] = 1
    rows[:row_local] = rows_in[...]
    for load in loads:
        load.wait()
    for store in stores:
        store.start()

    @pl.loop(0, (found + ROW_UNROLL - 1) // ROW_UNROLL)
    def _(step):
        results = []
        for i in range(ROW_UNROLL):
            at = step * ROW_UNROLL + i
            query = queries[jnp.minimum(list_row[at], row_local - 1)]
            pages = [held[list_block[at], page] for page in range(MAX_PAGES)]
            results.append(attend_row(query, pages, list_length[at]))
        for i, result in enumerate(results):
            rows[list_row[step * ROW_UNROLL + i]] = result

    if last:
        for h in range(query_heads):
            out[:, h * HD : (h + 1) * HD] = rows[:row_local, h, :].astype(out.dtype)
    else:
        out[...] = rows[:row_local]
    for store in stores:
        store.wait()


def settle(codes, own, last, tables, queries, rows, received, blocks):
    row_local, query_heads, _ = queries.shape
    smem = pl.BlockSpec(memory_space=pltpu.SMEM)
    vmem = pl.BlockSpec(memory_space=pltpu.VMEM)
    hbm = pl.BlockSpec(memory_space=pl.ANY)
    count = len(blocks) + (1 if own else 0)
    if last:
        out = jax.ShapeDtypeStruct((row_local, query_heads * HD), jnp.bfloat16)
    else:
        out = jax.ShapeDtypeStruct(rows.shape, rows.dtype)
    return pl.pallas_call(
        functools.partial(settle_kernel, codes, own, last),
        out_shape=[jax.ShapeDtypeStruct(received.shape, received.dtype), out],
        in_specs=[smem, smem, smem, vmem, vmem, hbm] + [hbm] * len(blocks),
        out_specs=[hbm, vmem],
        scratch_shapes=[
            pltpu.VMEM((row_local + 1, query_heads, HD), jnp.float32),
            pltpu.VMEM((count, MAX_PAGES) + received.shape[1:], received.dtype),
            pltpu.SMEM((row_local + ROW_UNROLL,), jnp.int32),
            pltpu.SMEM((row_local + ROW_UNROLL,), jnp.int32),
            pltpu.SMEM((row_local + ROW_UNROLL,), jnp.int32),
            pltpu.SemaphoreType.DMA((count,)),
            pltpu.SemaphoreType.DMA((count,)),
        ],
        input_output_aliases={5: 0},
        compiler_params=pltpu.CompilerParams(vmem_limit_bytes=VMEM_LIMIT),
        cost_estimate=pl.CostEstimate(
            flops=1 << 30, bytes_accessed=4 * sum(b.size for b in blocks), transcendentals=1 << 18
        ),
        name="settle_pages",
    )(*tables, queries, rows, received, *blocks)


def project_kernel(codes, out_weight, *rest):
    shards = rest[: len(codes)]
    own, *theirs = rest[len(codes) : -5]
    attended, weight, product, sems, weight_sems = rest[-5:]
    me = lax.axis_index("group")
    heads = lax.axis_size("head")
    my_head = lax.axis_index("head")
    row_local, width = shards[0].shape
    share = own.shape[0]
    copies = []
    for i, code in enumerate(codes):
        place = pl.ds(partner(me, code) * row_local, row_local)
        copies.append(pltpu.make_async_copy(shards[i], attended.at[place], sems.at[i]))
    loads = []
    for k in range(0, width, DEPTH):
        part = pl.ds(k, DEPTH)
        loads.append(pltpu.make_async_copy(out_weight.at[part], weight.at[part], weight_sems.at[k // DEPTH]))
    for copy in copies + loads:
        copy.start()
    for copy in copies:
        copy.wait()
    for k, load in zip(range(0, width, DEPTH), loads):
        load.wait()
        part = jnp.dot(
            attended[:, k : k + DEPTH], weight[k : k + DEPTH], preferred_element_type=jnp.float32
        )
        product[...] = part if k == 0 else product[...] + part
    own[...] = product[pl.ds(pl.multiple_of(my_head * share, share), share)]
    for ahead, target in enumerate(theirs, 1):
        start = pl.multiple_of(lax.rem(my_head + ahead, heads) * share, share)
        target[...] = product[pl.ds(start, share)].astype(target.dtype)


def project(gathered, out_weight, heads):
    codes = list(gathered)
    shards = [gathered[code] for code in codes]
    row_local, width = shards[0].shape
    row_total = row_local * len(shards)
    share, columns = row_total // heads, out_weight.shape[1]
    vmem = pl.BlockSpec(memory_space=pltpu.VMEM)
    hbm = pl.BlockSpec(memory_space=pl.ANY)
    theirs = jax.ShapeDtypeStruct((share, columns), jnp.bfloat16)
    return pl.pallas_call(
        functools.partial(project_kernel, codes),
        out_shape=[jax.ShapeDtypeStruct((share, columns), jnp.float32)] + [theirs] * (heads - 1),
        in_specs=[hbm] + [hbm] * len(shards),
        out_specs=[vmem] * heads,
        scratch_shapes=[
            pltpu.VMEM((row_total, width), jnp.bfloat16),
            pltpu.VMEM(out_weight.shape, jnp.bfloat16),
            pltpu.VMEM((row_total, columns), jnp.float32),
            pltpu.SemaphoreType.DMA((len(shards),)),
            pltpu.SemaphoreType.DMA((width // DEPTH,)),
        ],
        compiler_params=pltpu.CompilerParams(vmem_limit_bytes=VMEM_LIMIT),
        cost_estimate=pl.CostEstimate(
            flops=2 * row_total * width * columns, bytes_accessed=2 * out_weight.size, transcendentals=0
        ),
        name="project_rows",
    )(out_weight, *shards)


def local(kv_pool, lengths, prefill_of, decode_of, row_request, queries, out_weight):
    row_local, query_width = queries.shape
    query_heads = queries.reshape(row_local, query_width // HD, HD)
    heads = lax.axis_size("head")

    codes = page_codes(lax.axis_size("group"))
    pages = (lengths, prefill_of, decode_of, kv_pool)
    received, *early = prepare(codes[:EARLY], *pages)
    received, *late = prepare(codes[EARLY:], *pages, received)
    arrived = [send_by(block, code) for block, code in zip(early + late, codes)]
    rows = jnp.zeros(query_heads.shape, jnp.float32)
    tables = (lengths, prefill_of, row_request)
    for first in range(0, len(codes), WAVE):
        wave = slice(first, first + WAVE)
        last = first + WAVE >= len(codes)
        received, rows = settle(
            codes[wave], first == 0, last, tables, query_heads, rows, received, arrived[wave]
        )

    own, *theirs = project(gather_shards(rows), out_weight, heads)
    for ahead, part in enumerate(theirs, 1):
        pairs = [(h, (h + ahead) % heads) for h in range(heads)]
        own = own + lax.ppermute(part, "head", pairs).astype(jnp.float32)
    return (received, own.astype(jnp.bfloat16))


def solution(mesh):
    in_specs = (
        P("group", None, "head"),
        P(),
        P(),
        P(),
        P(),
        P("group", "head"),
        P("head", "group"),
    )
    out_specs = (P("group", None, "head"), P("head", "group"))
    assert mesh.shape["group"] & (mesh.shape["group"] - 1) == 0
    return jax.shard_map(local, mesh=mesh, in_specs=in_specs, out_specs=out_specs, check_vma=False)
```

```python
import functools
import math

import jax
import jax.numpy as jnp
from jax import lax
from jax.experimental import pallas as pl
from jax.experimental.pallas import tpu as pltpu
from jax.sharding import PartitionSpec as P

HD = 128
MAX_PAGES = 2
WAVE = 3
ROW_UNROLL = 4
EARLY = 4
DEPTH = 512
VMEM_LIMIT = 48 * 1024 * 1024


def factors(groups):
    near = math.gcd(groups, 4)
    return groups // near, near


def ahead(me, offset, dims, sign=1):
    far, near = dims
    return lax.rem(me // near + sign * offset[0] + far, far) * near + (me % near ^ offset[1])


def behind(me, offset, dims):
    return ahead(me, offset, dims, -1)


def kind_of(offset, dims):
    return offset[0] * dims[1] + offset[1]


def kind_behind(me, other, dims):
    far, near = dims
    return lax.rem(me // near - other // near + far, far) * near + (me % near ^ other % near)


def send_by(array, offset, dims):
    far, near = dims
    pairs = [
        (s, (s // near + offset[0]) % far * near + (s % near ^ offset[1])) for s in range(far * near)
    ]
    return lax.ppermute(array, "group", pairs)


def page_offsets(dims):
    far, near = dims
    steps = sorted(range(1, far), key=lambda z: (min(z, far - z), z))
    order = [(z, n) for z in steps for n in range(near)]
    for n in range(1, near):
        order.insert(min(2 * n, len(order)), (0, n))
    return order


def gather_shards(shard, dims):
    far, near = dims
    held = {(0, 0): shard}
    swaps = [1 << i for i in reversed(range(near.bit_length() - 1))]
    for stage in [[(z, 0) for z in range(1, far)]] + [[(0, n)] for n in swaps]:
        incoming = {}
        for step in stage:
            for offset, array in held.items():
                incoming[offset[0] + step[0], offset[1] | step[1]] = send_by(array, step, dims)
        held.update(incoming)
    return held


def prepare_kernel(dims, offsets, own, lengths_hbm, prefill_hbm, decode_hbm, pool, *rest):
    aliased = 0 if own else 1
    received, *sends = rest[aliased : aliased + 1 + len(offsets)]
    lengths, prefill_of, decode_of, held, zero_page, start_of, count_of, table_sem, in_sems, out_sem = rest[
        aliased + 1 + len(offsets) :
    ]
    me = lax.axis_index("group")
    groups = lax.axis_size("group")
    page_size = pool.shape[1]
    tables = [
        pltpu.make_async_copy(source, target, table_sem.at[i])
        for i, (source, target) in enumerate(
            [(lengths_hbm, lengths), (prefill_hbm, prefill_of), (decode_hbm, decode_of)]
        )
    ]
    for table in tables:
        table.start()
    for d in range(groups + 1):
        start_of[d] = 0
        count_of[d] = 0
    zero_page[...] = jnp.zeros_like(zero_page)
    for table in tables:
        table.wait()

    def visit(r, running):
        mine = prefill_of[r] == me
        count = (lengths[r] + page_size - 1) // page_size
        to = jnp.where(mine, decode_of[r], groups)
        start_of[to] = running
        count_of[to] = count
        return running + jnp.where(mine, count, 0)

    lax.fori_loop(0, lengths.shape[0], visit, jnp.int32(0), unroll=8)
    targets = [(ahead(me, offset, dims), send, 0) for offset, send in zip(offsets, sends)]
    if own:
        targets.append((me, received, me * MAX_PAGES))

    def each(do):
        for i, (to, target, base) in enumerate(targets):
            for page in range(MAX_PAGES):
                there = page < count_of[to]
                source = pool.at[jnp.where(there, start_of[to] + page, 0)]
                buffer, place = held.at[i, page], target.at[base + page]
                do(there, (source, buffer, in_sems.at[i, page]), (buffer, place, out_sem), (zero_page, place, out_sem))

    def fetch(there, load, store, blank):
        @pl.when(there)
        def _():
            pltpu.make_async_copy(*load).start()

        @pl.when(jnp.logical_not(there))
        def _():
            pltpu.make_async_copy(*blank).start()

    def forward(there, load, store, blank):
        @pl.when(there)
        def _():
            pltpu.make_async_copy(*load).wait()
            pltpu.make_async_copy(*store).start()

    def finish(there, load, store, blank):
        pltpu.make_async_copy(*blank).wait()

    each(fetch)
    each(forward)
    each(finish)


def prepare(dims, offsets, lengths, prefill_of, decode_of, pool, received=None):
    own = received is None
    groups = lax.axis_size("group")
    page = pool.shape[1:]
    blocks = len(offsets) + (1 if own else 0)
    hbm = pl.BlockSpec(memory_space=pl.ANY)
    block = jax.ShapeDtypeStruct((MAX_PAGES,) + page, pool.dtype)
    outs = [jax.ShapeDtypeStruct((groups * MAX_PAGES,) + page, pool.dtype)] + [block] * len(offsets)
    operands = [lengths, prefill_of, decode_of, pool] + ([] if own else [received])
    table = pltpu.SMEM(lengths.shape, jnp.int32)
    return pl.pallas_call(
        functools.partial(prepare_kernel, dims, offsets, own),
        out_shape=outs,
        in_specs=[hbm] * len(operands),
        out_specs=[hbm] * len(outs),
        scratch_shapes=[
            table,
            table,
            table,
            pltpu.VMEM((blocks, MAX_PAGES) + page, pool.dtype),
            pltpu.VMEM(page, pool.dtype),
            pltpu.SMEM((groups + 1,), jnp.int32),
            pltpu.SMEM((groups + 1,), jnp.int32),
            pltpu.SemaphoreType.DMA((3,)),
            pltpu.SemaphoreType.DMA((blocks, MAX_PAGES)),
            pltpu.SemaphoreType.DMA,
        ],
        input_output_aliases={} if own else {4: 0},
        compiler_params=pltpu.CompilerParams(vmem_limit_bytes=VMEM_LIMIT),
        cost_estimate=pl.CostEstimate(
            flops=0, bytes_accessed=4 * blocks * MAX_PAGES * math.prod(page), transcendentals=0
        ),
        name="outgoing_pages",
    )(*operands)


def attend_row(query, pages, length):
    first, second = pages
    kv_heads = first.shape[1] // (2 * HD)
    share = query.shape[0] // kv_heads
    scores = []
    for h in range(kv_heads):
        columns = slice(2 * h * HD, (2 * h + 1) * HD)
        keys = jnp.concatenate([first[:, columns], second[:, columns]], axis=0)
        every = lax.dot_general(
            query, keys, (((1,), (1,)), ((), ())), preferred_element_type=jnp.float32
        )
        scores.append(every[h * share : (h + 1) * share])
    score = jnp.concatenate(scores, axis=0) * (1.0 / math.sqrt(HD))
    live = lax.broadcasted_iota(jnp.int32, score.shape, 1) < length
    masked = jnp.where(live, score, -1e30)
    highest = jnp.max(masked, axis=1, keepdims=True)
    weights = jnp.where(live, jnp.exp(masked - highest), 0.0)
    totals = jnp.sum(weights, axis=1, keepdims=True)
    rounded = weights.astype(jnp.bfloat16)
    mixtures = []
    for h in range(kv_heads):
        columns = slice((2 * h + 1) * HD, (2 * h + 2) * HD)
        values = jnp.concatenate([first[:, columns], second[:, columns]], axis=0)
        every = jnp.dot(rounded, values, preferred_element_type=jnp.float32)
        mixtures.append(every[h * share : (h + 1) * share])
    return jnp.concatenate(mixtures, axis=0) / totals


def settle_kernel(dims, offsets, own, last, lengths, prefill_of, row_request, queries, rows_in, received_in, *rest):
    blocks = rest[: len(offsets)]
    received, out, rows, held, list_row, list_block, list_length, in_sems, out_sems = rest[len(offsets) :]
    me = lax.axis_index("group")
    row_local, query_heads, _ = queries.shape
    mine = pl.ds(me * MAX_PAGES, MAX_PAGES)
    places = [pl.ds(behind(me, offset, dims) * MAX_PAGES, MAX_PAGES) for offset in offsets]
    sources = list(blocks) + ([received_in.at[mine]] if own else [])
    kinds = [kind_of(offset, dims) for offset in offsets] + ([0] if own else [])
    loads = [pltpu.make_async_copy(s, held.at[i], in_sems.at[i]) for i, s in enumerate(sources)]
    stores = [
        pltpu.make_async_copy(held.at[i], received.at[place], out_sems.at[i]) for i, place in enumerate(places)
    ]
    for load in loads:
        load.start()

    found = jnp.int32(0)
    for b in range(row_local):
        request = row_request[me * row_local + b]
        kind = kind_behind(me, prefill_of[request], dims)
        block, match = jnp.int32(0), jnp.int32(0)
        for i, here in enumerate(kinds):
            block = jnp.where(kind == here, i, block)
            match = jnp.where(kind == here, 1, match)
        list_row[found] = b
        list_block[found] = block
        list_length[found] = lengths[request]
        found = found + match
    for i in range(ROW_UNROLL):
        list_row[found + i] = row_local
        list_block[found + i] = 0
        list_length[found + i] = 1
    rows[:row_local] = rows_in[...]
    for load in loads:
        load.wait()
    for store in stores:
        store.start()

    @pl.loop(0, (found + ROW_UNROLL - 1) // ROW_UNROLL)
    def _(step):
        results = []
        for i in range(ROW_UNROLL):
            at = step * ROW_UNROLL + i
            query = queries[jnp.minimum(list_row[at], row_local - 1)]
            pages = [held[list_block[at], page] for page in range(MAX_PAGES)]
            results.append(attend_row(query, pages, list_length[at]))
        for i, result in enumerate(results):
            rows[list_row[step * ROW_UNROLL + i]] = result

    if last:
        for h in range(query_heads):
            out[:, h * HD : (h + 1) * HD] = rows[:row_local, h, :].astype(out.dtype)
    else:
        out[...] = rows[:row_local]
    for store in stores:
        store.wait()


def settle(dims, offsets, own, last, tables, queries, rows, received, blocks):
    row_local, query_heads, _ = queries.shape
    smem = pl.BlockSpec(memory_space=pltpu.SMEM)
    vmem = pl.BlockSpec(memory_space=pltpu.VMEM)
    hbm = pl.BlockSpec(memory_space=pl.ANY)
    count = len(blocks) + (1 if own else 0)
    if last:
        out = jax.ShapeDtypeStruct((row_local, query_heads * HD), jnp.bfloat16)
    else:
        out = jax.ShapeDtypeStruct(rows.shape, rows.dtype)
    return pl.pallas_call(
        functools.partial(settle_kernel, dims, offsets, own, last),
        out_shape=[jax.ShapeDtypeStruct(received.shape, received.dtype), out],
        in_specs=[smem, smem, smem, vmem, vmem, hbm] + [hbm] * len(blocks),
        out_specs=[hbm, vmem],
        scratch_shapes=[
            pltpu.VMEM((row_local + 1, query_heads, HD), jnp.float32),
            pltpu.VMEM((count, MAX_PAGES) + received.shape[1:], received.dtype),
            pltpu.SMEM((row_local + ROW_UNROLL,), jnp.int32),
            pltpu.SMEM((row_local + ROW_UNROLL,), jnp.int32),
            pltpu.SMEM((row_local + ROW_UNROLL,), jnp.int32),
            pltpu.SemaphoreType.DMA((count,)),
            pltpu.SemaphoreType.DMA((count,)),
        ],
        input_output_aliases={5: 0},
        compiler_params=pltpu.CompilerParams(vmem_limit_bytes=VMEM_LIMIT),
        cost_estimate=pl.CostEstimate(
            flops=1 << 30, bytes_accessed=4 * sum(b.size for b in blocks), transcendentals=1 << 18
        ),
        name="settle_pages",
    )(*tables, queries, rows, received, *blocks)


def project_kernel(dims, offsets, out_weight, *rest):
    shards = rest[: len(offsets)]
    own, *theirs = rest[len(offsets) : -5]
    attended, weight, product, sems, weight_sems = rest[-5:]
    me = lax.axis_index("group")
    heads = lax.axis_size("head")
    my_head = lax.axis_index("head")
    row_local, width = shards[0].shape
    share = own.shape[0]
    copies = []
    for i, offset in enumerate(offsets):
        place = pl.ds(behind(me, offset, dims) * row_local, row_local)
        copies.append(pltpu.make_async_copy(shards[i], attended.at[place], sems.at[i]))
    loads = []
    for k in range(0, width, DEPTH):
        part = pl.ds(k, DEPTH)
        loads.append(pltpu.make_async_copy(out_weight.at[part], weight.at[part], weight_sems.at[k // DEPTH]))
    for copy in copies + loads:
        copy.start()
    for copy in copies:
        copy.wait()
    for k, load in zip(range(0, width, DEPTH), loads):
        load.wait()
        part = jnp.dot(
            attended[:, k : k + DEPTH], weight[k : k + DEPTH], preferred_element_type=jnp.float32
        )
        product[...] = part if k == 0 else product[...] + part
    own[...] = product[pl.ds(pl.multiple_of(my_head * share, share), share)]
    for ahead, target in enumerate(theirs, 1):
        start = pl.multiple_of(lax.rem(my_head + ahead, heads) * share, share)
        target[...] = product[pl.ds(start, share)].astype(target.dtype)


def project(dims, gathered, out_weight, heads):
    offsets = list(gathered)
    shards = [gathered[offset] for offset in offsets]
    row_local, width = shards[0].shape
    row_total = row_local * len(shards)
    share, columns = row_total // heads, out_weight.shape[1]
    vmem = pl.BlockSpec(memory_space=pltpu.VMEM)
    hbm = pl.BlockSpec(memory_space=pl.ANY)
    theirs = jax.ShapeDtypeStruct((share, columns), jnp.bfloat16)
    return pl.pallas_call(
        functools.partial(project_kernel, dims, offsets),
        out_shape=[jax.ShapeDtypeStruct((share, columns), jnp.float32)] + [theirs] * (heads - 1),
        in_specs=[hbm] + [hbm] * len(shards),
        out_specs=[vmem] * heads,
        scratch_shapes=[
            pltpu.VMEM((row_total, width), jnp.bfloat16),
            pltpu.VMEM(out_weight.shape, jnp.bfloat16),
            pltpu.VMEM((row_total, columns), jnp.float32),
            pltpu.SemaphoreType.DMA((len(shards),)),
            pltpu.SemaphoreType.DMA((width // DEPTH,)),
        ],
        compiler_params=pltpu.CompilerParams(vmem_limit_bytes=VMEM_LIMIT),
        cost_estimate=pl.CostEstimate(
            flops=2 * row_total * width * columns, bytes_accessed=2 * out_weight.size, transcendentals=0
        ),
        name="project_rows",
    )(out_weight, *shards)


def local(kv_pool, lengths, prefill_of, decode_of, row_request, queries, out_weight):
    row_local, query_width = queries.shape
    query_heads = queries.reshape(row_local, query_width // HD, HD)
    heads = lax.axis_size("head")

    dims = factors(lax.axis_size("group"))
    offsets = page_offsets(dims)
    pages = (lengths, prefill_of, decode_of, kv_pool)
    received, *early = prepare(dims, offsets[:EARLY], *pages)
    received, *late = prepare(dims, offsets[EARLY:], *pages, received)
    arrived = [send_by(block, offset, dims) for block, offset in zip(early + late, offsets)]
    rows = jnp.zeros(query_heads.shape, jnp.float32)
    tables = (lengths, prefill_of, row_request)
    for first in range(0, len(offsets), WAVE):
        wave = slice(first, first + WAVE)
        last = first + WAVE >= len(offsets)
        received, rows = settle(
            dims, offsets[wave], first == 0, last, tables, query_heads, rows, received, arrived[wave]
        )

    own, *theirs = project(dims, gather_shards(rows, dims), out_weight, heads)
    for ahead, part in enumerate(theirs, 1):
        pairs = [(h, (h + ahead) % heads) for h in range(heads)]
        own = own + lax.ppermute(part, "head", pairs).astype(jnp.float32)
    return (received, own.astype(jnp.bfloat16))


def solution(mesh):
    in_specs = (
        P("group", None, "head"),
        P(),
        P(),
        P(),
        P(),
        P("group", "head"),
        P("head", "group"),
    )
    out_specs = (P("group", None, "head"), P("head", "group"))
    return jax.shard_map(local, mesh=mesh, in_specs=in_specs, out_specs=out_specs, check_vma=False)
```

```python
import functools
import math

import jax
import jax.numpy as jnp
from jax import lax
from jax.experimental import pallas as pl
from jax.experimental.pallas import tpu as pltpu
from jax.sharding import PartitionSpec as P

HD = 128
MAX_PAGES = 2
ROW_UNROLL = 4
VMEM_LIMIT = 40 * 1024 * 1024


def factors(groups):
    near = math.gcd(groups, 4)
    return groups // near, near


def ahead(me, offset, dims, sign=1):
    far, near = dims
    return lax.rem(me // near + sign * offset[0] + far, far) * near + (me % near ^ offset[1])


def behind(me, offset, dims):
    return ahead(me, offset, dims, -1)


def send_by(array, offset, dims):
    far, near = dims
    pairs = [
        (s, (s // near + offset[0]) % far * near + (s % near ^ offset[1])) for s in range(far * near)
    ]
    return lax.ppermute(array, "group", pairs)


def gather_shards(shard, dims):
    far, near = dims
    held = {(0, 0): shard}
    swaps = [1 << i for i in reversed(range(near.bit_length() - 1))]
    for stage in [[(z, 0) for z in range(1, far)]] + [[(0, n)] for n in swaps]:
        incoming = {}
        for step in stage:
            for offset, array in held.items():
                incoming[offset[0] + step[0], offset[1] | step[1]] = send_by(array, step, dims)
        held.update(incoming)
    return held


def prepare_kernel(lengths_hbm, prefill_hbm, decode_hbm, pool, sends, *scratch):
    lengths, prefill_of, decode_of, held, zero_page, start_of, count_of, table_sem, in_sems, out_sem = scratch
    me = lax.axis_index("group")
    groups = sends.shape[0]
    page_total, page_size, _ = pool.shape
    sources = (lengths_hbm, prefill_hbm, decode_hbm)
    tables = [
        pltpu.make_async_copy(source, target, table_sem.at[i])
        for i, (source, target) in enumerate(zip(sources, (lengths, prefill_of, decode_of)))
    ]
    loads = [pltpu.make_async_copy(pool.at[p], held.at[p], in_sems.at[p]) for p in range(page_total)]
    for copy in tables + loads:
        copy.start()
    for d in range(groups + 1):
        start_of[d] = 0
        count_of[d] = 0
    zero_page[...] = jnp.zeros_like(zero_page)
    for table in tables:
        table.wait()

    def visit(r, running):
        mine = prefill_of[r] == me
        count = (lengths[r] + page_size - 1) // page_size
        to = jnp.where(mine, decode_of[r], groups)
        start_of[to] = running
        count_of[to] = count
        return running + jnp.where(mine, count, 0)

    lax.fori_loop(0, lengths.shape[0], visit, jnp.int32(0), unroll=8)
    for load in loads:
        load.wait()

    for d in range(groups):
        for page in range(MAX_PAGES):
            there = page < count_of[d]

            @pl.when(there)
            def _():
                pltpu.make_async_copy(held.at[start_of[d] + page], sends.at[d, page], out_sem).start()

            @pl.when(jnp.logical_not(there))
            def _():
                pltpu.make_async_copy(zero_page, sends.at[d, page], out_sem).start()

    for d in range(groups):
        for page in range(MAX_PAGES):
            pltpu.make_async_copy(zero_page, sends.at[d, page], out_sem).wait()


def prepare(groups, lengths, prefill_of, decode_of, pool):
    page = pool.shape[1:]
    hbm = pl.BlockSpec(memory_space=pl.ANY)
    table = pltpu.SMEM(lengths.shape, jnp.int32)
    return pl.pallas_call(
        prepare_kernel,
        out_shape=jax.ShapeDtypeStruct((groups, MAX_PAGES) + page, pool.dtype),
        in_specs=[hbm] * 4,
        out_specs=hbm,
        scratch_shapes=[
            table,
            table,
            table,
            pltpu.VMEM(pool.shape, pool.dtype),
            pltpu.VMEM(page, pool.dtype),
            pltpu.SMEM((groups + 1,), jnp.int32),
            pltpu.SMEM((groups + 1,), jnp.int32),
            pltpu.SemaphoreType.DMA((3,)),
            pltpu.SemaphoreType.DMA((pool.shape[0],)),
            pltpu.SemaphoreType.DMA,
        ],
        compiler_params=pltpu.CompilerParams(vmem_limit_bytes=VMEM_LIMIT),
        cost_estimate=pl.CostEstimate(flops=0, bytes_accessed=4 * pool.size, transcendentals=0),
        name="outgoing_pages",
    )(lengths, prefill_of, decode_of, pool)


def hand_on_kernel(blocks, arrived, received, held, in_sems, out_sems):
    step = arrived.shape[0] // blocks
    loads, stores = [], []
    for i in range(blocks):
        part = pl.ds(i * step, step)
        loads.append(pltpu.make_async_copy(arrived.at[part], held.at[part], in_sems.at[i]))
        stores.append(pltpu.make_async_copy(held.at[part], received.at[part], out_sems.at[i]))
        loads[-1].start()
    for load, store in zip(loads, stores):
        load.wait()
        store.start()
    for store in stores:
        store.wait()


def hand_on(arrived):
    hbm = pl.BlockSpec(memory_space=pl.ANY)
    blocks = math.gcd(arrived.shape[0], 16)
    return pl.pallas_call(
        functools.partial(hand_on_kernel, blocks),
        out_shape=jax.ShapeDtypeStruct(arrived.shape, arrived.dtype),
        in_specs=[hbm],
        out_specs=hbm,
        scratch_shapes=[
            pltpu.VMEM(arrived.shape, arrived.dtype),
            pltpu.SemaphoreType.DMA((blocks,)),
            pltpu.SemaphoreType.DMA((blocks,)),
        ],
        compiler_params=pltpu.CompilerParams(vmem_limit_bytes=VMEM_LIMIT),
        cost_estimate=pl.CostEstimate(flops=0, bytes_accessed=4 * arrived.size, transcendentals=0),
        name="place_pages",
    )(arrived)


def attend_row(query, pages, length):
    first, second = pages
    kv_heads = first.shape[1] // (2 * HD)
    share = query.shape[0] // kv_heads
    scores = []
    for h in range(kv_heads):
        columns = slice(2 * h * HD, (2 * h + 1) * HD)
        keys = jnp.concatenate([first[:, columns], second[:, columns]], axis=0)
        every = lax.dot_general(
            query, keys, (((1,), (1,)), ((), ())), preferred_element_type=jnp.float32
        )
        scores.append(every[h * share : (h + 1) * share])
    score = jnp.concatenate(scores, axis=0) * (1.0 / math.sqrt(HD))
    live = lax.broadcasted_iota(jnp.int32, score.shape, 1) < length
    masked = jnp.where(live, score, -1e30)
    highest = jnp.max(masked, axis=1, keepdims=True)
    weights = jnp.where(live, jnp.exp(masked - highest), 0.0)
    totals = jnp.sum(weights, axis=1, keepdims=True)
    rounded = weights.astype(jnp.bfloat16)
    mixtures = []
    for h in range(kv_heads):
        columns = slice((2 * h + 1) * HD, (2 * h + 2) * HD)
        values = jnp.concatenate([first[:, columns], second[:, columns]], axis=0)
        every = jnp.dot(rounded, values, preferred_element_type=jnp.float32)
        mixtures.append(every[h * share : (h + 1) * share])
    return jnp.concatenate(mixtures, axis=0) / totals


def attend_kernel(lengths, prefill_of, row_request, queries, incoming, out, rows, held, sems):
    me = lax.axis_index("group")
    row_local, query_heads, _ = queries.shape

    def request_of(b):
        return row_request[me * row_local + b]

    for b in range(row_local):
        pltpu.make_async_copy(incoming.at[prefill_of[request_of(b)]], held.at[b], sems.at[b]).start()
    for first in range(0, row_local, ROW_UNROLL):
        several = range(first, min(first + ROW_UNROLL, row_local))
        for b in several:
            pltpu.make_async_copy(incoming.at[0], held.at[b], sems.at[b]).wait()
        results = []
        for b in several:
            pages = [held[b, page] for page in range(MAX_PAGES)]
            results.append(attend_row(queries[b], pages, lengths[request_of(b)]))
        for b, result in zip(several, results):
            rows[b] = result
    for h in range(query_heads):
        out[:, h * HD : (h + 1) * HD] = rows[:, h, :].astype(out.dtype)


def attend(lengths, prefill_of, row_request, queries, incoming):
    row_local, query_heads, _ = queries.shape
    smem = pl.BlockSpec(memory_space=pltpu.SMEM)
    vmem = pl.BlockSpec(memory_space=pltpu.VMEM)
    hbm = pl.BlockSpec(memory_space=pl.ANY)
    return pl.pallas_call(
        attend_kernel,
        out_shape=jax.ShapeDtypeStruct((row_local, query_heads * HD), jnp.bfloat16),
        in_specs=[smem, smem, smem, vmem, hbm],
        out_specs=vmem,
        scratch_shapes=[
            pltpu.VMEM(queries.shape, jnp.float32),
            pltpu.VMEM((row_local,) + incoming.shape[1:], incoming.dtype),
            pltpu.SemaphoreType.DMA((row_local,)),
        ],
        compiler_params=pltpu.CompilerParams(vmem_limit_bytes=VMEM_LIMIT),
        cost_estimate=pl.CostEstimate(
            flops=1 << 32, bytes_accessed=2 * incoming.size, transcendentals=1 << 20
        ),
        name="attend_rows",
    )(lengths, prefill_of, row_request, queries, incoming)


def project_kernel(dims, offsets, out_weight, *rest):
    shards = rest[: len(offsets)]
    own, *theirs = rest[len(offsets) : -3]
    attended, product, sems = rest[-3:]
    me = lax.axis_index("group")
    heads = lax.axis_size("head")
    my_head = lax.axis_index("head")
    row_local = shards[0].shape[0]
    share = own.shape[0]
    copies = []
    for i, offset in enumerate(offsets):
        place = pl.ds(behind(me, offset, dims) * row_local, row_local)
        copies.append(pltpu.make_async_copy(shards[i], attended.at[place], sems.at[i]))
        copies[-1].start()
    for copy in copies:
        copy.wait()
    product[...] = jnp.dot(attended[...], out_weight[...], preferred_element_type=jnp.float32)
    own[...] = product[pl.ds(pl.multiple_of(my_head * share, share), share)]
    for ahead_by, target in enumerate(theirs, 1):
        start = pl.multiple_of(lax.rem(my_head + ahead_by, heads) * share, share)
        target[...] = product[pl.ds(start, share)].astype(target.dtype)


def project(dims, gathered, out_weight, heads):
    offsets = list(gathered)
    shards = [gathered[offset] for offset in offsets]
    row_local, width = shards[0].shape
    row_total = row_local * len(shards)
    share, columns = row_total // heads, out_weight.shape[1]
    vmem = pl.BlockSpec(memory_space=pltpu.VMEM)
    hbm = pl.BlockSpec(memory_space=pl.ANY)
    theirs = jax.ShapeDtypeStruct((share, columns), jnp.bfloat16)
    return pl.pallas_call(
        functools.partial(project_kernel, dims, offsets),
        out_shape=[jax.ShapeDtypeStruct((share, columns), jnp.float32)] + [theirs] * (heads - 1),
        in_specs=[vmem] + [hbm] * len(shards),
        out_specs=[vmem] * heads,
        scratch_shapes=[
            pltpu.VMEM((row_total, width), jnp.bfloat16),
            pltpu.VMEM((row_total, columns), jnp.float32),
            pltpu.SemaphoreType.DMA((len(shards),)),
        ],
        compiler_params=pltpu.CompilerParams(vmem_limit_bytes=VMEM_LIMIT),
        cost_estimate=pl.CostEstimate(
            flops=2 * row_total * width * columns, bytes_accessed=2 * out_weight.size, transcendentals=0
        ),
        name="project_rows",
    )(pltpu.with_memory_space_constraint(out_weight, pltpu.VMEM), *shards)


def local(kv_pool, lengths, prefill_of, decode_of, row_request, queries, out_weight):
    row_local, query_width = queries.shape
    query_heads = queries.reshape(row_local, query_width // HD, HD)
    dims = factors(lax.axis_size("group"))
    groups = math.prod(dims)
    heads = lax.axis_size("head")

    outgoing = prepare(groups, lengths, prefill_of, decode_of, kv_pool)
    incoming = lax.all_to_all(outgoing, "group", split_axis=0, concat_axis=0, tiled=True)
    rows = attend(lengths, prefill_of, row_request, query_heads, incoming)
    received = hand_on(incoming.reshape((groups * MAX_PAGES,) + kv_pool.shape[1:]))

    own, *theirs = project(dims, gather_shards(rows, dims), out_weight, heads)
    for ahead_by, part in enumerate(theirs, 1):
        pairs = [(h, (h + ahead_by) % heads) for h in range(heads)]
        own = own + lax.ppermute(part, "head", pairs).astype(jnp.float32)
    return (received, own.astype(jnp.bfloat16))


def solution(mesh):
    in_specs = (
        P("group", None, "head"),
        P(),
        P(),
        P(),
        P(),
        P("group", "head"),
        P("head", "group"),
    )
    out_specs = (P("group", None, "head"), P("head", "group"))
    return jax.shard_map(local, mesh=mesh, in_specs=in_specs, out_specs=out_specs, check_vma=False)
```

```python
import functools
import math

import jax
import jax.numpy as jnp
from jax import lax
from jax.experimental import pallas as pl
from jax.experimental.pallas import tpu as pltpu
from jax.sharding import PartitionSpec as P

HD = 128
MAX_PAGES = 2
WAVE = 3
ROW_UNROLL = 4
EARLY = 4
VMEM_LIMIT = 40 * 1024 * 1024


def factors(groups):
    near = math.gcd(groups, 4)
    return groups // near, near


def uniform(step, swap, dims):
    return tuple(((z + step) % dims[0], swap) for z in range(dims[0]))


def page_rounds(dims):
    far, near = dims
    if far != 4:
        near_rounds = [uniform(0, n, dims) for n in range(1, near)]
        return near_rounds + [uniform(z, n, dims) for z in range(1, far) for n in range(near)]
    outer = [((2, n), (0, n), (3, n), (1, n)) for n in range(near)]
    inner = [((1, n), (3, n), (0, n), (2, n)) for n in range(near)]
    outer += [((3, n), (1, n), (2, n), (0, n)) for n in range(1, near)]
    inner += [((0, n), (2, n), (1, n), (3, n)) for n in range(1, near)]
    return outer + [((3, 0), (2, 0), (1, 0), (0, 0))] + inner


def reverse(route):
    sources = {to: (z, swap) for z, (to, swap) in enumerate(route)}
    return tuple(sources[z] for z in range(len(route)))


def routed(me, route, dims):
    near = dims[1]
    z = me // near
    to, swap = jnp.int32(route[0][0]), jnp.int32(route[0][1])
    for place in range(1, dims[0]):
        to = jnp.where(z == place, route[place][0], to)
        swap = jnp.where(z == place, route[place][1], swap)
    return to * near + (me % near ^ swap)


def send_by(array, route, dims):
    far, near = dims
    pairs = [
        (z * near + n, route[z][0] * near + (n ^ route[z][1])) for z in range(far) for n in range(near)
    ]
    return lax.ppermute(array, "group", pairs)


def gather_shards(shard, dims):
    far, near = dims
    held = {(0, 0): shard}
    swaps = [1 << i for i in reversed(range(near.bit_length() - 1))]
    for stage in [[(z, 0) for z in range(1, far)]] + [[(0, n)] for n in swaps]:
        incoming = {}
        for step in stage:
            for offset, array in held.items():
                moved = send_by(array, uniform(*step, dims), dims)
                incoming[offset[0] + step[0], offset[1] | step[1]] = moved
        held.update(incoming)
    return held


def packed(lengths, prefill_of, decode_of, groups):
    bits = (groups - 1).bit_length()
    return (lengths << 2 * bits) | (prefill_of << bits) | decode_of


def unpacked(entry, groups):
    bits = (groups - 1).bit_length()
    mask = (1 << bits) - 1
    return entry >> 2 * bits, (entry >> bits) & mask, entry & mask


def prepare_kernel(dims, routes, own, table_hbm, pool, *rest):
    aliased = 0 if own else 1
    received, *sends = rest[aliased : aliased + 1 + len(routes)]
    table, held, zero_page, start_of, count_of, table_sem, in_sems, out_sem = rest[aliased + 1 + len(routes) :]
    me = lax.axis_index("group")
    groups = lax.axis_size("group")
    page_size = pool.shape[1]
    copy = pltpu.make_async_copy(table_hbm, table, table_sem)
    copy.start()
    for d in range(groups + 1):
        start_of[d] = 0
        count_of[d] = 0
    zero_page[...] = jnp.zeros_like(zero_page)
    copy.wait()

    def visit(r, running):
        length, home, destination = unpacked(table[r], groups)
        mine = home == me
        count = (length + page_size - 1) // page_size
        to = jnp.where(mine, destination, groups)
        start_of[to] = running
        count_of[to] = count
        return running + jnp.where(mine, count, 0)

    lax.fori_loop(0, table.shape[0], visit, jnp.int32(0), unroll=8)
    targets = [(routed(me, route, dims), send, 0) for route, send in zip(routes, sends)]
    if own:
        targets.append((me, received, me * MAX_PAGES))

    def each(do):
        for i, (to, target, base) in enumerate(targets):
            for page in range(MAX_PAGES):
                there = page < count_of[to]
                source = pool.at[jnp.where(there, start_of[to] + page, 0)]
                buffer, place = held.at[i, page], target.at[base + page]
                do(there, (source, buffer, in_sems.at[i, page]), (buffer, place, out_sem), (zero_page, place, out_sem))

    def fetch(there, load, store, blank):
        @pl.when(there)
        def _():
            pltpu.make_async_copy(*load).start()

        @pl.when(jnp.logical_not(there))
        def _():
            pltpu.make_async_copy(*blank).start()

    def forward(there, load, store, blank):
        @pl.when(there)
        def _():
            pltpu.make_async_copy(*load).wait()
            pltpu.make_async_copy(*store).start()

    def finish(there, load, store, blank):
        pltpu.make_async_copy(*blank).wait()

    each(fetch)
    each(forward)
    each(finish)


def prepare(dims, routes, table, pool, received=None):
    own = received is None
    groups = lax.axis_size("group")
    page = pool.shape[1:]
    blocks = len(routes) + (1 if own else 0)
    hbm = pl.BlockSpec(memory_space=pl.ANY)
    block = jax.ShapeDtypeStruct((MAX_PAGES,) + page, pool.dtype)
    outs = [jax.ShapeDtypeStruct((groups * MAX_PAGES,) + page, pool.dtype)] + [block] * len(routes)
    operands = [table, pool] + ([] if own else [received])
    return pl.pallas_call(
        functools.partial(prepare_kernel, dims, routes, own),
        out_shape=outs,
        in_specs=[hbm] * len(operands),
        out_specs=[hbm] * len(outs),
        scratch_shapes=[
            pltpu.SMEM(table.shape, jnp.int32),
            pltpu.VMEM((blocks, MAX_PAGES) + page, pool.dtype),
            pltpu.VMEM(page, pool.dtype),
            pltpu.SMEM((groups + 1,), jnp.int32),
            pltpu.SMEM((groups + 1,), jnp.int32),
            pltpu.SemaphoreType.DMA,
            pltpu.SemaphoreType.DMA((blocks, MAX_PAGES)),
            pltpu.SemaphoreType.DMA,
        ],
        input_output_aliases={} if own else {2: 0},
        compiler_params=pltpu.CompilerParams(vmem_limit_bytes=VMEM_LIMIT),
        cost_estimate=pl.CostEstimate(
            flops=0, bytes_accessed=4 * blocks * MAX_PAGES * math.prod(page), transcendentals=0
        ),
        name="outgoing_pages",
    )(*operands)


def attend_row(query, pages, length):
    first, second = pages
    kv_heads = first.shape[1] // (2 * HD)
    share = query.shape[0] // kv_heads
    scores = []
    for h in range(kv_heads):
        columns = slice(2 * h * HD, (2 * h + 1) * HD)
        keys = jnp.concatenate([first[:, columns], second[:, columns]], axis=0)
        every = lax.dot_general(
            query, keys, (((1,), (1,)), ((), ())), preferred_element_type=jnp.float32
        )
        scores.append(every[h * share : (h + 1) * share])
    score = jnp.concatenate(scores, axis=0) * (1.0 / math.sqrt(HD))
    live = lax.broadcasted_iota(jnp.int32, score.shape, 1) < length
    masked = jnp.where(live, score, -1e30)
    highest = jnp.max(masked, axis=1, keepdims=True)
    weights = jnp.where(live, jnp.exp(masked - highest), 0.0)
    totals = jnp.sum(weights, axis=1, keepdims=True)
    rounded = weights.astype(jnp.bfloat16)
    mixtures = []
    for h in range(kv_heads):
        columns = slice((2 * h + 1) * HD, (2 * h + 2) * HD)
        values = jnp.concatenate([first[:, columns], second[:, columns]], axis=0)
        every = jnp.dot(rounded, values, preferred_element_type=jnp.float32)
        mixtures.append(every[h * share : (h + 1) * share])
    return jnp.concatenate(mixtures, axis=0) / totals


def settle_kernel(dims, routes, own, last, table, row_request, queries, rows_in, received_in, *rest):
    blocks = rest[: len(routes)]
    received, out, rows, held, list_row, list_block, list_length, in_sems, out_sems = rest[len(routes) :]
    me = lax.axis_index("group")
    row_local, query_heads, _ = queries.shape
    mine = pl.ds(me * MAX_PAGES, MAX_PAGES)
    origins = [routed(me, reverse(route), dims) for route in routes]
    places = [pl.ds(origin * MAX_PAGES, MAX_PAGES) for origin in origins]
    sources = list(blocks) + ([received_in.at[mine]] if own else [])
    origins += [me] if own else []
    loads = [pltpu.make_async_copy(s, held.at[i], in_sems.at[i]) for i, s in enumerate(sources)]
    stores = [
        pltpu.make_async_copy(held.at[i], received.at[place], out_sems.at[i]) for i, place in enumerate(places)
    ]
    for load in loads:
        load.start()

    found = jnp.int32(0)
    for b in range(row_local):
        length, home, _ = unpacked(table[row_request[me * row_local + b]], math.prod(dims))
        block, match = jnp.int32(0), jnp.int32(0)
        for i, origin in enumerate(origins):
            block = jnp.where(home == origin, i, block)
            match = jnp.where(home == origin, 1, match)
        list_row[found] = b
        list_block[found] = block
        list_length[found] = length
        found = found + match
    for i in range(ROW_UNROLL):
        list_row[found + i] = row_local
        list_block[found + i] = 0
        list_length[found + i] = 1
    rows[:row_local] = rows_in[...]
    for load in loads:
        load.wait()
    for store in stores:
        store.start()

    @pl.loop(0, (found + ROW_UNROLL - 1) // ROW_UNROLL)
    def _(step):
        results = []
        for i in range(ROW_UNROLL):
            at = step * ROW_UNROLL + i
            query = queries[jnp.minimum(list_row[at], row_local - 1)]
            pages = [held[list_block[at], page] for page in range(MAX_PAGES)]
            results.append(attend_row(query, pages, list_length[at]))
        for i, result in enumerate(results):
            rows[list_row[step * ROW_UNROLL + i]] = result

    if last:
        for h in range(query_heads):
            out[:, h * HD : (h + 1) * HD] = rows[:row_local, h, :].astype(out.dtype)
    else:
        out[...] = rows[:row_local]
    for store in stores:
        store.wait()


def settle(dims, routes, own, last, table, row_request, queries, rows, received, blocks):
    row_local, query_heads, _ = queries.shape
    smem = pl.BlockSpec(memory_space=pltpu.SMEM)
    vmem = pl.BlockSpec(memory_space=pltpu.VMEM)
    hbm = pl.BlockSpec(memory_space=pl.ANY)
    count = len(blocks) + (1 if own else 0)
    if last:
        out = jax.ShapeDtypeStruct((row_local, query_heads * HD), jnp.bfloat16)
    else:
        out = jax.ShapeDtypeStruct(rows.shape, rows.dtype)
    return pl.pallas_call(
        functools.partial(settle_kernel, dims, routes, own, last),
        out_shape=[jax.ShapeDtypeStruct(received.shape, received.dtype), out],
        in_specs=[smem, smem, vmem, vmem, hbm] + [hbm] * len(blocks),
        out_specs=[hbm, vmem],
        scratch_shapes=[
            pltpu.VMEM((row_local + 1, query_heads, HD), jnp.float32),
            pltpu.VMEM((count, MAX_PAGES) + received.shape[1:], received.dtype),
            pltpu.SMEM((row_local + ROW_UNROLL,), jnp.int32),
            pltpu.SMEM((row_local + ROW_UNROLL,), jnp.int32),
            pltpu.SMEM((row_local + ROW_UNROLL,), jnp.int32),
            pltpu.SemaphoreType.DMA((count,)),
            pltpu.SemaphoreType.DMA((count,)),
        ],
        input_output_aliases={4: 0},
        compiler_params=pltpu.CompilerParams(vmem_limit_bytes=VMEM_LIMIT),
        cost_estimate=pl.CostEstimate(
            flops=1 << 30, bytes_accessed=4 * sum(b.size for b in blocks), transcendentals=1 << 18
        ),
        name="settle_pages",
    )(table, row_request, queries, rows, received, *blocks)


def project_kernel(dims, offsets, out_weight, *rest):
    shards = rest[: len(offsets)]
    own, *theirs = rest[len(offsets) : -3]
    attended, product, sems = rest[-3:]
    me = lax.axis_index("group")
    heads = lax.axis_size("head")
    my_head = lax.axis_index("head")
    row_local = shards[0].shape[0]
    share = own.shape[0]
    copies = []
    for i, offset in enumerate(offsets):
        place = pl.ds(routed(me, reverse(uniform(*offset, dims)), dims) * row_local, row_local)
        copies.append(pltpu.make_async_copy(shards[i], attended.at[place], sems.at[i]))
        copies[-1].start()
    for copy in copies:
        copy.wait()
    product[...] = jnp.dot(attended[...], out_weight[...], preferred_element_type=jnp.float32)
    own[...] = product[pl.ds(pl.multiple_of(my_head * share, share), share)]
    for ahead_by, target in enumerate(theirs, 1):
        start = pl.multiple_of(lax.rem(my_head + ahead_by, heads) * share, share)
        target[...] = product[pl.ds(start, share)].astype(target.dtype)


def project(dims, gathered, out_weight, heads):
    offsets = list(gathered)
    shards = [gathered[offset] for offset in offsets]
    row_local, width = shards[0].shape
    row_total = row_local * len(shards)
    share, columns = row_total // heads, out_weight.shape[1]
    vmem = pl.BlockSpec(memory_space=pltpu.VMEM)
    hbm = pl.BlockSpec(memory_space=pl.ANY)
    theirs = jax.ShapeDtypeStruct((share, columns), jnp.bfloat16)
    return pl.pallas_call(
        functools.partial(project_kernel, dims, offsets),
        out_shape=[jax.ShapeDtypeStruct((share, columns), jnp.float32)] + [theirs] * (heads - 1),
        in_specs=[vmem] + [hbm] * len(shards),
        out_specs=[vmem] * heads,
        scratch_shapes=[
            pltpu.VMEM((row_total, width), jnp.bfloat16),
            pltpu.VMEM((row_total, columns), jnp.float32),
            pltpu.SemaphoreType.DMA((len(shards),)),
        ],
        compiler_params=pltpu.CompilerParams(vmem_limit_bytes=VMEM_LIMIT),
        cost_estimate=pl.CostEstimate(
            flops=2 * row_total * width * columns, bytes_accessed=2 * out_weight.size, transcendentals=0
        ),
        name="project_rows",
    )(pltpu.with_memory_space_constraint(out_weight, pltpu.VMEM), *shards)


def local(kv_pool, lengths, prefill_of, decode_of, row_request, queries, out_weight):
    row_local, query_width = queries.shape
    query_heads = queries.reshape(row_local, query_width // HD, HD)
    heads = lax.axis_size("head")

    dims = factors(lax.axis_size("group"))
    routes = page_rounds(dims)
    table = packed(lengths, prefill_of, decode_of, math.prod(dims))
    received, *early = prepare(dims, routes[:EARLY], table, kv_pool)
    received, *late = prepare(dims, routes[EARLY:], table, kv_pool, received)
    arrived = [send_by(block, route, dims) for block, route in zip(early + late, routes)]
    rows = jnp.zeros(query_heads.shape, jnp.float32)
    for first in range(0, len(routes), WAVE):
        wave = slice(first, first + WAVE)
        last = first + WAVE >= len(routes)
        received, rows = settle(
            dims, routes[wave], first == 0, last, table, row_request, query_heads, rows, received, arrived[wave]
        )

    own, *theirs = project(dims, gather_shards(rows, dims), out_weight, heads)
    for ahead_by, part in enumerate(theirs, 1):
        pairs = [(h, (h + ahead_by) % heads) for h in range(heads)]
        own = own + lax.ppermute(part, "head", pairs).astype(jnp.float32)
    return (received, own.astype(jnp.bfloat16))


def solution(mesh):
    in_specs = (
        P("group", None, "head"),
        P(),
        P(),
        P(),
        P(),
        P("group", "head"),
        P("head", "group"),
    )
    out_specs = (P("group", None, "head"), P("head", "group"))
    return jax.shard_map(local, mesh=mesh, in_specs=in_specs, out_specs=out_specs, check_vma=False)
```

```python
import functools
import math

import jax
import jax.numpy as jnp
from jax import lax
from jax.experimental import pallas as pl
from jax.experimental.pallas import tpu as pltpu
from jax.sharding import PartitionSpec as P

HD = 128
MAX_PAGES = 2
ROW_UNROLL = 4
EARLY = 4
VMEM_LIMIT = 57 * 1024 * 1024


def factors(groups):
    near = math.gcd(groups, 4)
    return groups // near, near


def uniform(step, swap, dims):
    return tuple(((z + step) % dims[0], swap) for z in range(dims[0]))


def page_rounds(dims):
    far, near = dims
    steps = sorted(range(1, far), key=lambda z: (min(z, far - z), z))
    order = [(z, n) for z in steps for n in range(near)]
    for n in range(1, near):
        order.insert(min(2 * n, len(order)), (0, n))
    return [uniform(z, n, dims) for z, n in order]


def reverse(route):
    sources = {to: (z, swap) for z, (to, swap) in enumerate(route)}
    return tuple(sources[z] for z in range(len(route)))


def routed(me, route, dims):
    near = dims[1]
    z = me // near
    to, swap = jnp.int32(route[0][0]), jnp.int32(route[0][1])
    for place in range(1, dims[0]):
        to = jnp.where(z == place, route[place][0], to)
        swap = jnp.where(z == place, route[place][1], swap)
    return to * near + (me % near ^ swap)


def send_by(array, route, dims):
    far, near = dims
    pairs = [
        (z * near + n, route[z][0] * near + (n ^ route[z][1])) for z in range(far) for n in range(near)
    ]
    return lax.ppermute(array, "group", pairs)


def gather_stages(dims):
    far, near = dims
    swaps = [1 << i for i in reversed(range(near.bit_length() - 1))]
    return [[(z, 0) for z in range(1, far)]] + [[(0, n)] for n in swaps]


def gather_shards(shard, dims):
    held = {(0, 0): shard}
    for stage in gather_stages(dims):
        incoming = {}
        for step in stage:
            for offset, array in held.items():
                moved = send_by(array, uniform(*step, dims), dims)
                incoming[offset[0] + step[0], offset[1] | step[1]] = moved
        held.update(incoming)
    return {offset: (array, 0) for offset, array in held.items()}


def gather_stacked(shard, dims):
    rows = shard.shape[0]
    held, whole = {(0, 0): (shard, 0)}, shard
    for stage in gather_stages(dims):
        arrays, offsets = [whole], list(held)
        before = dict(held)
        for step in stage:
            moved = send_by(whole, uniform(*step, dims), dims)
            arrays.append(moved)
            for offset, (_, row) in before.items():
                held[offset[0] + step[0], offset[1] | step[1]] = (moved, row)
        yield arrays[1:], held
        whole = jnp.concatenate(arrays, axis=0)
        held = {}
        for i, step in enumerate([(0, 0)] + stage):
            for offset, (_, row) in before.items():
                held[offset[0] + step[0], offset[1] | step[1]] = (whole, i * len(offsets) * rows + row)


def packed(lengths, prefill_of, decode_of, groups):
    bits = (groups - 1).bit_length()
    return (lengths << 2 * bits) | (prefill_of << bits) | decode_of


def unpacked(entry, groups):
    bits = (groups - 1).bit_length()
    mask = (1 << bits) - 1
    return entry >> 2 * bits, (entry >> bits) & mask, entry & mask


def prepare_kernel(dims, sendings, columns, own, table_hbm, pool, *rest):
    table, held, zero_page, start_of, count_of, table_sem, in_sems, out_sem = rest[-8:]
    received, *sends = rest[-9 - len(sendings) : -8]
    me = lax.axis_index("group")
    groups = lax.axis_size("group")
    page_size = pool.shape[1]
    copy = pltpu.make_async_copy(table_hbm, table, table_sem)
    copy.start()
    for d in range(groups + 1):
        start_of[d] = 0
        count_of[d] = 0
    zero_page[...] = jnp.zeros_like(zero_page)
    copy.wait()

    def visit(r, running):
        length, home, destination = unpacked(table[r], groups)
        mine = home == me
        count = (length + page_size - 1) // page_size
        to = jnp.where(mine, destination, groups)
        start_of[to] = running
        count_of[to] = count
        return running + jnp.where(mine, count, 0)

    lax.fori_loop(0, table.shape[0], visit, jnp.int32(0), unroll=8)
    targets = [
        (routed(me, route, dims), send, 0, columns[part]) for (route, part), send in zip(sendings, sends)
    ]
    if own:
        targets.append((me, received, me * MAX_PAGES, (0, pool.shape[2])))

    def each(do):
        for i, (to, target, base, (first, width)) in enumerate(targets):
            for page in range(MAX_PAGES):
                there = page < count_of[to]
                lanes = pl.ds(first, width)
                source = pool.at[jnp.where(there, start_of[to] + page, 0), :, lanes]
                buffer, place = held.at[i, page, :, pl.ds(0, width)], target.at[base + page]
                blank = zero_page.at[:, pl.ds(0, width)]
                do(there, (source, buffer, in_sems.at[i, page]), (buffer, place, out_sem), (blank, place, out_sem))

    def fetch(there, load, store, blank):
        @pl.when(there)
        def _():
            pltpu.make_async_copy(*load).start()

        @pl.when(jnp.logical_not(there))
        def _():
            pltpu.make_async_copy(*blank).start()

    def forward(there, load, store, blank):
        @pl.when(there)
        def _():
            pltpu.make_async_copy(*load).wait()
            pltpu.make_async_copy(*store).start()

    def finish(there, load, store, blank):
        pltpu.make_async_copy(*blank).wait()

    each(fetch)
    each(forward)
    each(finish)


def prepare(dims, sendings, columns, table, pool, received=None, after=()):
    own = received is None
    groups = math.prod(dims)
    page_size, width = pool.shape[1:]
    count = len(sendings) + (1 if own else 0)
    widest = width if own else max(w for _, w in columns)
    hbm = pl.BlockSpec(memory_space=pl.ANY)
    outs = [jax.ShapeDtypeStruct((groups * MAX_PAGES, page_size, width), pool.dtype)]
    outs += [jax.ShapeDtypeStruct((MAX_PAGES, page_size, columns[part][1]), pool.dtype) for _, part in sendings]
    operands = [table, pool] + ([] if own else [received]) + list(after)
    return pl.pallas_call(
        functools.partial(prepare_kernel, dims, sendings, columns, own),
        out_shape=outs,
        in_specs=[hbm] * len(operands),
        out_specs=[hbm] * len(outs),
        scratch_shapes=[
            pltpu.SMEM(table.shape, jnp.int32),
            pltpu.VMEM((count, MAX_PAGES, page_size, widest), pool.dtype),
            pltpu.VMEM((page_size, widest), pool.dtype),
            pltpu.SMEM((groups + 1,), jnp.int32),
            pltpu.SMEM((groups + 1,), jnp.int32),
            pltpu.SemaphoreType.DMA,
            pltpu.SemaphoreType.DMA((count, MAX_PAGES)),
            pltpu.SemaphoreType.DMA,
        ],
        input_output_aliases={} if own else {2: 0},
        compiler_params=pltpu.CompilerParams(vmem_limit_bytes=VMEM_LIMIT),
        cost_estimate=pl.CostEstimate(
            flops=0, bytes_accessed=4 * sum(math.prod(o.shape) for o in outs[1:]), transcendentals=0
        ),
        name="outgoing_pages",
    )(*operands)


def attend_row(query, pages, length):
    first, second = pages
    kv_heads = first.shape[1] // (2 * HD)
    share = query.shape[0] // kv_heads
    scores = []
    for h in range(kv_heads):
        columns = slice(2 * h * HD, (2 * h + 1) * HD)
        keys = jnp.concatenate([first[:, columns], second[:, columns]], axis=0)
        every = lax.dot_general(
            query, keys, (((1,), (1,)), ((), ())), preferred_element_type=jnp.float32
        )
        scores.append(every[h * share : (h + 1) * share])
    score = jnp.concatenate(scores, axis=0) * (1.0 / math.sqrt(HD))
    live = lax.broadcasted_iota(jnp.int32, score.shape, 1) < length
    masked = jnp.where(live, score, -1e30)
    highest = jnp.max(masked, axis=1, keepdims=True)
    weights = jnp.where(live, jnp.exp(masked - highest), 0.0)
    totals = jnp.sum(weights, axis=1, keepdims=True)
    rounded = weights.astype(jnp.bfloat16)
    mixtures = []
    for h in range(kv_heads):
        columns = slice((2 * h + 1) * HD, (2 * h + 2) * HD)
        values = jnp.concatenate([first[:, columns], second[:, columns]], axis=0)
        every = jnp.dot(rounded, values, preferred_element_type=jnp.float32)
        mixtures.append(every[h * share : (h + 1) * share])
    return jnp.concatenate(mixtures, axis=0) / totals


def settle_kernel(dims, routes, lanes, heads_here, own, last, table, row_request, queries, rows_in, received_in, *rest):
    blocks = rest[: len(routes)]
    received, out, rows, held, list_row, list_block, list_length, in_sems, out_sems = rest[-9:]
    me = lax.axis_index("group")
    row_local = queries.shape[0]
    first_head, head_count = heads_here
    mine = pl.ds(me * MAX_PAGES, MAX_PAGES)
    lanes = pl.ds(*lanes)
    origins = [routed(me, reverse(route), dims) for route in routes]
    places = [pl.ds(origin * MAX_PAGES, MAX_PAGES) for origin in origins]
    sources = list(blocks) + ([received_in.at[mine, :, lanes]] if own else [])
    origins += [me] if own else []
    loads = [pltpu.make_async_copy(s, held.at[i], in_sems.at[i]) for i, s in enumerate(sources)]
    stores = [
        pltpu.make_async_copy(held.at[i], received.at[place, :, lanes], out_sems.at[i])
        for i, place in enumerate(places)
    ]
    for load in loads:
        load.start()

    found = jnp.int32(0)
    for b in range(row_local):
        length, home, _ = unpacked(table[row_request[me * row_local + b]], math.prod(dims))
        block, match = jnp.int32(0), jnp.int32(0)
        for i, origin in enumerate(origins):
            block = jnp.where(home == origin, i, block)
            match = jnp.where(home == origin, 1, match)
        list_row[found] = b
        list_block[found] = block
        list_length[found] = length
        found = found + match
    for i in range(ROW_UNROLL):
        list_row[found + i] = row_local
        list_block[found + i] = 0
        list_length[found + i] = 1
    rows[:row_local] = rows_in[...]
    for load in loads:
        load.wait()
    for store in stores:
        store.start()

    @pl.loop(0, (found + ROW_UNROLL - 1) // ROW_UNROLL)
    def _(step):
        results = []
        for i in range(ROW_UNROLL):
            at = step * ROW_UNROLL + i
            query = queries[jnp.minimum(list_row[at], row_local - 1), first_head : first_head + head_count]
            pages = [held[list_block[at], page] for page in range(MAX_PAGES)]
            results.append(attend_row(query, pages, list_length[at]))
        for i, result in enumerate(results):
            rows[list_row[step * ROW_UNROLL + i]] = result

    if last:
        for h in range(head_count):
            out[:, h * HD : (h + 1) * HD] = rows[:row_local, h, :].astype(out.dtype)
    else:
        out[...] = rows[:row_local]
    for store in stores:
        store.wait()


def settle(dims, routes, lanes, heads_here, own, last, table, row_request, queries, rows, received, blocks, after):
    row_local = queries.shape[0]
    smem = pl.BlockSpec(memory_space=pltpu.SMEM)
    vmem = pl.BlockSpec(memory_space=pltpu.VMEM)
    hbm = pl.BlockSpec(memory_space=pl.ANY)
    count = len(blocks) + (1 if own else 0)
    if last:
        out = jax.ShapeDtypeStruct((row_local, heads_here[1] * HD), jnp.bfloat16)
    else:
        out = jax.ShapeDtypeStruct(rows.shape, rows.dtype)
    return pl.pallas_call(
        functools.partial(settle_kernel, dims, routes, lanes, heads_here, own, last),
        out_shape=[jax.ShapeDtypeStruct(received.shape, received.dtype), out],
        in_specs=[smem, smem, vmem, vmem, hbm] + [hbm] * (len(blocks) + len(after)),
        out_specs=[hbm, vmem],
        scratch_shapes=[
            pltpu.VMEM((row_local + 1,) + rows.shape[1:], jnp.float32),
            pltpu.VMEM((count, MAX_PAGES, received.shape[1], lanes[1]), received.dtype),
            pltpu.SMEM((row_local + ROW_UNROLL,), jnp.int32),
            pltpu.SMEM((row_local + ROW_UNROLL,), jnp.int32),
            pltpu.SMEM((row_local + ROW_UNROLL,), jnp.int32),
            pltpu.SemaphoreType.DMA((count,)),
            pltpu.SemaphoreType.DMA((count,)),
        ],
        input_output_aliases={4: 0},
        compiler_params=pltpu.CompilerParams(vmem_limit_bytes=VMEM_LIMIT),
        cost_estimate=pl.CostEstimate(
            flops=1 << 30, bytes_accessed=4 * sum(b.size for b in blocks), transcendentals=1 << 18
        ),
        name="settle_pages",
    )(table, row_request, queries, rows, received, *blocks, *after)


def project_kernel(dims, pieces, arrays, row_local, aheads, inputs, added, out_weight, *rest):
    stacks = rest[:arrays]
    partials = rest[arrays : arrays + added]
    outs = rest[arrays + added : -2]
    attended, sems = rest[-2:]
    me = lax.axis_index("group")
    heads = lax.axis_size("head")
    my_head = lax.axis_index("head")
    share = outs[0].shape[0]

    def each(do):
        for i, (offset, stack, first) in enumerate(pieces):
            row = routed(me, reverse(uniform(*offset, dims)), dims) * row_local
            ahead = lax.rem(row // share - my_head + heads, heads)
            for at, wanted in enumerate(aheads):

                @pl.when(ahead == wanted)
                def _():
                    place = attended.at[pl.ds(pl.multiple_of(at * share + lax.rem(row, share), row_local), row_local)]
                    do(pltpu.make_async_copy(stacks[stack].at[pl.ds(first, row_local)], place, sems.at[i]))

    each(lambda copy: copy.start())
    each(lambda copy: copy.wait())
    product = jnp.dot(attended[...], out_weight[pl.ds(*inputs)], preferred_element_type=jnp.float32)
    for at, (ahead, out) in enumerate(zip(aheads, outs)):
        block = product[at * share : (at + 1) * share]
        if added:
            block = block + partials[ahead][...]
        out[...] = block.astype(out.dtype)


def project(dims, gathered, row_local, out_weight, inputs, heads, aheads, dtype, added=()):
    stacks = list({id(array): array for array, _ in gathered.values()}.values())
    places = {id(array): i for i, array in enumerate(stacks)}
    pieces = [(offset, places[id(array)], first) for offset, (array, first) in gathered.items()]
    width, columns = stacks[0].shape[1], out_weight.shape[1]
    share = row_local * len(pieces) // heads
    vmem = pl.BlockSpec(memory_space=pltpu.VMEM)
    hbm = pl.BlockSpec(memory_space=pl.ANY)
    return pl.pallas_call(
        functools.partial(project_kernel, dims, pieces, len(stacks), row_local, aheads, inputs, len(added)),
        out_shape=[jax.ShapeDtypeStruct((share, columns), dtype)] * len(aheads),
        in_specs=[vmem] + [hbm] * len(stacks) + [vmem] * len(added),
        out_specs=[vmem] * len(aheads),
        scratch_shapes=[
            pltpu.VMEM((len(aheads) * share, width), jnp.bfloat16),
            pltpu.SemaphoreType.DMA((len(pieces),)),
        ],
        compiler_params=pltpu.CompilerParams(vmem_limit_bytes=VMEM_LIMIT),
        cost_estimate=pl.CostEstimate(
            flops=2 * len(aheads) * share * width * columns, bytes_accessed=2 * width * columns, transcendentals=0
        ),
        name="project_rows",
    )(out_weight, *stacks, *added)


def local(kv_pool, lengths, prefill_of, decode_of, row_request, queries, out_weight):
    row_local, query_width = queries.shape
    query_heads = query_width // HD
    queries = queries.reshape(row_local, query_heads, HD)
    kv_heads = kv_pool.shape[2] // (2 * HD)
    share = query_heads // kv_heads
    dims = factors(lax.axis_size("group"))
    heads = lax.axis_size("head")

    cut = kv_heads // 2
    parts = [(first, last - first) for first, last in ((0, cut), (cut, kv_heads)) if last > first]
    columns = [(first * 2 * HD, count * 2 * HD) for first, count in parts]

    routes = page_rounds(dims)
    total = len(routes)
    table = packed(lengths, prefill_of, decode_of, math.prod(dims))
    received, arrived = None, {}

    def send(*several, after=()):
        nonlocal received
        chosen = [(part, i) for part, first, last in several for i in range(first, last)]
        sendings = [(routes[i], part) for part, i in chosen]
        received, *blocks = prepare(dims, sendings, columns, table, kv_pool, received, after)
        for (part, i), block in zip(chosen, blocks):
            arrived[part, i] = send_by(block, routes[i], dims)

    def take(part, first, last, rows, after=()):
        nonlocal received
        head_first, head_count = parts[part][0] * share, parts[part][1] * share
        if rows is None:
            rows = jnp.zeros((row_local, head_count, HD), jnp.float32)
        blocks = [arrived[part, i] for i in range(first, last)]
        received, rows = settle(
            dims, routes[first:last], columns[part], (head_first, head_count), first == 0, last == total,
            table, row_request, queries, rows, received, blocks, list(after),
        )
        return rows

    weight = pltpu.with_memory_space_constraint(out_weight, pltpu.VMEM)
    inputs = [(first * share * HD, count * share * HD) for first, count in parts]
    fifth = total // 5
    send((0, 0, EARLY))
    if len(parts) == 1:
        send((0, EARLY, total))
        rows = take(0, 0, 2 * fifth, None)
        rows = take(0, 2 * fifth, 4 * fifth, rows)
        rows = take(0, 4 * fifth, total, rows)
        done = []
    else:
        send((0, EARLY, total), (1, 0, fifth))
        rows = take(0, 0, 2 * fifth, None)
        rows = take(0, 2 * fifth, 4 * fifth, rows)
        send((1, fifth, 5 * fifth // 2 + 1))
        rows = take(0, 4 * fifth, total, rows)
        stages = gather_stacked(rows, dims)
        landed, _ = next(stages)
        send((1, 5 * fifth // 2 + 1, 7 * fifth // 2 + 1), after=landed)
        landed, _ = next(stages)
        rows = take(1, 0, fifth, None)
        send((1, 7 * fifth // 2 + 1, total), after=landed)
        for landed, gathered in stages:
            pass
        rows = take(1, fifth, 2 * fifth, rows)
        rows = take(1, 2 * fifth, 4 * fifth, rows, after=landed)
        done = project(dims, gathered, row_local, weight, inputs[0], heads, range(heads), jnp.float32)
        rows = take(1, 4 * fifth, total, rows, after=done)
    gathered = gather_shards(rows, dims)

    theirs = project(dims, gathered, row_local, weight, inputs[-1], heads, range(1, heads), jnp.bfloat16, done)
    (own,) = project(dims, gathered, row_local, weight, inputs[-1], heads, range(1), jnp.float32, done)
    for ahead, part in enumerate(theirs, 1):
        pairs = [(h, (h + ahead) % heads) for h in range(heads)]
        own = own + lax.ppermute(part, "head", pairs).astype(jnp.float32)
    return (received, own.astype(jnp.bfloat16))


def solution(mesh):
    in_specs = (
        P("group", None, "head"),
        P(),
        P(),
        P(),
        P(),
        P("group", "head"),
        P("head", "group"),
    )
    out_specs = (P("group", None, "head"), P("head", "group"))
    return jax.shard_map(local, mesh=mesh, in_specs=in_specs, out_specs=out_specs, check_vma=False)
```

```python
import functools
import math

import jax
import jax.numpy as jnp
from jax import lax
from jax.experimental import pallas as pl
from jax.experimental.pallas import tpu as pltpu
from jax.sharding import PartitionSpec as P

HD = 128
MAX_PAGES = 2
WAVE = 3
ROW_UNROLL = 4
EARLY = 4
VMEM_LIMIT = 57 * 1024 * 1024


def factors(groups):
    near = math.gcd(groups, 4)
    return groups // near, near


def uniform(step, swap, dims):
    return tuple(((z + step) % dims[0], swap) for z in range(dims[0]))


def page_rounds(dims):
    far, near = dims
    steps = sorted(range(1, far), key=lambda z: (min(z, far - z), z))
    order = [(z, n) for z in steps for n in range(near)]
    for n in range(1, near):
        order.insert(min(2 * n, len(order)), (0, n))
    return [uniform(z, n, dims) for z, n in order]


def reverse(route):
    sources = {to: (z, swap) for z, (to, swap) in enumerate(route)}
    return tuple(sources[z] for z in range(len(route)))


def routed(me, route, dims):
    near = dims[1]
    z = me // near
    to, swap = jnp.int32(route[0][0]), jnp.int32(route[0][1])
    for place in range(1, dims[0]):
        to = jnp.where(z == place, route[place][0], to)
        swap = jnp.where(z == place, route[place][1], swap)
    return to * near + (me % near ^ swap)


def send_by(array, route, dims):
    far, near = dims
    pairs = [
        (z * near + n, route[z][0] * near + (n ^ route[z][1])) for z in range(far) for n in range(near)
    ]
    return lax.ppermute(array, "group", pairs)


def gather_shards(shard, dims):
    far, near = dims
    held = {(0, 0): shard}
    swaps = [1 << i for i in reversed(range(near.bit_length() - 1))]
    for stage in [[(z, 0) for z in range(1, far)]] + [[(0, n)] for n in swaps]:
        incoming = {}
        for step in stage:
            for offset, array in held.items():
                moved = send_by(array, uniform(*step, dims), dims)
                incoming[offset[0] + step[0], offset[1] | step[1]] = moved
        held.update(incoming)
    return held


def packed(lengths, prefill_of, decode_of, groups):
    bits = (groups - 1).bit_length()
    return (lengths << 2 * bits) | (prefill_of << bits) | decode_of


def unpacked(entry, groups):
    bits = (groups - 1).bit_length()
    mask = (1 << bits) - 1
    return entry >> 2 * bits, (entry >> bits) & mask, entry & mask


def prepare_kernel(dims, routes, own, table_hbm, pool, *rest):
    aliased = 0 if own else 1
    received, *sends = rest[aliased : aliased + 1 + len(routes)]
    table, held, zero_page, start_of, count_of, table_sem, in_sems, out_sem = rest[aliased + 1 + len(routes) :]
    me = lax.axis_index("group")
    groups = lax.axis_size("group")
    page_size = pool.shape[1]
    copy = pltpu.make_async_copy(table_hbm, table, table_sem)
    copy.start()
    for d in range(groups + 1):
        start_of[d] = 0
        count_of[d] = 0
    zero_page[...] = jnp.zeros_like(zero_page)
    copy.wait()

    def visit(r, running):
        length, home, destination = unpacked(table[r], groups)
        mine = home == me
        count = (length + page_size - 1) // page_size
        to = jnp.where(mine, destination, groups)
        start_of[to] = running
        count_of[to] = count
        return running + jnp.where(mine, count, 0)

    lax.fori_loop(0, table.shape[0], visit, jnp.int32(0), unroll=8)
    targets = [(routed(me, route, dims), send, 0) for route, send in zip(routes, sends)]
    if own:
        targets.append((me, received, me * MAX_PAGES))

    def each(do):
        for i, (to, target, base) in enumerate(targets):
            for page in range(MAX_PAGES):
                there = page < count_of[to]
                source = pool.at[jnp.where(there, start_of[to] + page, 0)]
                buffer, place = held.at[i, page], target.at[base + page]
                do(there, (source, buffer, in_sems.at[i, page]), (buffer, place, out_sem), (zero_page, place, out_sem))

    def fetch(there, load, store, blank):
        @pl.when(there)
        def _():
            pltpu.make_async_copy(*load).start()

        @pl.when(jnp.logical_not(there))
        def _():
            pltpu.make_async_copy(*blank).start()

    def forward(there, load, store, blank):
        @pl.when(there)
        def _():
            pltpu.make_async_copy(*load).wait()
            pltpu.make_async_copy(*store).start()

    def finish(there, load, store, blank):
        pltpu.make_async_copy(*blank).wait()

    each(fetch)
    each(forward)
    each(finish)


def prepare(dims, routes, table, pool, received=None):
    own = received is None
    groups = lax.axis_size("group")
    page = pool.shape[1:]
    blocks = len(routes) + (1 if own else 0)
    hbm = pl.BlockSpec(memory_space=pl.ANY)
    block = jax.ShapeDtypeStruct((MAX_PAGES,) + page, pool.dtype)
    outs = [jax.ShapeDtypeStruct((groups * MAX_PAGES,) + page, pool.dtype)] + [block] * len(routes)
    operands = [table, pool] + ([] if own else [received])
    return pl.pallas_call(
        functools.partial(prepare_kernel, dims, routes, own),
        out_shape=outs,
        in_specs=[hbm] * len(operands),
        out_specs=[hbm] * len(outs),
        scratch_shapes=[
            pltpu.SMEM(table.shape, jnp.int32),
            pltpu.VMEM((blocks, MAX_PAGES) + page, pool.dtype),
            pltpu.VMEM(page, pool.dtype),
            pltpu.SMEM((groups + 1,), jnp.int32),
            pltpu.SMEM((groups + 1,), jnp.int32),
            pltpu.SemaphoreType.DMA,
            pltpu.SemaphoreType.DMA((blocks, MAX_PAGES)),
            pltpu.SemaphoreType.DMA,
        ],
        input_output_aliases={} if own else {2: 0},
        compiler_params=pltpu.CompilerParams(vmem_limit_bytes=VMEM_LIMIT),
        cost_estimate=pl.CostEstimate(
            flops=0, bytes_accessed=4 * blocks * MAX_PAGES * math.prod(page), transcendentals=0
        ),
        name="outgoing_pages",
    )(*operands)


def attend_row(query, pages, length):
    first, second = pages
    kv_heads = first.shape[1] // (2 * HD)
    share = query.shape[0] // kv_heads
    scores = []
    for h in range(kv_heads):
        columns = slice(2 * h * HD, (2 * h + 1) * HD)
        keys = jnp.concatenate([first[:, columns], second[:, columns]], axis=0)
        every = lax.dot_general(
            query, keys, (((1,), (1,)), ((), ())), preferred_element_type=jnp.float32
        )
        scores.append(every[h * share : (h + 1) * share])
    score = jnp.concatenate(scores, axis=0) * (1.0 / math.sqrt(HD))
    live = lax.broadcasted_iota(jnp.int32, score.shape, 1) < length
    masked = jnp.where(live, score, -1e30)
    highest = jnp.max(masked, axis=1, keepdims=True)
    weights = jnp.where(live, jnp.exp(masked - highest), 0.0)
    totals = jnp.sum(weights, axis=1, keepdims=True)
    rounded = weights.astype(jnp.bfloat16)
    mixtures = []
    for h in range(kv_heads):
        columns = slice((2 * h + 1) * HD, (2 * h + 2) * HD)
        values = jnp.concatenate([first[:, columns], second[:, columns]], axis=0)
        every = jnp.dot(rounded, values, preferred_element_type=jnp.float32)
        mixtures.append(every[h * share : (h + 1) * share])
    return jnp.concatenate(mixtures, axis=0) / totals


def settle_kernel(dims, routes, own, last, table, row_request, queries, rows_in, received_in, *rest):
    blocks = rest[: len(routes)]
    received, out, rows, held, list_row, list_block, list_length, in_sems, out_sems = rest[len(routes) :]
    me = lax.axis_index("group")
    row_local, query_heads, _ = queries.shape
    mine = pl.ds(me * MAX_PAGES, MAX_PAGES)
    origins = [routed(me, reverse(route), dims) for route in routes]
    places = [pl.ds(origin * MAX_PAGES, MAX_PAGES) for origin in origins]
    sources = list(blocks) + ([received_in.at[mine]] if own else [])
    origins += [me] if own else []
    loads = [pltpu.make_async_copy(s, held.at[i], in_sems.at[i]) for i, s in enumerate(sources)]
    stores = [
        pltpu.make_async_copy(held.at[i], received.at[place], out_sems.at[i]) for i, place in enumerate(places)
    ]
    for load in loads:
        load.start()

    found = jnp.int32(0)
    for b in range(row_local):
        length, home, _ = unpacked(table[row_request[me * row_local + b]], math.prod(dims))
        block, match = jnp.int32(0), jnp.int32(0)
        for i, origin in enumerate(origins):
            block = jnp.where(home == origin, i, block)
            match = jnp.where(home == origin, 1, match)
        list_row[found] = b
        list_block[found] = block
        list_length[found] = length
        found = found + match
    for i in range(ROW_UNROLL):
        list_row[found + i] = row_local
        list_block[found + i] = 0
        list_length[found + i] = 1
    rows[:row_local] = rows_in[...]
    for load in loads:
        load.wait()
    for store in stores:
        store.start()

    @pl.loop(0, (found + ROW_UNROLL - 1) // ROW_UNROLL)
    def _(step):
        results = []
        for i in range(ROW_UNROLL):
            at = step * ROW_UNROLL + i
            query = queries[jnp.minimum(list_row[at], row_local - 1)]
            pages = [held[list_block[at], page] for page in range(MAX_PAGES)]
            results.append(attend_row(query, pages, list_length[at]))
        for i, result in enumerate(results):
            rows[list_row[step * ROW_UNROLL + i]] = result

    if last:
        for h in range(query_heads):
            out[:, h * HD : (h + 1) * HD] = rows[:row_local, h, :].astype(out.dtype)
    else:
        out[...] = rows[:row_local]
    for store in stores:
        store.wait()


def settle(dims, routes, own, last, table, row_request, queries, rows, received, blocks):
    row_local, query_heads, _ = queries.shape
    smem = pl.BlockSpec(memory_space=pltpu.SMEM)
    vmem = pl.BlockSpec(memory_space=pltpu.VMEM)
    hbm = pl.BlockSpec(memory_space=pl.ANY)
    count = len(blocks) + (1 if own else 0)
    if last:
        out = jax.ShapeDtypeStruct((row_local, query_heads * HD), jnp.bfloat16)
    else:
        out = jax.ShapeDtypeStruct(rows.shape, rows.dtype)
    return pl.pallas_call(
        functools.partial(settle_kernel, dims, routes, own, last),
        out_shape=[jax.ShapeDtypeStruct(received.shape, received.dtype), out],
        in_specs=[smem, smem, vmem, vmem, hbm] + [hbm] * len(blocks),
        out_specs=[hbm, vmem],
        scratch_shapes=[
            pltpu.VMEM((row_local + 1, query_heads, HD), jnp.float32),
            pltpu.VMEM((count, MAX_PAGES) + received.shape[1:], received.dtype),
            pltpu.SMEM((row_local + ROW_UNROLL,), jnp.int32),
            pltpu.SMEM((row_local + ROW_UNROLL,), jnp.int32),
            pltpu.SMEM((row_local + ROW_UNROLL,), jnp.int32),
            pltpu.SemaphoreType.DMA((count,)),
            pltpu.SemaphoreType.DMA((count,)),
        ],
        input_output_aliases={4: 0},
        compiler_params=pltpu.CompilerParams(vmem_limit_bytes=VMEM_LIMIT),
        cost_estimate=pl.CostEstimate(
            flops=1 << 30, bytes_accessed=4 * sum(b.size for b in blocks), transcendentals=1 << 18
        ),
        name="settle_pages",
    )(table, row_request, queries, rows, received, *blocks)


def project_kernel(dims, offsets, out_weight, *rest):
    shards = rest[: len(offsets)]
    own, *theirs = rest[len(offsets) : -3]
    attended, product, sems = rest[-3:]
    me = lax.axis_index("group")
    heads = lax.axis_size("head")
    my_head = lax.axis_index("head")
    row_local = shards[0].shape[0]
    share = own.shape[0]
    copies = []
    for i, offset in enumerate(offsets):
        place = pl.ds(routed(me, reverse(uniform(*offset, dims)), dims) * row_local, row_local)
        copies.append(pltpu.make_async_copy(shards[i], attended.at[place], sems.at[i]))
        copies[-1].start()
    for copy in copies:
        copy.wait()
    product[...] = jnp.dot(attended[...], out_weight[...], preferred_element_type=jnp.float32)
    own[...] = product[pl.ds(pl.multiple_of(my_head * share, share), share)]
    for ahead_by, target in enumerate(theirs, 1):
        start = pl.multiple_of(lax.rem(my_head + ahead_by, heads) * share, share)
        target[...] = product[pl.ds(start, share)].astype(target.dtype)


def project(dims, gathered, out_weight, heads):
    offsets = list(gathered)
    shards = [gathered[offset] for offset in offsets]
    row_local, width = shards[0].shape
    row_total = row_local * len(shards)
    share, columns = row_total // heads, out_weight.shape[1]
    vmem = pl.BlockSpec(memory_space=pltpu.VMEM)
    hbm = pl.BlockSpec(memory_space=pl.ANY)
    theirs = jax.ShapeDtypeStruct((share, columns), jnp.bfloat16)
    return pl.pallas_call(
        functools.partial(project_kernel, dims, offsets),
        out_shape=[jax.ShapeDtypeStruct((share, columns), jnp.float32)] + [theirs] * (heads - 1),
        in_specs=[vmem] + [hbm] * len(shards),
        out_specs=[vmem] * heads,
        scratch_shapes=[
            pltpu.VMEM((row_total, width), jnp.bfloat16),
            pltpu.VMEM((row_total, columns), jnp.float32),
            pltpu.SemaphoreType.DMA((len(shards),)),
        ],
        compiler_params=pltpu.CompilerParams(vmem_limit_bytes=VMEM_LIMIT),
        cost_estimate=pl.CostEstimate(
            flops=2 * row_total * width * columns, bytes_accessed=2 * out_weight.size, transcendentals=0
        ),
        name="project_rows",
    )(pltpu.with_memory_space_constraint(out_weight, pltpu.VMEM), *shards)


def local(kv_pool, lengths, prefill_of, decode_of, row_request, queries, out_weight):
    row_local, query_width = queries.shape
    query_heads = queries.reshape(row_local, query_width // HD, HD)
    heads = lax.axis_size("head")

    dims = factors(lax.axis_size("group"))
    routes = page_rounds(dims)
    table = packed(lengths, prefill_of, decode_of, math.prod(dims))
    received, *early = prepare(dims, routes[:EARLY], table, kv_pool)
    received, *late = prepare(dims, routes[EARLY:], table, kv_pool, received)
    arrived = [send_by(block, route, dims) for block, route in zip(early + late, routes)]
    rows = jnp.zeros(query_heads.shape, jnp.float32)
    for first in range(0, len(routes), WAVE):
        wave = slice(first, first + WAVE)
        last = first + WAVE >= len(routes)
        received, rows = settle(
            dims, routes[wave], first == 0, last, table, row_request, query_heads, rows, received, arrived[wave]
        )

    own, *theirs = project(dims, gather_shards(rows, dims), out_weight, heads)
    for ahead_by, part in enumerate(theirs, 1):
        pairs = [(h, (h + ahead_by) % heads) for h in range(heads)]
        own = own + lax.ppermute(part, "head", pairs).astype(jnp.float32)
    return (received, own.astype(jnp.bfloat16))


def solution(mesh):
    in_specs = (
        P("group", None, "head"),
        P(),
        P(),
        P(),
        P(),
        P("group", "head"),
        P("head", "group"),
    )
    out_specs = (P("group", None, "head"), P("head", "group"))
    return jax.shard_map(local, mesh=mesh, in_specs=in_specs, out_specs=out_specs, check_vma=False)
```

```python
import functools
import math

import jax
import jax.numpy as jnp
from jax import lax
from jax.experimental import pallas as pl
from jax.experimental.pallas import tpu as pltpu
from jax.sharding import PartitionSpec as P

HD = 128
MAX_PAGES = 2
WAVE = 3
ROW_UNROLL = 4
EARLY = 4
VMEM_LIMIT = 20 * 1024 * 1024


def factors(groups):
    near = math.gcd(groups, 4)
    return groups // near, near


def uniform(step, swap, dims):
    return tuple(((z + step) % dims[0], swap) for z in range(dims[0]))


def page_rounds(dims):
    far, near = dims
    steps = sorted(range(1, far), key=lambda z: (min(z, far - z), z))
    order = [(z, n) for z in steps for n in range(near)]
    for n in range(1, near):
        order.insert(min(2 * n, len(order)), (0, n))
    return [uniform(z, n, dims) for z, n in order]


def reverse(route):
    sources = {to: (z, swap) for z, (to, swap) in enumerate(route)}
    return tuple(sources[z] for z in range(len(route)))


def routed(me, route, dims):
    near = dims[1]
    z = me // near
    to, swap = jnp.int32(route[0][0]), jnp.int32(route[0][1])
    for place in range(1, dims[0]):
        to = jnp.where(z == place, route[place][0], to)
        swap = jnp.where(z == place, route[place][1], swap)
    return to * near + (me % near ^ swap)


def send_by(array, route, dims):
    far, near = dims
    pairs = [
        (z * near + n, route[z][0] * near + (n ^ route[z][1])) for z in range(far) for n in range(near)
    ]
    return lax.ppermute(array, "group", pairs)


def gather_shards(shard, dims):
    far, near = dims
    held = {(0, 0): shard}
    swaps = [1 << i for i in reversed(range(near.bit_length() - 1))]
    for stage in [[(z, 0) for z in range(1, far)]] + [[(0, n)] for n in swaps]:
        incoming = {}
        for step in stage:
            for offset, array in held.items():
                moved = send_by(array, uniform(*step, dims), dims)
                incoming[offset[0] + step[0], offset[1] | step[1]] = moved
        held.update(incoming)
    return held


def packed(lengths, prefill_of, decode_of, groups):
    bits = (groups - 1).bit_length()
    return (lengths << 2 * bits) | (prefill_of << bits) | decode_of


def unpacked(entry, groups):
    bits = (groups - 1).bit_length()
    mask = (1 << bits) - 1
    return entry >> 2 * bits, (entry >> bits) & mask, entry & mask


def prepare_kernel(dims, routes, own, table_hbm, pool, *rest):
    aliased = 0 if own else 1
    received, *sends = rest[aliased : aliased + 1 + len(routes)]
    table, held, zero_page, start_of, count_of, table_sem, in_sems, out_sem = rest[aliased + 1 + len(routes) :]
    me = lax.axis_index("group")
    groups = lax.axis_size("group")
    page_size = pool.shape[1]
    copy = pltpu.make_async_copy(table_hbm, table, table_sem)
    copy.start()
    for d in range(groups + 1):
        start_of[d] = 0
        count_of[d] = 0
    zero_page[...] = jnp.zeros_like(zero_page)
    copy.wait()

    def visit(r, running):
        length, home, destination = unpacked(table[r], groups)
        mine = home == me
        count = (length + page_size - 1) // page_size
        to = jnp.where(mine, destination, groups)
        start_of[to] = running
        count_of[to] = count
        return running + jnp.where(mine, count, 0)

    lax.fori_loop(0, table.shape[0], visit, jnp.int32(0), unroll=8)
    targets = [(routed(me, route, dims), send, 0) for route, send in zip(routes, sends)]
    if own:
        targets.append((me, received, me * MAX_PAGES))

    def each(do):
        for i, (to, target, base) in enumerate(targets):
            for page in range(MAX_PAGES):
                there = page < count_of[to]
                source = pool.at[jnp.where(there, start_of[to] + page, 0)]
                buffer, place = held.at[i, page], target.at[base + page]
                do(there, (source, buffer, in_sems.at[i, page]), (buffer, place, out_sem), (zero_page, place, out_sem))

    def fetch(there, load, store, blank):
        @pl.when(there)
        def _():
            pltpu.make_async_copy(*load).start()

        @pl.when(jnp.logical_not(there))
        def _():
            pltpu.make_async_copy(*blank).start()

    def forward(there, load, store, blank):
        @pl.when(there)
        def _():
            pltpu.make_async_copy(*load).wait()
            pltpu.make_async_copy(*store).start()

    def finish(there, load, store, blank):
        pltpu.make_async_copy(*blank).wait()

    each(fetch)
    each(forward)
    each(finish)


def prepare(dims, routes, table, pool, received=None):
    own = received is None
    groups = lax.axis_size("group")
    page = pool.shape[1:]
    blocks = len(routes) + (1 if own else 0)
    hbm = pl.BlockSpec(memory_space=pl.ANY)
    block = jax.ShapeDtypeStruct((MAX_PAGES,) + page, pool.dtype)
    outs = [jax.ShapeDtypeStruct((groups * MAX_PAGES,) + page, pool.dtype)] + [block] * len(routes)
    operands = [table, pool] + ([] if own else [received])
    return pl.pallas_call(
        functools.partial(prepare_kernel, dims, routes, own),
        out_shape=outs,
        in_specs=[hbm] * len(operands),
        out_specs=[hbm] * len(outs),
        scratch_shapes=[
            pltpu.SMEM(table.shape, jnp.int32),
            pltpu.VMEM((blocks, MAX_PAGES) + page, pool.dtype),
            pltpu.VMEM(page, pool.dtype),
            pltpu.SMEM((groups + 1,), jnp.int32),
            pltpu.SMEM((groups + 1,), jnp.int32),
            pltpu.SemaphoreType.DMA,
            pltpu.SemaphoreType.DMA((blocks, MAX_PAGES)),
            pltpu.SemaphoreType.DMA,
        ],
        input_output_aliases={} if own else {2: 0},
        compiler_params=pltpu.CompilerParams(vmem_limit_bytes=VMEM_LIMIT),
        cost_estimate=pl.CostEstimate(
            flops=0, bytes_accessed=4 * blocks * MAX_PAGES * math.prod(page), transcendentals=0
        ),
        name="outgoing_pages",
    )(*operands)


def attend_row(query, pages, length):
    first, second = pages
    kv_heads = first.shape[1] // (2 * HD)
    share = query.shape[0] // kv_heads
    scores = []
    for h in range(kv_heads):
        columns = slice(2 * h * HD, (2 * h + 1) * HD)
        keys = jnp.concatenate([first[:, columns], second[:, columns]], axis=0)
        every = lax.dot_general(
            query, keys, (((1,), (1,)), ((), ())), preferred_element_type=jnp.float32
        )
        scores.append(every[h * share : (h + 1) * share])
    score = jnp.concatenate(scores, axis=0) * (1.0 / math.sqrt(HD))
    live = lax.broadcasted_iota(jnp.int32, score.shape, 1) < length
    masked = jnp.where(live, score, -1e30)
    highest = jnp.max(masked, axis=1, keepdims=True)
    weights = jnp.where(live, jnp.exp(masked - highest), 0.0)
    totals = jnp.sum(weights, axis=1, keepdims=True)
    rounded = weights.astype(jnp.bfloat16)
    mixtures = []
    for h in range(kv_heads):
        columns = slice((2 * h + 1) * HD, (2 * h + 2) * HD)
        values = jnp.concatenate([first[:, columns], second[:, columns]], axis=0)
        every = jnp.dot(rounded, values, preferred_element_type=jnp.float32)
        mixtures.append(every[h * share : (h + 1) * share])
    return jnp.concatenate(mixtures, axis=0) / totals


def settle_kernel(dims, routes, own, last, table, row_request, queries, rows_in, received_in, *rest):
    blocks = rest[: len(routes)]
    received, out, rows, held, list_row, list_block, list_length, in_sems, out_sems = rest[len(routes) :]
    me = lax.axis_index("group")
    row_local, query_heads, _ = queries.shape
    mine = pl.ds(me * MAX_PAGES, MAX_PAGES)
    origins = [routed(me, reverse(route), dims) for route in routes]
    places = [pl.ds(origin * MAX_PAGES, MAX_PAGES) for origin in origins]
    sources = list(blocks) + ([received_in.at[mine]] if own else [])
    origins += [me] if own else []
    loads = [pltpu.make_async_copy(s, held.at[i], in_sems.at[i]) for i, s in enumerate(sources)]
    stores = [
        pltpu.make_async_copy(held.at[i], received.at[place], out_sems.at[i]) for i, place in enumerate(places)
    ]
    for load in loads:
        load.start()

    found = jnp.int32(0)
    for b in range(row_local):
        length, home, _ = unpacked(table[row_request[me * row_local + b]], math.prod(dims))
        block, match = jnp.int32(0), jnp.int32(0)
        for i, origin in enumerate(origins):
            block = jnp.where(home == origin, i, block)
            match = jnp.where(home == origin, 1, match)
        list_row[found] = b
        list_block[found] = block
        list_length[found] = length
        found = found + match
    for i in range(ROW_UNROLL):
        list_row[found + i] = row_local
        list_block[found + i] = 0
        list_length[found + i] = 1
    rows[:row_local] = rows_in[...]
    for load in loads:
        load.wait()
    for store in stores:
        store.start()

    @pl.loop(0, (found + ROW_UNROLL - 1) // ROW_UNROLL)
    def _(step):
        results = []
        for i in range(ROW_UNROLL):
            at = step * ROW_UNROLL + i
            query = queries[jnp.minimum(list_row[at], row_local - 1)]
            pages = [held[list_block[at], page] for page in range(MAX_PAGES)]
            results.append(attend_row(query, pages, list_length[at]))
        for i, result in enumerate(results):
            rows[list_row[step * ROW_UNROLL + i]] = result

    if last:
        for h in range(query_heads):
            out[:, h * HD : (h + 1) * HD] = rows[:row_local, h, :].astype(out.dtype)
    else:
        out[...] = rows[:row_local]
    for store in stores:
        store.wait()


def settle(dims, routes, own, last, table, row_request, queries, rows, received, blocks):
    row_local, query_heads, _ = queries.shape
    smem = pl.BlockSpec(memory_space=pltpu.SMEM)
    vmem = pl.BlockSpec(memory_space=pltpu.VMEM)
    hbm = pl.BlockSpec(memory_space=pl.ANY)
    count = len(blocks) + (1 if own else 0)
    if last:
        out = jax.ShapeDtypeStruct((row_local, query_heads * HD), jnp.bfloat16)
    else:
        out = jax.ShapeDtypeStruct(rows.shape, rows.dtype)
    return pl.pallas_call(
        functools.partial(settle_kernel, dims, routes, own, last),
        out_shape=[jax.ShapeDtypeStruct(received.shape, received.dtype), out],
        in_specs=[smem, smem, vmem, vmem, hbm] + [hbm] * len(blocks),
        out_specs=[hbm, vmem],
        scratch_shapes=[
            pltpu.VMEM((row_local + 1, query_heads, HD), jnp.float32),
            pltpu.VMEM((count, MAX_PAGES) + received.shape[1:], received.dtype),
            pltpu.SMEM((row_local + ROW_UNROLL,), jnp.int32),
            pltpu.SMEM((row_local + ROW_UNROLL,), jnp.int32),
            pltpu.SMEM((row_local + ROW_UNROLL,), jnp.int32),
            pltpu.SemaphoreType.DMA((count,)),
            pltpu.SemaphoreType.DMA((count,)),
        ],
        input_output_aliases={4: 0},
        compiler_params=pltpu.CompilerParams(vmem_limit_bytes=VMEM_LIMIT),
        cost_estimate=pl.CostEstimate(
            flops=1 << 30, bytes_accessed=4 * sum(b.size for b in blocks), transcendentals=1 << 18
        ),
        name="settle_pages",
    )(table, row_request, queries, rows, received, *blocks)


def project_kernel(dims, offsets, out_weight, *rest):
    shards = rest[: len(offsets)]
    own, *theirs = rest[len(offsets) : -3]
    attended, product, sems = rest[-3:]
    me = lax.axis_index("group")
    heads = lax.axis_size("head")
    my_head = lax.axis_index("head")
    row_local = shards[0].shape[0]
    share = own.shape[0]
    copies = []
    for i, offset in enumerate(offsets):
        place = pl.ds(routed(me, reverse(uniform(*offset, dims)), dims) * row_local, row_local)
        copies.append(pltpu.make_async_copy(shards[i], attended.at[place], sems.at[i]))
        copies[-1].start()
    for copy in copies:
        copy.wait()
    product[...] = jnp.dot(attended[...], out_weight[...], preferred_element_type=jnp.float32)
    own[...] = product[pl.ds(pl.multiple_of(my_head * share, share), share)]
    for ahead_by, target in enumerate(theirs, 1):
        start = pl.multiple_of(lax.rem(my_head + ahead_by, heads) * share, share)
        target[...] = product[pl.ds(start, share)].astype(target.dtype)


def project(dims, gathered, out_weight, heads):
    offsets = list(gathered)
    shards = [gathered[offset] for offset in offsets]
    row_local, width = shards[0].shape
    row_total = row_local * len(shards)
    share, columns = row_total // heads, out_weight.shape[1]
    vmem = pl.BlockSpec(memory_space=pltpu.VMEM)
    hbm = pl.BlockSpec(memory_space=pl.ANY)
    theirs = jax.ShapeDtypeStruct((share, columns), jnp.bfloat16)
    return pl.pallas_call(
        functools.partial(project_kernel, dims, offsets),
        out_shape=[jax.ShapeDtypeStruct((share, columns), jnp.float32)] + [theirs] * (heads - 1),
        in_specs=[vmem] + [hbm] * len(shards),
        out_specs=[vmem] * heads,
        scratch_shapes=[
            pltpu.VMEM((row_total, width), jnp.bfloat16),
            pltpu.VMEM((row_total, columns), jnp.float32),
            pltpu.SemaphoreType.DMA((len(shards),)),
        ],
        compiler_params=pltpu.CompilerParams(vmem_limit_bytes=VMEM_LIMIT),
        cost_estimate=pl.CostEstimate(
            flops=2 * row_total * width * columns, bytes_accessed=2 * out_weight.size, transcendentals=0
        ),
        name="project_rows",
    )(pltpu.with_memory_space_constraint(out_weight, pltpu.VMEM), *shards)


def local(kv_pool, lengths, prefill_of, decode_of, row_request, queries, out_weight):
    row_local, query_width = queries.shape
    query_heads = queries.reshape(row_local, query_width // HD, HD)
    heads = lax.axis_size("head")

    dims = factors(lax.axis_size("group"))
    routes = page_rounds(dims)
    table = packed(lengths, prefill_of, decode_of, math.prod(dims))
    kv_pool = pltpu.with_memory_space_constraint(kv_pool, pltpu.HBM)
    received, *early = prepare(dims, routes[:EARLY], table, kv_pool)
    received, *late = prepare(dims, routes[EARLY:], table, kv_pool, received)
    arrived = [send_by(block, route, dims) for block, route in zip(early + late, routes)]
    rows = jnp.zeros(query_heads.shape, jnp.float32)
    for first in range(0, len(routes), WAVE):
        wave = slice(first, first + WAVE)
        last = first + WAVE >= len(routes)
        received, rows = settle(
            dims, routes[wave], first == 0, last, table, row_request, query_heads, rows, received, arrived[wave]
        )

    own, *theirs = project(dims, gather_shards(rows, dims), out_weight, heads)
    for ahead_by, part in enumerate(theirs, 1):
        pairs = [(h, (h + ahead_by) % heads) for h in range(heads)]
        own = own + lax.ppermute(part, "head", pairs).astype(jnp.float32)
    return (received, own.astype(jnp.bfloat16))


def solution(mesh):
    in_specs = (
        P("group", None, "head"),
        P(),
        P(),
        P(),
        P(),
        P("group", "head"),
        P("head", "group"),
    )
    out_specs = (P("group", None, "head"), P("head", "group"))
    return jax.shard_map(local, mesh=mesh, in_specs=in_specs, out_specs=out_specs, check_vma=False)
```

```python
import functools
import math

import jax
import jax.numpy as jnp
from jax import lax
from jax.experimental import pallas as pl
from jax.experimental.pallas import tpu as pltpu
from jax.sharding import PartitionSpec as P

HD = 128
MAX_PAGES = 2
WAVE = 3
ROW_UNROLL = 4
EARLY = 4
VMEM_LIMIT = 20 * 1024 * 1024


def factors(groups):
    near = math.gcd(groups, 4)
    return groups // near, near


def uniform(step, swap, dims):
    return tuple(((z + step) % dims[0], swap) for z in range(dims[0]))


def page_rounds(dims):
    far, near = dims
    single, longer = [(1, n) for n in range(near)], [(z, n) for n in range(near) for z in range(2, far)]
    order, near_left = single[:2], [(0, n) for n in range(1, near)]
    single = single[2:]
    while longer or single or near_left:
        order += near_left[:1] + longer[: max(far - 2, 1)] + single[:1]
        near_left, longer, single = near_left[1:], longer[max(far - 2, 1) :], single[1:]
    return [uniform(z, n, dims) for z, n in order]


def reverse(route):
    sources = {to: (z, swap) for z, (to, swap) in enumerate(route)}
    return tuple(sources[z] for z in range(len(route)))


def routed(me, route, dims):
    near = dims[1]
    z = me // near
    to, swap = jnp.int32(route[0][0]), jnp.int32(route[0][1])
    for place in range(1, dims[0]):
        to = jnp.where(z == place, route[place][0], to)
        swap = jnp.where(z == place, route[place][1], swap)
    return to * near + (me % near ^ swap)


def send_by(array, route, dims):
    far, near = dims
    pairs = [
        (z * near + n, route[z][0] * near + (n ^ route[z][1])) for z in range(far) for n in range(near)
    ]
    return lax.ppermute(array, "group", pairs)


def gather_shards(shard, dims):
    far, near = dims
    held = {(0, 0): shard}
    swaps = [1 << i for i in reversed(range(near.bit_length() - 1))]
    for stage in [[(z, 0) for z in range(1, far)]] + [[(0, n)] for n in swaps]:
        incoming = {}
        for step in stage:
            for offset, array in held.items():
                moved = send_by(array, uniform(*step, dims), dims)
                incoming[offset[0] + step[0], offset[1] | step[1]] = moved
        held.update(incoming)
    return held


def packed(lengths, prefill_of, decode_of, groups):
    bits = (groups - 1).bit_length()
    return (lengths << 2 * bits) | (prefill_of << bits) | decode_of


def unpacked(entry, groups):
    bits = (groups - 1).bit_length()
    mask = (1 << bits) - 1
    return entry >> 2 * bits, (entry >> bits) & mask, entry & mask


def prepare_kernel(dims, routes, own, table_hbm, pool, *rest):
    aliased = 0 if own else 1
    received, *sends = rest[aliased : aliased + 1 + len(routes)]
    table, held, zero_page, start_of, count_of, table_sem, in_sems, out_sem = rest[aliased + 1 + len(routes) :]
    me = lax.axis_index("group")
    groups = lax.axis_size("group")
    page_size = pool.shape[1]
    copy = pltpu.make_async_copy(table_hbm, table, table_sem)
    copy.start()
    for d in range(groups + 1):
        start_of[d] = 0
        count_of[d] = 0
    zero_page[...] = jnp.zeros_like(zero_page)
    copy.wait()

    def visit(r, running):
        length, home, destination = unpacked(table[r], groups)
        mine = home == me
        count = (length + page_size - 1) // page_size
        to = jnp.where(mine, destination, groups)
        start_of[to] = running
        count_of[to] = count
        return running + jnp.where(mine, count, 0)

    lax.fori_loop(0, table.shape[0], visit, jnp.int32(0), unroll=8)
    targets = [(routed(me, route, dims), send, 0) for route, send in zip(routes, sends)]
    if own:
        targets.append((me, received, me * MAX_PAGES))

    def each(do):
        for i, (to, target, base) in enumerate(targets):
            for page in range(MAX_PAGES):
                there = page < count_of[to]
                source = pool.at[jnp.where(there, start_of[to] + page, 0)]
                buffer, place = held.at[i, page], target.at[base + page]
                do(there, (source, buffer, in_sems.at[i, page]), (buffer, place, out_sem), (zero_page, place, out_sem))

    def fetch(there, load, store, blank):
        @pl.when(there)
        def _():
            pltpu.make_async_copy(*load).start()

        @pl.when(jnp.logical_not(there))
        def _():
            pltpu.make_async_copy(*blank).start()

    def forward(there, load, store, blank):
        @pl.when(there)
        def _():
            pltpu.make_async_copy(*load).wait()
            pltpu.make_async_copy(*store).start()

    def finish(there, load, store, blank):
        pltpu.make_async_copy(*blank).wait()

    each(fetch)
    each(forward)
    each(finish)


def prepare(dims, routes, table, pool, received=None):
    own = received is None
    groups = lax.axis_size("group")
    page = pool.shape[1:]
    blocks = len(routes) + (1 if own else 0)
    hbm = pl.BlockSpec(memory_space=pl.ANY)
    block = jax.ShapeDtypeStruct((MAX_PAGES,) + page, pool.dtype)
    outs = [jax.ShapeDtypeStruct((groups * MAX_PAGES,) + page, pool.dtype)] + [block] * len(routes)
    operands = [table, pool] + ([] if own else [received])
    return pl.pallas_call(
        functools.partial(prepare_kernel, dims, routes, own),
        out_shape=outs,
        in_specs=[hbm] * len(operands),
        out_specs=[hbm] * len(outs),
        scratch_shapes=[
            pltpu.SMEM(table.shape, jnp.int32),
            pltpu.VMEM((blocks, MAX_PAGES) + page, pool.dtype),
            pltpu.VMEM(page, pool.dtype),
            pltpu.SMEM((groups + 1,), jnp.int32),
            pltpu.SMEM((groups + 1,), jnp.int32),
            pltpu.SemaphoreType.DMA,
            pltpu.SemaphoreType.DMA((blocks, MAX_PAGES)),
            pltpu.SemaphoreType.DMA,
        ],
        input_output_aliases={} if own else {2: 0},
        compiler_params=pltpu.CompilerParams(vmem_limit_bytes=VMEM_LIMIT),
        cost_estimate=pl.CostEstimate(
            flops=0, bytes_accessed=4 * blocks * MAX_PAGES * math.prod(page), transcendentals=0
        ),
        name="outgoing_pages",
    )(*operands)


def attend_row(query, pages, length):
    first, second = pages
    kv_heads = first.shape[1] // (2 * HD)
    share = query.shape[0] // kv_heads
    scores = []
    for h in range(kv_heads):
        columns = slice(2 * h * HD, (2 * h + 1) * HD)
        keys = jnp.concatenate([first[:, columns], second[:, columns]], axis=0)
        every = lax.dot_general(
            query, keys, (((1,), (1,)), ((), ())), preferred_element_type=jnp.float32
        )
        scores.append(every[h * share : (h + 1) * share])
    score = jnp.concatenate(scores, axis=0) * (1.0 / math.sqrt(HD))
    live = lax.broadcasted_iota(jnp.int32, score.shape, 1) < length
    masked = jnp.where(live, score, -1e30)
    highest = jnp.max(masked, axis=1, keepdims=True)
    weights = jnp.where(live, jnp.exp(masked - highest), 0.0)
    totals = jnp.sum(weights, axis=1, keepdims=True)
    rounded = weights.astype(jnp.bfloat16)
    mixtures = []
    for h in range(kv_heads):
        columns = slice((2 * h + 1) * HD, (2 * h + 2) * HD)
        values = jnp.concatenate([first[:, columns], second[:, columns]], axis=0)
        every = jnp.dot(rounded, values, preferred_element_type=jnp.float32)
        mixtures.append(every[h * share : (h + 1) * share])
    return jnp.concatenate(mixtures, axis=0) / totals


def settle_kernel(dims, routes, own, last, table, row_request, queries, rows_in, received_in, *rest):
    blocks = rest[: len(routes)]
    received, out, rows, held, list_row, list_block, list_length, in_sems, out_sems = rest[len(routes) :]
    me = lax.axis_index("group")
    row_local, query_heads, _ = queries.shape
    mine = pl.ds(me * MAX_PAGES, MAX_PAGES)
    origins = [routed(me, reverse(route), dims) for route in routes]
    places = [pl.ds(origin * MAX_PAGES, MAX_PAGES) for origin in origins]
    sources = list(blocks) + ([received_in.at[mine]] if own else [])
    origins += [me] if own else []
    loads = [pltpu.make_async_copy(s, held.at[i], in_sems.at[i]) for i, s in enumerate(sources)]
    stores = [
        pltpu.make_async_copy(held.at[i], received.at[place], out_sems.at[i]) for i, place in enumerate(places)
    ]
    for load in loads:
        load.start()

    found = jnp.int32(0)
    for b in range(row_local):
        length, home, _ = unpacked(table[row_request[me * row_local + b]], math.prod(dims))
        block, match = jnp.int32(0), jnp.int32(0)
        for i, origin in enumerate(origins):
            block = jnp.where(home == origin, i, block)
            match = jnp.where(home == origin, 1, match)
        list_row[found] = b
        list_block[found] = block
        list_length[found] = length
        found = found + match
    for i in range(ROW_UNROLL):
        list_row[found + i] = row_local
        list_block[found + i] = 0
        list_length[found + i] = 1
    rows[:row_local] = rows_in[...]
    for load in loads:
        load.wait()
    for store in stores:
        store.start()

    @pl.loop(0, (found + ROW_UNROLL - 1) // ROW_UNROLL)
    def _(step):
        results = []
        for i in range(ROW_UNROLL):
            at = step * ROW_UNROLL + i
            query = queries[jnp.minimum(list_row[at], row_local - 1)]
            pages = [held[list_block[at], page] for page in range(MAX_PAGES)]
            results.append(attend_row(query, pages, list_length[at]))
        for i, result in enumerate(results):
            rows[list_row[step * ROW_UNROLL + i]] = result

    if last:
        for h in range(query_heads):
            out[:, h * HD : (h + 1) * HD] = rows[:row_local, h, :].astype(out.dtype)
    else:
        out[...] = rows[:row_local]
    for store in stores:
        store.wait()


def settle(dims, routes, own, last, table, row_request, queries, rows, received, blocks):
    row_local, query_heads, _ = queries.shape
    smem = pl.BlockSpec(memory_space=pltpu.SMEM)
    vmem = pl.BlockSpec(memory_space=pltpu.VMEM)
    hbm = pl.BlockSpec(memory_space=pl.ANY)
    count = len(blocks) + (1 if own else 0)
    if last:
        out = jax.ShapeDtypeStruct((row_local, query_heads * HD), jnp.bfloat16)
    else:
        out = jax.ShapeDtypeStruct(rows.shape, rows.dtype)
    return pl.pallas_call(
        functools.partial(settle_kernel, dims, routes, own, last),
        out_shape=[jax.ShapeDtypeStruct(received.shape, received.dtype), out],
        in_specs=[smem, smem, vmem, vmem, hbm] + [hbm] * len(blocks),
        out_specs=[hbm, vmem],
        scratch_shapes=[
            pltpu.VMEM((row_local + 1, query_heads, HD), jnp.float32),
            pltpu.VMEM((count, MAX_PAGES) + received.shape[1:], received.dtype),
            pltpu.SMEM((row_local + ROW_UNROLL,), jnp.int32),
            pltpu.SMEM((row_local + ROW_UNROLL,), jnp.int32),
            pltpu.SMEM((row_local + ROW_UNROLL,), jnp.int32),
            pltpu.SemaphoreType.DMA((count,)),
            pltpu.SemaphoreType.DMA((count,)),
        ],
        input_output_aliases={4: 0},
        compiler_params=pltpu.CompilerParams(vmem_limit_bytes=VMEM_LIMIT),
        cost_estimate=pl.CostEstimate(
            flops=1 << 30, bytes_accessed=4 * sum(b.size for b in blocks), transcendentals=1 << 18
        ),
        name="settle_pages",
    )(table, row_request, queries, rows, received, *blocks)


def project_kernel(dims, offsets, out_weight, *rest):
    shards = rest[: len(offsets)]
    own, *theirs = rest[len(offsets) : -3]
    attended, product, sems = rest[-3:]
    me = lax.axis_index("group")
    heads = lax.axis_size("head")
    my_head = lax.axis_index("head")
    row_local = shards[0].shape[0]
    share = own.shape[0]
    copies = []
    for i, offset in enumerate(offsets):
        place = pl.ds(routed(me, reverse(uniform(*offset, dims)), dims) * row_local, row_local)
        copies.append(pltpu.make_async_copy(shards[i], attended.at[place], sems.at[i]))
        copies[-1].start()
    for copy in copies:
        copy.wait()
    product[...] = jnp.dot(attended[...], out_weight[...], preferred_element_type=jnp.float32)
    own[...] = product[pl.ds(pl.multiple_of(my_head * share, share), share)]
    for ahead_by, target in enumerate(theirs, 1):
        start = pl.multiple_of(lax.rem(my_head + ahead_by, heads) * share, share)
        target[...] = product[pl.ds(start, share)].astype(target.dtype)


def project(dims, gathered, out_weight, heads):
    offsets = list(gathered)
    shards = [gathered[offset] for offset in offsets]
    row_local, width = shards[0].shape
    row_total = row_local * len(shards)
    share, columns = row_total // heads, out_weight.shape[1]
    vmem = pl.BlockSpec(memory_space=pltpu.VMEM)
    hbm = pl.BlockSpec(memory_space=pl.ANY)
    theirs = jax.ShapeDtypeStruct((share, columns), jnp.bfloat16)
    return pl.pallas_call(
        functools.partial(project_kernel, dims, offsets),
        out_shape=[jax.ShapeDtypeStruct((share, columns), jnp.float32)] + [theirs] * (heads - 1),
        in_specs=[vmem] + [hbm] * len(shards),
        out_specs=[vmem] * heads,
        scratch_shapes=[
            pltpu.VMEM((row_total, width), jnp.bfloat16),
            pltpu.VMEM((row_total, columns), jnp.float32),
            pltpu.SemaphoreType.DMA((len(shards),)),
        ],
        compiler_params=pltpu.CompilerParams(vmem_limit_bytes=VMEM_LIMIT),
        cost_estimate=pl.CostEstimate(
            flops=2 * row_total * width * columns, bytes_accessed=2 * out_weight.size, transcendentals=0
        ),
        name="project_rows",
    )(pltpu.with_memory_space_constraint(out_weight, pltpu.VMEM), *shards)


def local(kv_pool, lengths, prefill_of, decode_of, row_request, queries, out_weight):
    row_local, query_width = queries.shape
    query_heads = queries.reshape(row_local, query_width // HD, HD)
    heads = lax.axis_size("head")

    dims = factors(lax.axis_size("group"))
    routes = page_rounds(dims)
    table = packed(lengths, prefill_of, decode_of, math.prod(dims))
    kv_pool = pltpu.with_memory_space_constraint(kv_pool, pltpu.HBM)
    received, *early = prepare(dims, routes[:EARLY], table, kv_pool)
    received, *late = prepare(dims, routes[EARLY:], table, kv_pool, received)
    arrived = [send_by(block, route, dims) for block, route in zip(early + late, routes)]
    rows = jnp.zeros(query_heads.shape, jnp.float32)
    for first in range(0, len(routes), WAVE):
        wave = slice(first, first + WAVE)
        last = first + WAVE >= len(routes)
        received, rows = settle(
            dims, routes[wave], first == 0, last, table, row_request, query_heads, rows, received, arrived[wave]
        )

    own, *theirs = project(dims, gather_shards(rows, dims), out_weight, heads)
    for ahead_by, part in enumerate(theirs, 1):
        pairs = [(h, (h + ahead_by) % heads) for h in range(heads)]
        own = own + lax.ppermute(part, "head", pairs).astype(jnp.float32)
    return (received, own.astype(jnp.bfloat16))


def solution(mesh):
    in_specs = (
        P("group", None, "head"),
        P(),
        P(),
        P(),
        P(),
        P("group", "head"),
        P("head", "group"),
    )
    out_specs = (P("group", None, "head"), P("head", "group"))
    return jax.shard_map(local, mesh=mesh, in_specs=in_specs, out_specs=out_specs, check_vma=False)
```

```python
import functools
import math

import jax
import jax.numpy as jnp
from jax import lax
from jax.experimental import pallas as pl
from jax.experimental.pallas import tpu as pltpu
from jax.sharding import PartitionSpec as P

HD = 128
MAX_PAGES = 2
WAVE = 3
ROW_UNROLL = 4
EARLY = 2
VMEM_LIMIT = 20 * 1024 * 1024


def factors(groups):
    near = math.gcd(groups, 4)
    return groups // near, near


def uniform(step, swap, dims):
    return tuple(((z + step) % dims[0], swap) for z in range(dims[0]))


def page_rounds(dims):
    far, near = dims
    single, longer = [(1, n) for n in range(near)], [(z, n) for n in range(near) for z in range(2, far)]
    order, near_left = single[:2], [(0, n) for n in range(1, near)]
    single = single[2:]
    while longer or single or near_left:
        order += near_left[:1] + longer[: max(far - 2, 1)] + single[:1]
        near_left, longer, single = near_left[1:], longer[max(far - 2, 1) :], single[1:]
    return [uniform(z, n, dims) for z, n in order]


def reverse(route):
    sources = {to: (z, swap) for z, (to, swap) in enumerate(route)}
    return tuple(sources[z] for z in range(len(route)))


def routed(me, route, dims):
    near = dims[1]
    z = me // near
    to, swap = jnp.int32(route[0][0]), jnp.int32(route[0][1])
    for place in range(1, dims[0]):
        to = jnp.where(z == place, route[place][0], to)
        swap = jnp.where(z == place, route[place][1], swap)
    return to * near + (me % near ^ swap)


def send_by(array, route, dims):
    far, near = dims
    pairs = [
        (z * near + n, route[z][0] * near + (n ^ route[z][1])) for z in range(far) for n in range(near)
    ]
    return lax.ppermute(array, "group", pairs)


def swap(array, mask):
    groups = lax.axis_size("group")
    return lax.ppermute(array, "group", [(s, s ^ mask) for s in range(groups)])


def gather_shards(shard):
    held = {0: shard}
    mask = lax.axis_size("group") // 2
    while mask:
        held.update({done | mask: swap(array, mask) for done, array in held.items()})
        mask //= 2
    return held


def packed(lengths, prefill_of, decode_of, groups):
    bits = (groups - 1).bit_length()
    return (lengths << 2 * bits) | (prefill_of << bits) | decode_of


def unpacked(entry, groups):
    bits = (groups - 1).bit_length()
    mask = (1 << bits) - 1
    return entry >> 2 * bits, (entry >> bits) & mask, entry & mask


def prepare_kernel(dims, routes, own, table_hbm, pool, *rest):
    table, held, zero_page, start_of, count_of, table_sem, in_sems, out_sem = rest[-8:]
    received = rest[-8 - len(routes) - own : -8 - len(routes)]
    sends = rest[-8 - len(routes) : -8]
    me = lax.axis_index("group")
    groups = lax.axis_size("group")
    page_size = pool.shape[1]
    copy = pltpu.make_async_copy(table_hbm, table, table_sem)
    copy.start()
    for d in range(groups + 1):
        start_of[d] = 0
        count_of[d] = 0
    zero_page[...] = jnp.zeros_like(zero_page)
    copy.wait()

    def visit(r, running):
        length, home, destination = unpacked(table[r], groups)
        mine = home == me
        count = (length + page_size - 1) // page_size
        to = jnp.where(mine, destination, groups)
        start_of[to] = running
        count_of[to] = count
        return running + jnp.where(mine, count, 0)

    lax.fori_loop(0, table.shape[0], visit, jnp.int32(0), unroll=8)
    targets = [(routed(me, route, dims), send, 0) for route, send in zip(routes, sends)]
    if own:
        targets.append((me, received[0], me * MAX_PAGES))

    def each(do):
        for i, (to, target, base) in enumerate(targets):
            for page in range(MAX_PAGES):
                there = page < count_of[to]
                source = pool.at[jnp.where(there, start_of[to] + page, 0)]
                buffer, place = held.at[i, page], target.at[base + page]
                do(there, (source, buffer, in_sems.at[i, page]), (buffer, place, out_sem), (zero_page, place, out_sem))

    def fetch(there, load, store, blank):
        @pl.when(there)
        def _():
            pltpu.make_async_copy(*load).start()

        @pl.when(jnp.logical_not(there))
        def _():
            pltpu.make_async_copy(*blank).start()

    def forward(there, load, store, blank):
        @pl.when(there)
        def _():
            pltpu.make_async_copy(*load).wait()
            pltpu.make_async_copy(*store).start()

    def finish(there, load, store, blank):
        pltpu.make_async_copy(*blank).wait()

    each(fetch)
    each(forward)
    each(finish)


def prepare(dims, routes, table, pool, own, after=()):
    groups = lax.axis_size("group")
    page = pool.shape[1:]
    blocks = len(routes) + (1 if own else 0)
    hbm = pl.BlockSpec(memory_space=pl.ANY)
    block = jax.ShapeDtypeStruct((MAX_PAGES,) + page, pool.dtype)
    outs = [jax.ShapeDtypeStruct((groups * MAX_PAGES,) + page, pool.dtype)] * own + [block] * len(routes)
    operands = [table, pool, *after]
    return pl.pallas_call(
        functools.partial(prepare_kernel, dims, routes, own),
        out_shape=outs,
        in_specs=[hbm] * len(operands),
        out_specs=[hbm] * len(outs),
        scratch_shapes=[
            pltpu.SMEM(table.shape, jnp.int32),
            pltpu.VMEM((blocks, MAX_PAGES) + page, pool.dtype),
            pltpu.VMEM(page, pool.dtype),
            pltpu.SMEM((groups + 1,), jnp.int32),
            pltpu.SMEM((groups + 1,), jnp.int32),
            pltpu.SemaphoreType.DMA,
            pltpu.SemaphoreType.DMA((blocks, MAX_PAGES)),
            pltpu.SemaphoreType.DMA,
        ],
        compiler_params=pltpu.CompilerParams(vmem_limit_bytes=VMEM_LIMIT),
        cost_estimate=pl.CostEstimate(
            flops=0, bytes_accessed=4 * blocks * MAX_PAGES * math.prod(page), transcendentals=0
        ),
        name="outgoing_pages",
    )(*operands)


def attend_row(query, pages, length):
    first, second = pages
    kv_heads = first.shape[1] // (2 * HD)
    share = query.shape[0] // kv_heads
    scores = []
    for h in range(kv_heads):
        columns = slice(2 * h * HD, (2 * h + 1) * HD)
        keys = jnp.concatenate([first[:, columns], second[:, columns]], axis=0)
        every = lax.dot_general(
            query, keys, (((1,), (1,)), ((), ())), preferred_element_type=jnp.float32
        )
        scores.append(every[h * share : (h + 1) * share])
    score = jnp.concatenate(scores, axis=0) * (1.0 / math.sqrt(HD))
    live = lax.broadcasted_iota(jnp.int32, score.shape, 1) < length
    masked = jnp.where(live, score, -1e30)
    highest = jnp.max(masked, axis=1, keepdims=True)
    weights = jnp.where(live, jnp.exp(masked - highest), 0.0)
    totals = jnp.sum(weights, axis=1, keepdims=True)
    rounded = weights.astype(jnp.bfloat16)
    mixtures = []
    for h in range(kv_heads):
        columns = slice((2 * h + 1) * HD, (2 * h + 2) * HD)
        values = jnp.concatenate([first[:, columns], second[:, columns]], axis=0)
        every = jnp.dot(rounded, values, preferred_element_type=jnp.float32)
        mixtures.append(every[h * share : (h + 1) * share])
    return jnp.concatenate(mixtures, axis=0) / totals


def settle_kernel(dims, routes, own, last, table, row_request, queries, rows_in, received_in, *rest):
    blocks = rest[: len(routes)]
    received, out, rows, held, list_row, list_block, list_length, in_sems, out_sems = rest[len(routes) :]
    me = lax.axis_index("group")
    row_local, query_heads, _ = queries.shape
    mine = pl.ds(me * MAX_PAGES, MAX_PAGES)
    origins = [routed(me, reverse(route), dims) for route in routes]
    places = [pl.ds(origin * MAX_PAGES, MAX_PAGES) for origin in origins]
    sources = list(blocks) + ([received_in.at[mine]] if own else [])
    origins += [me] if own else []
    loads = [pltpu.make_async_copy(s, held.at[i], in_sems.at[i]) for i, s in enumerate(sources)]
    stores = [
        pltpu.make_async_copy(held.at[i], received.at[place], out_sems.at[i]) for i, place in enumerate(places)
    ]
    for load in loads:
        load.start()

    found = jnp.int32(0)
    for b in range(row_local):
        length, home, _ = unpacked(table[row_request[me * row_local + b]], math.prod(dims))
        block, match = jnp.int32(0), jnp.int32(0)
        for i, origin in enumerate(origins):
            block = jnp.where(home == origin, i, block)
            match = jnp.where(home == origin, 1, match)
        list_row[found] = b
        list_block[found] = block
        list_length[found] = length
        found = found + match
    for i in range(ROW_UNROLL):
        list_row[found + i] = row_local
        list_block[found + i] = 0
        list_length[found + i] = 1
    rows[:row_local] = rows_in[...]
    for load in loads:
        load.wait()
    for store in stores:
        store.start()

    @pl.loop(0, (found + ROW_UNROLL - 1) // ROW_UNROLL)
    def _(step):
        results = []
        for i in range(ROW_UNROLL):
            at = step * ROW_UNROLL + i
            query = queries[jnp.minimum(list_row[at], row_local - 1)]
            pages = [held[list_block[at], page] for page in range(MAX_PAGES)]
            results.append(attend_row(query, pages, list_length[at]))
        for i, result in enumerate(results):
            rows[list_row[step * ROW_UNROLL + i]] = result

    if last:
        for h in range(query_heads):
            out[:, h * HD : (h + 1) * HD] = rows[:row_local, h, :].astype(out.dtype)
    else:
        out[...] = rows[:row_local]
    for store in stores:
        store.wait()


def settle(dims, routes, own, last, table, row_request, queries, rows, received, blocks):
    row_local, query_heads, _ = queries.shape
    smem = pl.BlockSpec(memory_space=pltpu.SMEM)
    vmem = pl.BlockSpec(memory_space=pltpu.VMEM)
    hbm = pl.BlockSpec(memory_space=pl.ANY)
    count = len(blocks) + (1 if own else 0)
    if last:
        out = jax.ShapeDtypeStruct((row_local, query_heads * HD), jnp.bfloat16)
    else:
        out = jax.ShapeDtypeStruct(rows.shape, rows.dtype)
    return pl.pallas_call(
        functools.partial(settle_kernel, dims, routes, own, last),
        out_shape=[jax.ShapeDtypeStruct(received.shape, received.dtype), out],
        in_specs=[smem, smem, vmem, vmem, hbm] + [hbm] * len(blocks),
        out_specs=[hbm, vmem],
        scratch_shapes=[
            pltpu.VMEM((row_local + 1, query_heads, HD), jnp.float32),
            pltpu.VMEM((count, MAX_PAGES) + received.shape[1:], received.dtype),
            pltpu.SMEM((row_local + ROW_UNROLL,), jnp.int32),
            pltpu.SMEM((row_local + ROW_UNROLL,), jnp.int32),
            pltpu.SMEM((row_local + ROW_UNROLL,), jnp.int32),
            pltpu.SemaphoreType.DMA((count,)),
            pltpu.SemaphoreType.DMA((count,)),
        ],
        input_output_aliases={4: 0},
        compiler_params=pltpu.CompilerParams(vmem_limit_bytes=VMEM_LIMIT),
        cost_estimate=pl.CostEstimate(
            flops=1 << 30, bytes_accessed=4 * sum(b.size for b in blocks), transcendentals=1 << 18
        ),
        name="settle_pages",
    )(table, row_request, queries, rows, received, *blocks)


def multiply_rows(shards, out_weight, attended, sems):
    copies = []
    row_local = shards[0].shape[0]
    for i, shard in enumerate(shards):
        copies.append(pltpu.make_async_copy(shard, attended.at[pl.ds(i * row_local, row_local)], sems.at[i]))
        copies[-1].start()
    for copy in copies:
        copy.wait()
    return jnp.dot(attended[...], out_weight[...], preferred_element_type=jnp.float32)


def project_some_kernel(count, out_weight, *rest):
    out, attended, sems = rest[count:]
    out[...] = multiply_rows(rest[:count], out_weight, attended, sems)


def project_rest_kernel(masks, count, out_weight, some, *rest):
    own, *theirs = rest[count:-3]
    attended, product, sems = rest[-3:]
    me = lax.axis_index("group")
    heads = lax.axis_size("head")
    my_head = lax.axis_index("head")
    row_local = rest[0].shape[0]
    share = own.shape[0]
    product[...] = multiply_rows(rest[:count], out_weight, attended, sems)
    for i, mask in enumerate(masks):
        done = len(masks) - count
        part = some if i < done else product
        at = i if i < done else i - done
        values = part[at * row_local : (at + 1) * row_local]
        row = (me ^ mask) * row_local
        ahead = lax.rem(row // share - my_head + heads, heads)
        place = pl.ds(pl.multiple_of(lax.rem(row, share), row_local), row_local)
        for k, out in enumerate([own, *theirs]):

            @pl.when(ahead == k)
            def _():
                out[place] = values.astype(out.dtype)


def project(gathered, out_weight, heads):
    masks = [mask for mask in gathered if mask % 2 == 0] + [mask for mask in gathered if mask % 2]
    some = len(masks) // 2
    row_local, width = gathered[0].shape
    columns = out_weight.shape[1]
    share = row_local * len(masks) // heads
    vmem = pl.BlockSpec(memory_space=pltpu.VMEM)
    hbm = pl.BlockSpec(memory_space=pl.ANY)

    def call(kernel, name, outs, blocks, extra, scratch):
        rows = row_local * len(blocks)
        return pl.pallas_call(
            kernel,
            out_shape=outs,
            in_specs=[vmem] * (1 + len(extra)) + [hbm] * len(blocks),
            out_specs=[vmem] * len(outs),
            scratch_shapes=[
                pltpu.VMEM((rows, width), jnp.bfloat16),
                *scratch,
                pltpu.SemaphoreType.DMA((len(blocks),)),
            ],
            compiler_params=pltpu.CompilerParams(vmem_limit_bytes=VMEM_LIMIT),
            cost_estimate=pl.CostEstimate(
                flops=2 * rows * width * columns, bytes_accessed=2 * out_weight.size, transcendentals=0
            ),
            name=name,
        )(out_weight, *extra, *blocks)

    out_weight = pltpu.with_memory_space_constraint(out_weight, pltpu.VMEM)
    first = [gathered[mask] for mask in masks[:some]]
    last = [gathered[mask] for mask in masks[some:]]
    (done,) = call(
        functools.partial(project_some_kernel, some), "project_some_rows",
        [jax.ShapeDtypeStruct((some * row_local, columns), jnp.float32)], first, [], [],
    )
    theirs = jax.ShapeDtypeStruct((share, columns), jnp.bfloat16)
    return call(
        functools.partial(project_rest_kernel, masks, len(last)), "project_rows",
        [jax.ShapeDtypeStruct((share, columns), jnp.float32)] + [theirs] * (heads - 1), last, [done],
        [pltpu.VMEM((len(last) * row_local, columns), jnp.float32)],
    )


def local(kv_pool, lengths, prefill_of, decode_of, row_request, queries, out_weight):
    row_local, query_width = queries.shape
    query_heads = queries.reshape(row_local, query_width // HD, HD)
    heads = lax.axis_size("head")

    dims = factors(lax.axis_size("group"))
    routes = page_rounds(dims)
    table = packed(lengths, prefill_of, decode_of, math.prod(dims))
    kv_pool = pltpu.with_memory_space_constraint(kv_pool, pltpu.HBM)
    early = prepare(dims, routes[:EARLY], table, kv_pool, False)
    received, *late = prepare(dims, routes[EARLY:], table, kv_pool, True, early[:1])
    arrived = [send_by(block, route, dims) for block, route in zip([*early, *late], routes)]
    rows = jnp.zeros(query_heads.shape, jnp.float32)
    for first in range(0, len(routes), WAVE):
        wave = slice(first, first + WAVE)
        last = first + WAVE >= len(routes)
        received, rows = settle(
            dims, routes[wave], first == 0, last, table, row_request, query_heads, rows, received, arrived[wave]
        )

    own, *theirs = project(gather_shards(rows), out_weight, heads)
    for ahead_by, part in enumerate(theirs, 1):
        pairs = [(h, (h + ahead_by) % heads) for h in range(heads)]
        own = own + lax.ppermute(part, "head", pairs).astype(jnp.float32)
    return (received, own.astype(jnp.bfloat16))


def solution(mesh):
    in_specs = (
        P("group", None, "head"),
        P(),
        P(),
        P(),
        P(),
        P("group", "head"),
        P("head", "group"),
    )
    assert mesh.shape["group"] & (mesh.shape["group"] - 1) == 0
    out_specs = (P("group", None, "head"), P("head", "group"))
    return jax.shard_map(local, mesh=mesh, in_specs=in_specs, out_specs=out_specs, check_vma=False)
```

```python
import functools
import math

import jax
import jax.numpy as jnp
from jax import lax
from jax.experimental import pallas as pl
from jax.experimental.pallas import tpu as pltpu
from jax.sharding import PartitionSpec as P

HD = 128
MAX_PAGES = 2
WAVE = 3
ROW_UNROLL = 4
EARLY = 2
VMEM_LIMIT = 20 * 1024 * 1024


def factors(groups):
    near = math.gcd(groups, 4)
    return groups // near, near


def uniform(step, swap, dims):
    return tuple(((z + step) % dims[0], swap) for z in range(dims[0]))


def page_rounds(dims):
    far, near = dims
    half = max(near // 2, 1)
    order = []
    for low in range(0, near, half):
        swaps = range(low, min(low + half, near))
        opening = [(1, n) for n in swaps] if low == 0 else [(z, n) for n in swaps for z in (1, 0)]
        rest = [(z, n) for n in swaps for z in range(2, far)]
        order += opening + ([(0, n) for n in swaps if n] if low == 0 else []) + rest
    return [uniform(z, n, dims) for z, n in order]


def reverse(route):
    sources = {to: (z, swap) for z, (to, swap) in enumerate(route)}
    return tuple(sources[z] for z in range(len(route)))


def routed(me, route, dims):
    near = dims[1]
    z = me // near
    to, swap = jnp.int32(route[0][0]), jnp.int32(route[0][1])
    for place in range(1, dims[0]):
        to = jnp.where(z == place, route[place][0], to)
        swap = jnp.where(z == place, route[place][1], swap)
    return to * near + (me % near ^ swap)


def send_by(array, route, dims):
    far, near = dims
    pairs = [
        (z * near + n, route[z][0] * near + (n ^ route[z][1])) for z in range(far) for n in range(near)
    ]
    return lax.ppermute(array, "group", pairs)


def swap(array, mask):
    groups = lax.axis_size("group")
    return lax.ppermute(array, "group", [(s, s ^ mask) for s in range(groups)])


def gather_shards(shard):
    held = {0: shard}
    mask = lax.axis_size("group") // 2
    while mask:
        held.update({done | mask: swap(array, mask) for done, array in held.items()})
        mask //= 2
    return held


def packed(lengths, prefill_of, decode_of, groups):
    bits = (groups - 1).bit_length()
    return (lengths << 2 * bits) | (prefill_of << bits) | decode_of


def unpacked(entry, groups):
    bits = (groups - 1).bit_length()
    mask = (1 << bits) - 1
    return entry >> 2 * bits, (entry >> bits) & mask, entry & mask


def prepare_kernel(dims, routes, own, table_hbm, pool, *rest):
    table, held, zero_page, start_of, count_of, table_sem, in_sems, out_sem = rest[-8:]
    received = rest[-8 - len(routes) - own : -8 - len(routes)]
    sends = rest[-8 - len(routes) : -8]
    me = lax.axis_index("group")
    groups = lax.axis_size("group")
    page_size = pool.shape[1]
    copy = pltpu.make_async_copy(table_hbm, table, table_sem)
    copy.start()
    for d in range(groups + 1):
        start_of[d] = 0
        count_of[d] = 0
    zero_page[...] = jnp.zeros_like(zero_page)
    copy.wait()

    def visit(r, running):
        length, home, destination = unpacked(table[r], groups)
        mine = home == me
        count = (length + page_size - 1) // page_size
        to = jnp.where(mine, destination, groups)
        start_of[to] = running
        count_of[to] = count
        return running + jnp.where(mine, count, 0)

    lax.fori_loop(0, table.shape[0], visit, jnp.int32(0), unroll=8)
    targets = [(routed(me, route, dims), send, 0) for route, send in zip(routes, sends)]
    if own:
        targets.append((me, received[0], me * MAX_PAGES))

    def each(do):
        for i, (to, target, base) in enumerate(targets):
            for page in range(MAX_PAGES):
                there = page < count_of[to]
                source = pool.at[jnp.where(there, start_of[to] + page, 0)]
                buffer, place = held.at[i, page], target.at[base + page]
                do(there, (source, buffer, in_sems.at[i, page]), (buffer, place, out_sem), (zero_page, place, out_sem))

    def fetch(there, load, store, blank):
        @pl.when(there)
        def _():
            pltpu.make_async_copy(*load).start()

        @pl.when(jnp.logical_not(there))
        def _():
            pltpu.make_async_copy(*blank).start()

    def forward(there, load, store, blank):
        @pl.when(there)
        def _():
            pltpu.make_async_copy(*load).wait()
            pltpu.make_async_copy(*store).start()

    def finish(there, load, store, blank):
        pltpu.make_async_copy(*blank).wait()

    each(fetch)
    each(forward)
    each(finish)


def prepare(dims, routes, table, pool, own, after=()):
    groups = lax.axis_size("group")
    page = pool.shape[1:]
    blocks = len(routes) + (1 if own else 0)
    hbm = pl.BlockSpec(memory_space=pl.ANY)
    block = jax.ShapeDtypeStruct((MAX_PAGES,) + page, pool.dtype)
    outs = [jax.ShapeDtypeStruct((groups * MAX_PAGES,) + page, pool.dtype)] * own + [block] * len(routes)
    operands = [table, pool, *after]
    return pl.pallas_call(
        functools.partial(prepare_kernel, dims, routes, own),
        out_shape=outs,
        in_specs=[hbm] * len(operands),
        out_specs=[hbm] * len(outs),
        scratch_shapes=[
            pltpu.SMEM(table.shape, jnp.int32),
            pltpu.VMEM((blocks, MAX_PAGES) + page, pool.dtype),
            pltpu.VMEM(page, pool.dtype),
            pltpu.SMEM((groups + 1,), jnp.int32),
            pltpu.SMEM((groups + 1,), jnp.int32),
            pltpu.SemaphoreType.DMA,
            pltpu.SemaphoreType.DMA((blocks, MAX_PAGES)),
            pltpu.SemaphoreType.DMA,
        ],
        compiler_params=pltpu.CompilerParams(vmem_limit_bytes=VMEM_LIMIT),
        cost_estimate=pl.CostEstimate(
            flops=0, bytes_accessed=4 * blocks * MAX_PAGES * math.prod(page), transcendentals=0
        ),
        name="outgoing_pages",
    )(*operands)


def attend_row(query, pages, length):
    first, second = pages
    kv_heads = first.shape[1] // (2 * HD)
    share = query.shape[0] // kv_heads
    scores = []
    for h in range(kv_heads):
        columns = slice(2 * h * HD, (2 * h + 1) * HD)
        keys = jnp.concatenate([first[:, columns], second[:, columns]], axis=0)
        every = lax.dot_general(
            query, keys, (((1,), (1,)), ((), ())), preferred_element_type=jnp.float32
        )
        scores.append(every[h * share : (h + 1) * share])
    score = jnp.concatenate(scores, axis=0) * (1.0 / math.sqrt(HD))
    live = lax.broadcasted_iota(jnp.int32, score.shape, 1) < length
    masked = jnp.where(live, score, -1e30)
    highest = jnp.max(masked, axis=1, keepdims=True)
    weights = jnp.where(live, jnp.exp(masked - highest), 0.0)
    totals = jnp.sum(weights, axis=1, keepdims=True)
    rounded = weights.astype(jnp.bfloat16)
    mixtures = []
    for h in range(kv_heads):
        columns = slice((2 * h + 1) * HD, (2 * h + 2) * HD)
        values = jnp.concatenate([first[:, columns], second[:, columns]], axis=0)
        every = jnp.dot(rounded, values, preferred_element_type=jnp.float32)
        mixtures.append(every[h * share : (h + 1) * share])
    return jnp.concatenate(mixtures, axis=0) / totals


def settle_kernel(dims, routes, own, last, table, row_request, queries, rows_in, received_in, *rest):
    blocks = rest[: len(routes)]
    received, out, rows, held, list_row, list_block, list_length, in_sems, out_sems = rest[len(routes) :]
    me = lax.axis_index("group")
    row_local, query_heads, _ = queries.shape
    mine = pl.ds(me * MAX_PAGES, MAX_PAGES)
    origins = [routed(me, reverse(route), dims) for route in routes]
    places = [pl.ds(origin * MAX_PAGES, MAX_PAGES) for origin in origins]
    sources = list(blocks) + ([received_in.at[mine]] if own else [])
    origins += [me] if own else []
    loads = [pltpu.make_async_copy(s, held.at[i], in_sems.at[i]) for i, s in enumerate(sources)]
    stores = [
        pltpu.make_async_copy(held.at[i], received.at[place], out_sems.at[i]) for i, place in enumerate(places)
    ]
    for load in loads:
        load.start()

    found = jnp.int32(0)
    for b in range(row_local):
        length, home, _ = unpacked(table[row_request[me * row_local + b]], math.prod(dims))
        block, match = jnp.int32(0), jnp.int32(0)
        for i, origin in enumerate(origins):
            block = jnp.where(home == origin, i, block)
            match = jnp.where(home == origin, 1, match)
        list_row[found] = b
        list_block[found] = block
        list_length[found] = length
        found = found + match
    for i in range(ROW_UNROLL):
        list_row[found + i] = row_local
        list_block[found + i] = 0
        list_length[found + i] = 1
    rows[:row_local] = rows_in[...]
    for load in loads:
        load.wait()
    for store in stores:
        store.start()

    @pl.loop(0, (found + ROW_UNROLL - 1) // ROW_UNROLL)
    def _(step):
        results = []
        for i in range(ROW_UNROLL):
            at = step * ROW_UNROLL + i
            query = queries[jnp.minimum(list_row[at], row_local - 1)]
            pages = [held[list_block[at], page] for page in range(MAX_PAGES)]
            results.append(attend_row(query, pages, list_length[at]))
        for i, result in enumerate(results):
            rows[list_row[step * ROW_UNROLL + i]] = result

    if last:
        for h in range(query_heads):
            out[:, h * HD : (h + 1) * HD] = rows[:row_local, h, :].astype(out.dtype)
    else:
        out[...] = rows[:row_local]
    for store in stores:
        store.wait()


def settle(dims, routes, own, last, table, row_request, queries, rows, received, blocks):
    row_local, query_heads, _ = queries.shape
    smem = pl.BlockSpec(memory_space=pltpu.SMEM)
    vmem = pl.BlockSpec(memory_space=pltpu.VMEM)
    hbm = pl.BlockSpec(memory_space=pl.ANY)
    count = len(blocks) + (1 if own else 0)
    if last:
        out = jax.ShapeDtypeStruct((row_local, query_heads * HD), jnp.bfloat16)
    else:
        out = jax.ShapeDtypeStruct(rows.shape, rows.dtype)
    return pl.pallas_call(
        functools.partial(settle_kernel, dims, routes, own, last),
        out_shape=[jax.ShapeDtypeStruct(received.shape, received.dtype), out],
        in_specs=[smem, smem, vmem, vmem, hbm] + [hbm] * len(blocks),
        out_specs=[hbm, vmem],
        scratch_shapes=[
            pltpu.VMEM((row_local + 1, query_heads, HD), jnp.float32),
            pltpu.VMEM((count, MAX_PAGES) + received.shape[1:], received.dtype),
            pltpu.SMEM((row_local + ROW_UNROLL,), jnp.int32),
            pltpu.SMEM((row_local + ROW_UNROLL,), jnp.int32),
            pltpu.SMEM((row_local + ROW_UNROLL,), jnp.int32),
            pltpu.SemaphoreType.DMA((count,)),
            pltpu.SemaphoreType.DMA((count,)),
        ],
        input_output_aliases={4: 0},
        compiler_params=pltpu.CompilerParams(vmem_limit_bytes=VMEM_LIMIT),
        cost_estimate=pl.CostEstimate(
            flops=1 << 30, bytes_accessed=4 * sum(b.size for b in blocks), transcendentals=1 << 18
        ),
        name="settle_pages",
    )(table, row_request, queries, rows, received, *blocks)


def multiply_rows(shards, out_weight, attended, sems):
    copies = []
    row_local = shards[0].shape[0]
    for i, shard in enumerate(shards):
        copies.append(pltpu.make_async_copy(shard, attended.at[pl.ds(i * row_local, row_local)], sems.at[i]))
        copies[-1].start()
    for copy in copies:
        copy.wait()
    return jnp.dot(attended[...], out_weight[...], preferred_element_type=jnp.float32)


def project_some_kernel(count, out_weight, *rest):
    out, attended, sems = rest[count:]
    out[...] = multiply_rows(rest[:count], out_weight, attended, sems)


def project_rest_kernel(masks, count, out_weight, some, *rest):
    own, *theirs = rest[count:-3]
    attended, product, sems = rest[-3:]
    me = lax.axis_index("group")
    heads = lax.axis_size("head")
    my_head = lax.axis_index("head")
    row_local = rest[0].shape[0]
    share = own.shape[0]
    product[...] = multiply_rows(rest[:count], out_weight, attended, sems)
    for i, mask in enumerate(masks):
        done = len(masks) - count
        part = some if i < done else product
        at = i if i < done else i - done
        values = part[at * row_local : (at + 1) * row_local]
        row = (me ^ mask) * row_local
        ahead = lax.rem(row // share - my_head + heads, heads)
        place = pl.ds(pl.multiple_of(lax.rem(row, share), row_local), row_local)
        for k, out in enumerate([own, *theirs]):

            @pl.when(ahead == k)
            def _():
                out[place] = values.astype(out.dtype)


def project(gathered, out_weight, heads):
    masks = [mask for mask in gathered if mask % 2 == 0] + [mask for mask in gathered if mask % 2]
    some = len(masks) // 2
    row_local, width = gathered[0].shape
    columns = out_weight.shape[1]
    share = row_local * len(masks) // heads
    vmem = pl.BlockSpec(memory_space=pltpu.VMEM)
    hbm = pl.BlockSpec(memory_space=pl.ANY)

    def call(kernel, name, outs, blocks, extra, scratch):
        rows = row_local * len(blocks)
        return pl.pallas_call(
            kernel,
            out_shape=outs,
            in_specs=[vmem] * (1 + len(extra)) + [hbm] * len(blocks),
            out_specs=[vmem] * len(outs),
            scratch_shapes=[
                pltpu.VMEM((rows, width), jnp.bfloat16),
                *scratch,
                pltpu.SemaphoreType.DMA((len(blocks),)),
            ],
            compiler_params=pltpu.CompilerParams(vmem_limit_bytes=VMEM_LIMIT),
            cost_estimate=pl.CostEstimate(
                flops=2 * rows * width * columns, bytes_accessed=2 * out_weight.size, transcendentals=0
            ),
            name=name,
        )(out_weight, *extra, *blocks)

    out_weight = pltpu.with_memory_space_constraint(out_weight, pltpu.VMEM)
    first = [gathered[mask] for mask in masks[:some]]
    last = [gathered[mask] for mask in masks[some:]]
    (done,) = call(
        functools.partial(project_some_kernel, some), "project_some_rows",
        [jax.ShapeDtypeStruct((some * row_local, columns), jnp.float32)], first, [], [],
    )
    theirs = jax.ShapeDtypeStruct((share, columns), jnp.bfloat16)
    return call(
        functools.partial(project_rest_kernel, masks, len(last)), "project_rows",
        [jax.ShapeDtypeStruct((share, columns), jnp.float32)] + [theirs] * (heads - 1), last, [done],
        [pltpu.VMEM((len(last) * row_local, columns), jnp.float32)],
    )


def local(kv_pool, lengths, prefill_of, decode_of, row_request, queries, out_weight):
    row_local, query_width = queries.shape
    query_heads = queries.reshape(row_local, query_width // HD, HD)
    heads = lax.axis_size("head")

    dims = factors(lax.axis_size("group"))
    routes = page_rounds(dims)
    table = packed(lengths, prefill_of, decode_of, math.prod(dims))
    kv_pool = pltpu.with_memory_space_constraint(kv_pool, pltpu.HBM)
    early = prepare(dims, routes[:EARLY], table, kv_pool, False)
    received, *late = prepare(dims, routes[EARLY:], table, kv_pool, True, early[:1])
    arrived = [send_by(block, route, dims) for block, route in zip([*early, *late], routes)]
    rows = jnp.zeros(query_heads.shape, jnp.float32)
    for first in range(0, len(routes), WAVE):
        wave = slice(first, first + WAVE)
        last = first + WAVE >= len(routes)
        received, rows = settle(
            dims, routes[wave], first == 0, last, table, row_request, query_heads, rows, received, arrived[wave]
        )

    own, *theirs = project(gather_shards(rows), out_weight, heads)
    for ahead_by, part in enumerate(theirs, 1):
        pairs = [(h, (h + ahead_by) % heads) for h in range(heads)]
        own = own + lax.ppermute(part, "head", pairs).astype(jnp.float32)
    return (received, own.astype(jnp.bfloat16))


def solution(mesh):
    in_specs = (
        P("group", None, "head"),
        P(),
        P(),
        P(),
        P(),
        P("group", "head"),
        P("head", "group"),
    )
    assert mesh.shape["group"] & (mesh.shape["group"] - 1) == 0
    out_specs = (P("group", None, "head"), P("head", "group"))
    return jax.shard_map(local, mesh=mesh, in_specs=in_specs, out_specs=out_specs, check_vma=False)
```

```python
import functools
import math

import jax
import jax.numpy as jnp
from jax import lax
from jax.experimental import pallas as pl
from jax.experimental.pallas import tpu as pltpu
from jax.sharding import PartitionSpec as P

HD = 128
MAX_PAGES = 2
WAVE = 3
ROW_UNROLL = 4
EARLY = 2
VMEM_LIMIT = 20 * 1024 * 1024


def factors(groups):
    near = math.gcd(groups, 4)
    return groups // near, near


def uniform(step, swap, dims):
    return tuple(((z + step) % dims[0], swap) for z in range(dims[0]))


def page_rounds(dims):
    far, near = dims
    half = max(near // 2, 1)
    if far != 4:
        swaps = [range(low, min(low + half, near)) for low in range(0, near, half)]
        return [uniform(z, n, dims) for part in swaps for z in range(far) for n in part if z or n]

    def outer(swaps):
        rounds = [((2, n), (0, n), (3, n), (1, n)) for n in swaps]
        return rounds + [((3, n), (1, n), (2, n), (0, n)) for n in swaps if n]

    def inner(swaps):
        rounds = [((0, n), (2, n), (1, n), (3, n)) for n in swaps if n]
        return rounds + [((1, n), (3, n), (0, n), (2, n)) for n in swaps]

    same, other = range(half), range(half, near)
    across = [((3, 0), (2, 0), (1, 0), (0, 0))]
    return outer(same) + across + inner(same) + inner(other) + outer(other)


def reverse(route):
    sources = {to: (z, swap) for z, (to, swap) in enumerate(route)}
    return tuple(sources[z] for z in range(len(route)))


def routed(me, route, dims):
    near = dims[1]
    z = me // near
    to, swap = jnp.int32(route[0][0]), jnp.int32(route[0][1])
    for place in range(1, dims[0]):
        to = jnp.where(z == place, route[place][0], to)
        swap = jnp.where(z == place, route[place][1], swap)
    return to * near + (me % near ^ swap)


def send_by(array, route, dims):
    far, near = dims
    pairs = [
        (z * near + n, route[z][0] * near + (n ^ route[z][1])) for z in range(far) for n in range(near)
    ]
    return lax.ppermute(array, "group", pairs)


def swap(array, mask):
    groups = lax.axis_size("group")
    return lax.ppermute(array, "group", [(s, s ^ mask) for s in range(groups)])


def gather_shards(shard):
    held = {0: shard}
    mask = lax.axis_size("group") // 2
    while mask:
        held.update({done | mask: swap(array, mask) for done, array in held.items()})
        mask //= 2
    return held


def packed(lengths, prefill_of, decode_of, groups):
    bits = (groups - 1).bit_length()
    return (lengths << 2 * bits) | (prefill_of << bits) | decode_of


def unpacked(entry, groups):
    bits = (groups - 1).bit_length()
    mask = (1 << bits) - 1
    return entry >> 2 * bits, (entry >> bits) & mask, entry & mask


def prepare_kernel(dims, routes, own, table_hbm, pool, *rest):
    table, held, zero_page, start_of, count_of, table_sem, in_sems, out_sem = rest[-8:]
    received = rest[-8 - len(routes) - own : -8 - len(routes)]
    sends = rest[-8 - len(routes) : -8]
    me = lax.axis_index("group")
    groups = lax.axis_size("group")
    page_size = pool.shape[1]
    copy = pltpu.make_async_copy(table_hbm, table, table_sem)
    copy.start()
    for d in range(groups + 1):
        start_of[d] = 0
        count_of[d] = 0
    zero_page[...] = jnp.zeros_like(zero_page)
    copy.wait()

    def visit(r, running):
        length, home, destination = unpacked(table[r], groups)
        mine = home == me
        count = (length + page_size - 1) // page_size
        to = jnp.where(mine, destination, groups)
        start_of[to] = running
        count_of[to] = count
        return running + jnp.where(mine, count, 0)

    lax.fori_loop(0, table.shape[0], visit, jnp.int32(0), unroll=8)
    targets = [(routed(me, route, dims), send, 0) for route, send in zip(routes, sends)]
    if own:
        targets.append((me, received[0], me * MAX_PAGES))

    def each(do):
        for i, (to, target, base) in enumerate(targets):
            for page in range(MAX_PAGES):
                there = page < count_of[to]
                source = pool.at[jnp.where(there, start_of[to] + page, 0)]
                buffer, place = held.at[i, page], target.at[base + page]
                do(there, (source, buffer, in_sems.at[i, page]), (buffer, place, out_sem), (zero_page, place, out_sem))

    def fetch(there, load, store, blank):
        @pl.when(there)
        def _():
            pltpu.make_async_copy(*load).start()

        @pl.when(jnp.logical_not(there))
        def _():
            pltpu.make_async_copy(*blank).start()

    def forward(there, load, store, blank):
        @pl.when(there)
        def _():
            pltpu.make_async_copy(*load).wait()
            pltpu.make_async_copy(*store).start()

    def finish(there, load, store, blank):
        pltpu.make_async_copy(*blank).wait()

    each(fetch)
    each(forward)
    each(finish)


def prepare(dims, routes, table, pool, own, after=()):
    groups = lax.axis_size("group")
    page = pool.shape[1:]
    blocks = len(routes) + (1 if own else 0)
    hbm = pl.BlockSpec(memory_space=pl.ANY)
    block = jax.ShapeDtypeStruct((MAX_PAGES,) + page, pool.dtype)
    outs = [jax.ShapeDtypeStruct((groups * MAX_PAGES,) + page, pool.dtype)] * own + [block] * len(routes)
    operands = [table, pool, *after]
    return pl.pallas_call(
        functools.partial(prepare_kernel, dims, routes, own),
        out_shape=outs,
        in_specs=[hbm] * len(operands),
        out_specs=[hbm] * len(outs),
        scratch_shapes=[
            pltpu.SMEM(table.shape, jnp.int32),
            pltpu.VMEM((blocks, MAX_PAGES) + page, pool.dtype),
            pltpu.VMEM(page, pool.dtype),
            pltpu.SMEM((groups + 1,), jnp.int32),
            pltpu.SMEM((groups + 1,), jnp.int32),
            pltpu.SemaphoreType.DMA,
            pltpu.SemaphoreType.DMA((blocks, MAX_PAGES)),
            pltpu.SemaphoreType.DMA,
        ],
        compiler_params=pltpu.CompilerParams(vmem_limit_bytes=VMEM_LIMIT),
        cost_estimate=pl.CostEstimate(
            flops=0, bytes_accessed=4 * blocks * MAX_PAGES * math.prod(page), transcendentals=0
        ),
        name="outgoing_pages",
    )(*operands)


def attend_row(query, pages, length):
    first, second = pages
    kv_heads = first.shape[1] // (2 * HD)
    share = query.shape[0] // kv_heads
    scores = []
    for h in range(kv_heads):
        columns = slice(2 * h * HD, (2 * h + 1) * HD)
        keys = jnp.concatenate([first[:, columns], second[:, columns]], axis=0)
        every = lax.dot_general(
            query, keys, (((1,), (1,)), ((), ())), preferred_element_type=jnp.float32
        )
        scores.append(every[h * share : (h + 1) * share])
    score = jnp.concatenate(scores, axis=0) * (1.0 / math.sqrt(HD))
    live = lax.broadcasted_iota(jnp.int32, score.shape, 1) < length
    masked = jnp.where(live, score, -1e30)
    highest = jnp.max(masked, axis=1, keepdims=True)
    weights = jnp.where(live, jnp.exp(masked - highest), 0.0)
    totals = jnp.sum(weights, axis=1, keepdims=True)
    rounded = weights.astype(jnp.bfloat16)
    mixtures = []
    for h in range(kv_heads):
        columns = slice((2 * h + 1) * HD, (2 * h + 2) * HD)
        values = jnp.concatenate([first[:, columns], second[:, columns]], axis=0)
        every = jnp.dot(rounded, values, preferred_element_type=jnp.float32)
        mixtures.append(every[h * share : (h + 1) * share])
    return jnp.concatenate(mixtures, axis=0) / totals


def settle_kernel(dims, routes, own, last, table, row_request, queries, rows_in, received_in, *rest):
    blocks = rest[: len(routes)]
    received, out, rows, held, list_row, list_block, list_length, in_sems, out_sems = rest[len(routes) :]
    me = lax.axis_index("group")
    row_local, query_heads, _ = queries.shape
    mine = pl.ds(me * MAX_PAGES, MAX_PAGES)
    origins = [routed(me, reverse(route), dims) for route in routes]
    places = [pl.ds(origin * MAX_PAGES, MAX_PAGES) for origin in origins]
    sources = list(blocks) + ([received_in.at[mine]] if own else [])
    origins += [me] if own else []
    loads = [pltpu.make_async_copy(s, held.at[i], in_sems.at[i]) for i, s in enumerate(sources)]
    stores = [
        pltpu.make_async_copy(held.at[i], received.at[place], out_sems.at[i]) for i, place in enumerate(places)
    ]
    for load in loads:
        load.start()

    found = jnp.int32(0)
    for b in range(row_local):
        length, home, _ = unpacked(table[row_request[me * row_local + b]], math.prod(dims))
        block, match = jnp.int32(0), jnp.int32(0)
        for i, origin in enumerate(origins):
            block = jnp.where(home == origin, i, block)
            match = jnp.where(home == origin, 1, match)
        list_row[found] = b
        list_block[found] = block
        list_length[found] = length
        found = found + match
    for i in range(ROW_UNROLL):
        list_row[found + i] = row_local
        list_block[found + i] = 0
        list_length[found + i] = 1
    rows[:row_local] = rows_in[...]
    for load in loads:
        load.wait()
    for store in stores:
        store.start()

    @pl.loop(0, (found + ROW_UNROLL - 1) // ROW_UNROLL)
    def _(step):
        results = []
        for i in range(ROW_UNROLL):
            at = step * ROW_UNROLL + i
            query = queries[jnp.minimum(list_row[at], row_local - 1)]
            pages = [held[list_block[at], page] for page in range(MAX_PAGES)]
            results.append(attend_row(query, pages, list_length[at]))
        for i, result in enumerate(results):
            rows[list_row[step * ROW_UNROLL + i]] = result

    if last:
        for h in range(query_heads):
            out[:, h * HD : (h + 1) * HD] = rows[:row_local, h, :].astype(out.dtype)
    else:
        out[...] = rows[:row_local]
    for store in stores:
        store.wait()


def settle(dims, routes, own, last, table, row_request, queries, rows, received, blocks):
    row_local, query_heads, _ = queries.shape
    smem = pl.BlockSpec(memory_space=pltpu.SMEM)
    vmem = pl.BlockSpec(memory_space=pltpu.VMEM)
    hbm = pl.BlockSpec(memory_space=pl.ANY)
    count = len(blocks) + (1 if own else 0)
    if last:
        out = jax.ShapeDtypeStruct((row_local, query_heads * HD), jnp.bfloat16)
    else:
        out = jax.ShapeDtypeStruct(rows.shape, rows.dtype)
    return pl.pallas_call(
        functools.partial(settle_kernel, dims, routes, own, last),
        out_shape=[jax.ShapeDtypeStruct(received.shape, received.dtype), out],
        in_specs=[smem, smem, vmem, vmem, hbm] + [hbm] * len(blocks),
        out_specs=[hbm, vmem],
        scratch_shapes=[
            pltpu.VMEM((row_local + 1, query_heads, HD), jnp.float32),
            pltpu.VMEM((count, MAX_PAGES) + received.shape[1:], received.dtype),
            pltpu.SMEM((row_local + ROW_UNROLL,), jnp.int32),
            pltpu.SMEM((row_local + ROW_UNROLL,), jnp.int32),
            pltpu.SMEM((row_local + ROW_UNROLL,), jnp.int32),
            pltpu.SemaphoreType.DMA((count,)),
            pltpu.SemaphoreType.DMA((count,)),
        ],
        input_output_aliases={4: 0},
        compiler_params=pltpu.CompilerParams(vmem_limit_bytes=VMEM_LIMIT),
        cost_estimate=pl.CostEstimate(
            flops=1 << 30, bytes_accessed=4 * sum(b.size for b in blocks), transcendentals=1 << 18
        ),
        name="settle_pages",
    )(table, row_request, queries, rows, received, *blocks)


def multiply_rows(shards, out_weight, attended, sems):
    copies = []
    row_local = shards[0].shape[0]
    for i, shard in enumerate(shards):
        copies.append(pltpu.make_async_copy(shard, attended.at[pl.ds(i * row_local, row_local)], sems.at[i]))
        copies[-1].start()
    for copy in copies:
        copy.wait()
    return jnp.dot(attended[...], out_weight[...], preferred_element_type=jnp.float32)


def project_some_kernel(count, out_weight, *rest):
    out, attended, sems = rest[count:]
    out[...] = multiply_rows(rest[:count], out_weight, attended, sems)


def project_rest_kernel(masks, count, out_weight, some, *rest):
    own, *theirs = rest[count:-3]
    attended, product, sems = rest[-3:]
    me = lax.axis_index("group")
    heads = lax.axis_size("head")
    my_head = lax.axis_index("head")
    row_local = rest[0].shape[0]
    share = own.shape[0]
    product[...] = multiply_rows(rest[:count], out_weight, attended, sems)
    for i, mask in enumerate(masks):
        done = len(masks) - count
        part = some if i < done else product
        at = i if i < done else i - done
        values = part[at * row_local : (at + 1) * row_local]
        row = (me ^ mask) * row_local
        ahead = lax.rem(row // share - my_head + heads, heads)
        place = pl.ds(pl.multiple_of(lax.rem(row, share), row_local), row_local)
        for k, out in enumerate([own, *theirs]):

            @pl.when(ahead == k)
            def _():
                out[place] = values.astype(out.dtype)


def project(gathered, out_weight, heads):
    masks = [mask for mask in gathered if mask % 2 == 0] + [mask for mask in gathered if mask % 2]
    some = len(masks) // 2
    row_local, width = gathered[0].shape
    columns = out_weight.shape[1]
    share = row_local * len(masks) // heads
    vmem = pl.BlockSpec(memory_space=pltpu.VMEM)
    hbm = pl.BlockSpec(memory_space=pl.ANY)

    def call(kernel, name, outs, blocks, extra, scratch):
        rows = row_local * len(blocks)
        return pl.pallas_call(
            kernel,
            out_shape=outs,
            in_specs=[vmem] * (1 + len(extra)) + [hbm] * len(blocks),
            out_specs=[vmem] * len(outs),
            scratch_shapes=[
                pltpu.VMEM((rows, width), jnp.bfloat16),
                *scratch,
                pltpu.SemaphoreType.DMA((len(blocks),)),
            ],
            compiler_params=pltpu.CompilerParams(vmem_limit_bytes=VMEM_LIMIT),
            cost_estimate=pl.CostEstimate(
                flops=2 * rows * width * columns, bytes_accessed=2 * out_weight.size, transcendentals=0
            ),
            name=name,
        )(out_weight, *extra, *blocks)

    out_weight = pltpu.with_memory_space_constraint(out_weight, pltpu.VMEM)
    first = [gathered[mask] for mask in masks[:some]]
    last = [gathered[mask] for mask in masks[some:]]
    (done,) = call(
        functools.partial(project_some_kernel, some), "project_some_rows",
        [jax.ShapeDtypeStruct((some * row_local, columns), jnp.float32)], first, [], [],
    )
    theirs = jax.ShapeDtypeStruct((share, columns), jnp.bfloat16)
    return call(
        functools.partial(project_rest_kernel, masks, len(last)), "project_rows",
        [jax.ShapeDtypeStruct((share, columns), jnp.float32)] + [theirs] * (heads - 1), last, [done],
        [pltpu.VMEM((len(last) * row_local, columns), jnp.float32)],
    )


def local(kv_pool, lengths, prefill_of, decode_of, row_request, queries, out_weight):
    row_local, query_width = queries.shape
    query_heads = queries.reshape(row_local, query_width // HD, HD)
    heads = lax.axis_size("head")

    dims = factors(lax.axis_size("group"))
    routes = page_rounds(dims)
    table = packed(lengths, prefill_of, decode_of, math.prod(dims))
    kv_pool = pltpu.with_memory_space_constraint(kv_pool, pltpu.HBM)
    early = prepare(dims, routes[:EARLY], table, kv_pool, False)
    received, *late = prepare(dims, routes[EARLY:], table, kv_pool, True, early[:1])
    arrived = [send_by(block, route, dims) for block, route in zip([*early, *late], routes)]
    rows = jnp.zeros(query_heads.shape, jnp.float32)
    for first in range(0, len(routes), WAVE):
        wave = slice(first, first + WAVE)
        last = first + WAVE >= len(routes)
        received, rows = settle(
            dims, routes[wave], first == 0, last, table, row_request, query_heads, rows, received, arrived[wave]
        )

    own, *theirs = project(gather_shards(rows), out_weight, heads)
    for ahead_by, part in enumerate(theirs, 1):
        pairs = [(h, (h + ahead_by) % heads) for h in range(heads)]
        own = own + lax.ppermute(part, "head", pairs).astype(jnp.float32)
    return (received, own.astype(jnp.bfloat16))


def solution(mesh):
    in_specs = (
        P("group", None, "head"),
        P(),
        P(),
        P(),
        P(),
        P("group", "head"),
        P("head", "group"),
    )
    assert mesh.shape["group"] & (mesh.shape["group"] - 1) == 0
    out_specs = (P("group", None, "head"), P("head", "group"))
    return jax.shard_map(local, mesh=mesh, in_specs=in_specs, out_specs=out_specs, check_vma=False)
```

```python
import functools
import math

import jax
import jax.numpy as jnp
from jax import lax
from jax.experimental import pallas as pl
from jax.experimental.pallas import tpu as pltpu
from jax.sharding import PartitionSpec as P

HD = 128
MAX_PAGES = 2
WAVE = 3
ROW_UNROLL = 4
EARLY = 2
VMEM_LIMIT = 20 * 1024 * 1024


def factors(groups):
    near = math.gcd(groups, 4)
    return groups // near, near


def uniform(step, swap, dims):
    return tuple(((z + step) % dims[0], swap) for z in range(dims[0]))


def page_rounds(dims):
    far, near = dims
    half = max(near // 2, 1)
    if far != 4:
        swaps = [range(low, min(low + half, near)) for low in range(0, near, half)]
        return [uniform(z, n, dims) for part in swaps for z in range(far) for n in part if z or n]

    def rounds(swaps):
        outer = [((2, n), (0, n), (3, n), (1, n)) for n in swaps]
        inner = [((1, n), (3, n), (0, n), (2, n)) for n in swaps]
        across = [tuple((3 - z, n) for z in range(far)) for n in swaps]
        here = [uniform(0, n, dims) for n in swaps if n]
        return outer + inner + [r for pair in zip([[]] * (len(across) - len(here)) + here, across) for r in pair if r]

    return rounds(range(half)) + rounds(range(half, near))


def reverse(route):
    sources = {to: (z, swap) for z, (to, swap) in enumerate(route)}
    return tuple(sources[z] for z in range(len(route)))


def routed(me, route, dims):
    near = dims[1]
    z = me // near
    to, swap = jnp.int32(route[0][0]), jnp.int32(route[0][1])
    for place in range(1, dims[0]):
        to = jnp.where(z == place, route[place][0], to)
        swap = jnp.where(z == place, route[place][1], swap)
    return to * near + (me % near ^ swap)


def send_by(array, route, dims):
    far, near = dims
    pairs = [
        (z * near + n, route[z][0] * near + (n ^ route[z][1])) for z in range(far) for n in range(near)
    ]
    return lax.ppermute(array, "group", pairs)


def swap(array, mask):
    groups = lax.axis_size("group")
    return lax.ppermute(array, "group", [(s, s ^ mask) for s in range(groups)])


def gather_shards(shard):
    held = {0: shard}
    mask = lax.axis_size("group") // 2
    while mask:
        held.update({done | mask: swap(array, mask) for done, array in held.items()})
        mask //= 2
    return held


def packed(lengths, prefill_of, decode_of, groups):
    bits = (groups - 1).bit_length()
    return (lengths << 2 * bits) | (prefill_of << bits) | decode_of


def unpacked(entry, groups):
    bits = (groups - 1).bit_length()
    mask = (1 << bits) - 1
    return entry >> 2 * bits, (entry >> bits) & mask, entry & mask


def prepare_kernel(dims, routes, own, table_hbm, pool, *rest):
    table, held, zero_page, start_of, count_of, table_sem, in_sems, out_sem = rest[-8:]
    received = rest[-8 - len(routes) - own : -8 - len(routes)]
    sends = rest[-8 - len(routes) : -8]
    me = lax.axis_index("group")
    groups = lax.axis_size("group")
    page_size = pool.shape[1]
    copy = pltpu.make_async_copy(table_hbm, table, table_sem)
    copy.start()
    for d in range(groups + 1):
        start_of[d] = 0
        count_of[d] = 0
    zero_page[...] = jnp.zeros_like(zero_page)
    copy.wait()

    def visit(r, running):
        length, home, destination = unpacked(table[r], groups)
        mine = home == me
        count = (length + page_size - 1) // page_size
        to = jnp.where(mine, destination, groups)
        start_of[to] = running
        count_of[to] = count
        return running + jnp.where(mine, count, 0)

    lax.fori_loop(0, table.shape[0], visit, jnp.int32(0), unroll=8)
    targets = [(routed(me, route, dims), send, 0) for route, send in zip(routes, sends)]
    if own:
        targets.append((me, received[0], me * MAX_PAGES))

    def each(do):
        for i, (to, target, base) in enumerate(targets):
            for page in range(MAX_PAGES):
                there = page < count_of[to]
                source = pool.at[jnp.where(there, start_of[to] + page, 0)]
                buffer, place = held.at[i, page], target.at[base + page]
                do(there, (source, buffer, in_sems.at[i, page]), (buffer, place, out_sem), (zero_page, place, out_sem))

    def fetch(there, load, store, blank):
        @pl.when(there)
        def _():
            pltpu.make_async_copy(*load).start()

        @pl.when(jnp.logical_not(there))
        def _():
            pltpu.make_async_copy(*blank).start()

    def forward(there, load, store, blank):
        @pl.when(there)
        def _():
            pltpu.make_async_copy(*load).wait()
            pltpu.make_async_copy(*store).start()

    def finish(there, load, store, blank):
        pltpu.make_async_copy(*blank).wait()

    each(fetch)
    each(forward)
    each(finish)


def prepare(dims, routes, table, pool, own, after=()):
    groups = lax.axis_size("group")
    page = pool.shape[1:]
    blocks = len(routes) + (1 if own else 0)
    hbm = pl.BlockSpec(memory_space=pl.ANY)
    block = jax.ShapeDtypeStruct((MAX_PAGES,) + page, pool.dtype)
    outs = [jax.ShapeDtypeStruct((groups * MAX_PAGES,) + page, pool.dtype)] * own + [block] * len(routes)
    operands = [table, pool, *after]
    return pl.pallas_call(
        functools.partial(prepare_kernel, dims, routes, own),
        out_shape=outs,
        in_specs=[hbm] * len(operands),
        out_specs=[hbm] * len(outs),
        scratch_shapes=[
            pltpu.SMEM(table.shape, jnp.int32),
            pltpu.VMEM((blocks, MAX_PAGES) + page, pool.dtype),
            pltpu.VMEM(page, pool.dtype),
            pltpu.SMEM((groups + 1,), jnp.int32),
            pltpu.SMEM((groups + 1,), jnp.int32),
            pltpu.SemaphoreType.DMA,
            pltpu.SemaphoreType.DMA((blocks, MAX_PAGES)),
            pltpu.SemaphoreType.DMA,
        ],
        compiler_params=pltpu.CompilerParams(vmem_limit_bytes=VMEM_LIMIT),
        cost_estimate=pl.CostEstimate(
            flops=0, bytes_accessed=4 * blocks * MAX_PAGES * math.prod(page), transcendentals=0
        ),
        name="outgoing_pages",
    )(*operands)


def attend_row(query, pages, length):
    first, second = pages
    kv_heads = first.shape[1] // (2 * HD)
    share = query.shape[0] // kv_heads
    scores = []
    for h in range(kv_heads):
        columns = slice(2 * h * HD, (2 * h + 1) * HD)
        keys = jnp.concatenate([first[:, columns], second[:, columns]], axis=0)
        every = lax.dot_general(
            query, keys, (((1,), (1,)), ((), ())), preferred_element_type=jnp.float32
        )
        scores.append(every[h * share : (h + 1) * share])
    score = jnp.concatenate(scores, axis=0) * (1.0 / math.sqrt(HD))
    live = lax.broadcasted_iota(jnp.int32, score.shape, 1) < length
    masked = jnp.where(live, score, -1e30)
    highest = jnp.max(masked, axis=1, keepdims=True)
    weights = jnp.where(live, jnp.exp(masked - highest), 0.0)
    totals = jnp.sum(weights, axis=1, keepdims=True)
    rounded = weights.astype(jnp.bfloat16)
    mixtures = []
    for h in range(kv_heads):
        columns = slice((2 * h + 1) * HD, (2 * h + 2) * HD)
        values = jnp.concatenate([first[:, columns], second[:, columns]], axis=0)
        every = jnp.dot(rounded, values, preferred_element_type=jnp.float32)
        mixtures.append(every[h * share : (h + 1) * share])
    return jnp.concatenate(mixtures, axis=0) / totals


def settle_kernel(dims, routes, own, last, table, row_request, queries, rows_in, received_in, *rest):
    blocks = rest[: len(routes)]
    received, out, rows, held, list_row, list_block, list_length, in_sems, out_sems = rest[len(routes) :]
    me = lax.axis_index("group")
    row_local, query_heads, _ = queries.shape
    mine = pl.ds(me * MAX_PAGES, MAX_PAGES)
    origins = [routed(me, reverse(route), dims) for route in routes]
    places = [pl.ds(origin * MAX_PAGES, MAX_PAGES) for origin in origins]
    sources = list(blocks) + ([received_in.at[mine]] if own else [])
    origins += [me] if own else []
    loads = [pltpu.make_async_copy(s, held.at[i], in_sems.at[i]) for i, s in enumerate(sources)]
    stores = [
        pltpu.make_async_copy(held.at[i], received.at[place], out_sems.at[i]) for i, place in enumerate(places)
    ]
    for load in loads:
        load.start()

    found = jnp.int32(0)
    for b in range(row_local):
        length, home, _ = unpacked(table[row_request[me * row_local + b]], math.prod(dims))
        block, match = jnp.int32(0), jnp.int32(0)
        for i, origin in enumerate(origins):
            block = jnp.where(home == origin, i, block)
            match = jnp.where(home == origin, 1, match)
        list_row[found] = b
        list_block[found] = block
        list_length[found] = length
        found = found + match
    for i in range(ROW_UNROLL):
        list_row[found + i] = row_local
        list_block[found + i] = 0
        list_length[found + i] = 1
    rows[:row_local] = rows_in[...]
    for load in loads:
        load.wait()
    for store in stores:
        store.start()

    @pl.loop(0, (found + ROW_UNROLL - 1) // ROW_UNROLL)
    def _(step):
        results = []
        for i in range(ROW_UNROLL):
            at = step * ROW_UNROLL + i
            query = queries[jnp.minimum(list_row[at], row_local - 1)]
            pages = [held[list_block[at], page] for page in range(MAX_PAGES)]
            results.append(attend_row(query, pages, list_length[at]))
        for i, result in enumerate(results):
            rows[list_row[step * ROW_UNROLL + i]] = result

    if last:
        for h in range(query_heads):
            out[:, h * HD : (h + 1) * HD] = rows[:row_local, h, :].astype(out.dtype)
    else:
        out[...] = rows[:row_local]
    for store in stores:
        store.wait()


def settle(dims, routes, own, last, table, row_request, queries, rows, received, blocks):
    row_local, query_heads, _ = queries.shape
    smem = pl.BlockSpec(memory_space=pltpu.SMEM)
    vmem = pl.BlockSpec(memory_space=pltpu.VMEM)
    hbm = pl.BlockSpec(memory_space=pl.ANY)
    count = len(blocks) + (1 if own else 0)
    if last:
        out = jax.ShapeDtypeStruct((row_local, query_heads * HD), jnp.bfloat16)
    else:
        out = jax.ShapeDtypeStruct(rows.shape, rows.dtype)
    return pl.pallas_call(
        functools.partial(settle_kernel, dims, routes, own, last),
        out_shape=[jax.ShapeDtypeStruct(received.shape, received.dtype), out],
        in_specs=[smem, smem, vmem, vmem, hbm] + [hbm] * len(blocks),
        out_specs=[hbm, vmem],
        scratch_shapes=[
            pltpu.VMEM((row_local + 1, query_heads, HD), jnp.float32),
            pltpu.VMEM((count, MAX_PAGES) + received.shape[1:], received.dtype),
            pltpu.SMEM((row_local + ROW_UNROLL,), jnp.int32),
            pltpu.SMEM((row_local + ROW_UNROLL,), jnp.int32),
            pltpu.SMEM((row_local + ROW_UNROLL,), jnp.int32),
            pltpu.SemaphoreType.DMA((count,)),
            pltpu.SemaphoreType.DMA((count,)),
        ],
        input_output_aliases={4: 0},
        compiler_params=pltpu.CompilerParams(vmem_limit_bytes=VMEM_LIMIT),
        cost_estimate=pl.CostEstimate(
            flops=1 << 30, bytes_accessed=4 * sum(b.size for b in blocks), transcendentals=1 << 18
        ),
        name="settle_pages",
    )(table, row_request, queries, rows, received, *blocks)


def multiply_rows(shards, out_weight, attended, sems):
    copies = []
    row_local = shards[0].shape[0]
    for i, shard in enumerate(shards):
        copies.append(pltpu.make_async_copy(shard, attended.at[pl.ds(i * row_local, row_local)], sems.at[i]))
        copies[-1].start()
    for copy in copies:
        copy.wait()
    return jnp.dot(attended[...], out_weight[...], preferred_element_type=jnp.float32)


def project_some_kernel(count, out_weight, *rest):
    out, attended, sems = rest[count:]
    out[...] = multiply_rows(rest[:count], out_weight, attended, sems)


def project_rest_kernel(masks, count, out_weight, some, *rest):
    own, *theirs = rest[count:-3]
    attended, product, sems = rest[-3:]
    me = lax.axis_index("group")
    heads = lax.axis_size("head")
    my_head = lax.axis_index("head")
    row_local = rest[0].shape[0]
    share = own.shape[0]
    product[...] = multiply_rows(rest[:count], out_weight, attended, sems)
    for i, mask in enumerate(masks):
        done = len(masks) - count
        part = some if i < done else product
        at = i if i < done else i - done
        values = part[at * row_local : (at + 1) * row_local]
        row = (me ^ mask) * row_local
        ahead = lax.rem(row // share - my_head + heads, heads)
        place = pl.ds(pl.multiple_of(lax.rem(row, share), row_local), row_local)
        for k, out in enumerate([own, *theirs]):

            @pl.when(ahead == k)
            def _():
                out[place] = values.astype(out.dtype)


def project(gathered, out_weight, heads):
    masks = [mask for mask in gathered if mask % 2 == 0] + [mask for mask in gathered if mask % 2]
    some = len(masks) // 2
    row_local, width = gathered[0].shape
    columns = out_weight.shape[1]
    share = row_local * len(masks) // heads
    vmem = pl.BlockSpec(memory_space=pltpu.VMEM)
    hbm = pl.BlockSpec(memory_space=pl.ANY)

    def call(kernel, name, outs, blocks, extra, scratch):
        rows = row_local * len(blocks)
        return pl.pallas_call(
            kernel,
            out_shape=outs,
            in_specs=[vmem] * (1 + len(extra)) + [hbm] * len(blocks),
            out_specs=[vmem] * len(outs),
            scratch_shapes=[
                pltpu.VMEM((rows, width), jnp.bfloat16),
                *scratch,
                pltpu.SemaphoreType.DMA((len(blocks),)),
            ],
            compiler_params=pltpu.CompilerParams(vmem_limit_bytes=VMEM_LIMIT),
            cost_estimate=pl.CostEstimate(
                flops=2 * rows * width * columns, bytes_accessed=2 * out_weight.size, transcendentals=0
            ),
            name=name,
        )(out_weight, *extra, *blocks)

    out_weight = pltpu.with_memory_space_constraint(out_weight, pltpu.VMEM)
    first = [gathered[mask] for mask in masks[:some]]
    last = [gathered[mask] for mask in masks[some:]]
    (done,) = call(
        functools.partial(project_some_kernel, some), "project_some_rows",
        [jax.ShapeDtypeStruct((some * row_local, columns), jnp.float32)], first, [], [],
    )
    theirs = jax.ShapeDtypeStruct((share, columns), jnp.bfloat16)
    return call(
        functools.partial(project_rest_kernel, masks, len(last)), "project_rows",
        [jax.ShapeDtypeStruct((share, columns), jnp.float32)] + [theirs] * (heads - 1), last, [done],
        [pltpu.VMEM((len(last) * row_local, columns), jnp.float32)],
    )


def local(kv_pool, lengths, prefill_of, decode_of, row_request, queries, out_weight):
    row_local, query_width = queries.shape
    query_heads = queries.reshape(row_local, query_width // HD, HD)
    heads = lax.axis_size("head")

    dims = factors(lax.axis_size("group"))
    routes = page_rounds(dims)
    table = packed(lengths, prefill_of, decode_of, math.prod(dims))
    kv_pool = pltpu.with_memory_space_constraint(kv_pool, pltpu.HBM)
    early = prepare(dims, routes[:EARLY], table, kv_pool, False)
    received, *late = prepare(dims, routes[EARLY:], table, kv_pool, True, early[:1])
    arrived = [send_by(block, route, dims) for block, route in zip([*early, *late], routes)]
    rows = jnp.zeros(query_heads.shape, jnp.float32)
    for first in range(0, len(routes), WAVE):
        wave = slice(first, first + WAVE)
        last = first + WAVE >= len(routes)
        received, rows = settle(
            dims, routes[wave], first == 0, last, table, row_request, query_heads, rows, received, arrived[wave]
        )

    own, *theirs = project(gather_shards(rows), out_weight, heads)
    for ahead_by, part in enumerate(theirs, 1):
        pairs = [(h, (h + ahead_by) % heads) for h in range(heads)]
        own = own + lax.ppermute(part, "head", pairs).astype(jnp.float32)
    return (received, own.astype(jnp.bfloat16))


def solution(mesh):
    in_specs = (
        P("group", None, "head"),
        P(),
        P(),
        P(),
        P(),
        P("group", "head"),
        P("head", "group"),
    )
    assert mesh.shape["group"] & (mesh.shape["group"] - 1) == 0
    out_specs = (P("group", None, "head"), P("head", "group"))
    return jax.shard_map(local, mesh=mesh, in_specs=in_specs, out_specs=out_specs, check_vma=False)
```

```python
import functools
import math

import jax
import jax.numpy as jnp
from jax import lax
from jax.experimental import pallas as pl
from jax.experimental.pallas import tpu as pltpu
from jax.sharding import PartitionSpec as P

HD = 128
MAX_PAGES = 2
WAVE = 3
ROW_UNROLL = 4
EARLY = 2
VMEM_LIMIT = 20 * 1024 * 1024


def factors(groups):
    near = math.gcd(groups, 4)
    return groups // near, near


def uniform(step, swap, dims):
    return tuple(((z + step) % dims[0], swap) for z in range(dims[0]))


def page_rounds(dims):
    far, near = dims
    half = max(near // 2, 1)
    order = []
    for low in range(0, near, half):
        swaps = range(low, min(low + half, near))
        steps = [z if low == 0 else far - z for z in range(1, far)]
        opening = [(steps[0], n) for n in swaps] + [(0, n) for n in swaps if n]
        if low:
            opening = [(z, n) for n in swaps for z in (steps[0], 0)]
        order += opening + [(z, n) for n in swaps for z in steps[1:]]
    return [uniform(z, n, dims) for z, n in order]


def reverse(route):
    sources = {to: (z, swap) for z, (to, swap) in enumerate(route)}
    return tuple(sources[z] for z in range(len(route)))


def routed(me, route, dims):
    near = dims[1]
    z = me // near
    to, swap = jnp.int32(route[0][0]), jnp.int32(route[0][1])
    for place in range(1, dims[0]):
        to = jnp.where(z == place, route[place][0], to)
        swap = jnp.where(z == place, route[place][1], swap)
    return to * near + (me % near ^ swap)


def send_by(array, route, dims):
    far, near = dims
    pairs = [
        (z * near + n, route[z][0] * near + (n ^ route[z][1])) for z in range(far) for n in range(near)
    ]
    return lax.ppermute(array, "group", pairs)


def swap(array, mask):
    groups = lax.axis_size("group")
    return lax.ppermute(array, "group", [(s, s ^ mask) for s in range(groups)])


def tied(array, after):
    return lax.optimization_barrier((array, after))[0]


def gather_shards(shard):
    groups = lax.axis_size("group")
    across, halves = swap(shard, groups // 2), []
    for start in (0, groups // 2):
        held, mask = {start: across if start else shard}, groups // 4
        while mask > 1:
            held.update({done | mask: swap(array, mask) for done, array in held.items()})
            mask //= 2
        halves.append(held)
        across = tied(across, held[max(held)])
    held = halves[0] | halves[1]
    return held | {done | 1: swap(array, 1) for done, array in held.items()}


def packed(lengths, prefill_of, decode_of, groups):
    bits = (groups - 1).bit_length()
    return (lengths << 2 * bits) | (prefill_of << bits) | decode_of


def unpacked(entry, groups):
    bits = (groups - 1).bit_length()
    mask = (1 << bits) - 1
    return entry >> 2 * bits, (entry >> bits) & mask, entry & mask


def prepare_kernel(dims, routes, own, table_hbm, pool, *rest):
    table, held, zero_page, start_of, count_of, table_sem, in_sems, out_sem = rest[-8:]
    received = rest[-8 - len(routes) - own : -8 - len(routes)]
    sends = rest[-8 - len(routes) : -8]
    me = lax.axis_index("group")
    groups = lax.axis_size("group")
    page_size = pool.shape[1]
    copy = pltpu.make_async_copy(table_hbm, table, table_sem)
    copy.start()
    for d in range(groups + 1):
        start_of[d] = 0
        count_of[d] = 0
    zero_page[...] = jnp.zeros_like(zero_page)
    copy.wait()

    def visit(r, running):
        length, home, destination = unpacked(table[r], groups)
        mine = home == me
        count = (length + page_size - 1) // page_size
        to = jnp.where(mine, destination, groups)
        start_of[to] = running
        count_of[to] = count
        return running + jnp.where(mine, count, 0)

    lax.fori_loop(0, table.shape[0], visit, jnp.int32(0), unroll=8)
    targets = [(routed(me, route, dims), send, 0) for route, send in zip(routes, sends)]
    if own:
        targets.append((me, received[0], me * MAX_PAGES))

    def each(do):
        for i, (to, target, base) in enumerate(targets):
            for page in range(MAX_PAGES):
                there = page < count_of[to]
                source = pool.at[jnp.where(there, start_of[to] + page, 0)]
                buffer, place = held.at[i, page], target.at[base + page]
                do(there, (source, buffer, in_sems.at[i, page]), (buffer, place, out_sem), (zero_page, place, out_sem))

    def fetch(there, load, store, blank):
        @pl.when(there)
        def _():
            pltpu.make_async_copy(*load).start()

        @pl.when(jnp.logical_not(there))
        def _():
            pltpu.make_async_copy(*blank).start()

    def forward(there, load, store, blank):
        @pl.when(there)
        def _():
            pltpu.make_async_copy(*load).wait()
            pltpu.make_async_copy(*store).start()

    def finish(there, load, store, blank):
        pltpu.make_async_copy(*blank).wait()

    each(fetch)
    each(forward)
    each(finish)


def prepare(dims, routes, table, pool, own, after=()):
    groups = lax.axis_size("group")
    page = pool.shape[1:]
    blocks = len(routes) + (1 if own else 0)
    hbm = pl.BlockSpec(memory_space=pl.ANY)
    block = jax.ShapeDtypeStruct((MAX_PAGES,) + page, pool.dtype)
    outs = [jax.ShapeDtypeStruct((groups * MAX_PAGES,) + page, pool.dtype)] * own + [block] * len(routes)
    operands = [table, pool, *after]
    return pl.pallas_call(
        functools.partial(prepare_kernel, dims, routes, own),
        out_shape=outs,
        in_specs=[hbm] * len(operands),
        out_specs=[hbm] * len(outs),
        scratch_shapes=[
            pltpu.SMEM(table.shape, jnp.int32),
            pltpu.VMEM((blocks, MAX_PAGES) + page, pool.dtype),
            pltpu.VMEM(page, pool.dtype),
            pltpu.SMEM((groups + 1,), jnp.int32),
            pltpu.SMEM((groups + 1,), jnp.int32),
            pltpu.SemaphoreType.DMA,
            pltpu.SemaphoreType.DMA((blocks, MAX_PAGES)),
            pltpu.SemaphoreType.DMA,
        ],
        compiler_params=pltpu.CompilerParams(vmem_limit_bytes=VMEM_LIMIT),
        cost_estimate=pl.CostEstimate(
            flops=0, bytes_accessed=4 * blocks * MAX_PAGES * math.prod(page), transcendentals=0
        ),
        name="outgoing_pages",
    )(*operands)


def attend_row(query, pages, length):
    first, second = pages
    kv_heads = first.shape[1] // (2 * HD)
    share = query.shape[0] // kv_heads
    scores = []
    for h in range(kv_heads):
        columns = slice(2 * h * HD, (2 * h + 1) * HD)
        keys = jnp.concatenate([first[:, columns], second[:, columns]], axis=0)
        every = lax.dot_general(
            query, keys, (((1,), (1,)), ((), ())), preferred_element_type=jnp.float32
        )
        scores.append(every[h * share : (h + 1) * share])
    score = jnp.concatenate(scores, axis=0) * (1.0 / math.sqrt(HD))
    live = lax.broadcasted_iota(jnp.int32, score.shape, 1) < length
    masked = jnp.where(live, score, -1e30)
    highest = jnp.max(masked, axis=1, keepdims=True)
    weights = jnp.where(live, jnp.exp(masked - highest), 0.0)
    totals = jnp.sum(weights, axis=1, keepdims=True)
    rounded = weights.astype(jnp.bfloat16)
    mixtures = []
    for h in range(kv_heads):
        columns = slice((2 * h + 1) * HD, (2 * h + 2) * HD)
        values = jnp.concatenate([first[:, columns], second[:, columns]], axis=0)
        every = jnp.dot(rounded, values, preferred_element_type=jnp.float32)
        mixtures.append(every[h * share : (h + 1) * share])
    return jnp.concatenate(mixtures, axis=0) / totals


def settle_kernel(dims, routes, own, last, table, row_request, queries, rows_in, received_in, *rest):
    blocks = rest[: len(routes)]
    received, out, rows, held, list_row, list_block, list_length, in_sems, out_sems = rest[len(routes) :]
    me = lax.axis_index("group")
    row_local, query_heads, _ = queries.shape
    mine = pl.ds(me * MAX_PAGES, MAX_PAGES)
    origins = [routed(me, reverse(route), dims) for route in routes]
    places = [pl.ds(origin * MAX_PAGES, MAX_PAGES) for origin in origins]
    sources = list(blocks) + ([received_in.at[mine]] if own else [])
    origins += [me] if own else []
    loads = [pltpu.make_async_copy(s, held.at[i], in_sems.at[i]) for i, s in enumerate(sources)]
    stores = [
        pltpu.make_async_copy(held.at[i], received.at[place], out_sems.at[i]) for i, place in enumerate(places)
    ]
    for load in loads:
        load.start()

    found = jnp.int32(0)
    for b in range(row_local):
        length, home, _ = unpacked(table[row_request[me * row_local + b]], math.prod(dims))
        block, match = jnp.int32(0), jnp.int32(0)
        for i, origin in enumerate(origins):
            block = jnp.where(home == origin, i, block)
            match = jnp.where(home == origin, 1, match)
        list_row[found] = b
        list_block[found] = block
        list_length[found] = length
        found = found + match
    for i in range(ROW_UNROLL):
        list_row[found + i] = row_local
        list_block[found + i] = 0
        list_length[found + i] = 1
    rows[:row_local] = rows_in[...]
    for load in loads:
        load.wait()
    for store in stores:
        store.start()

    @pl.loop(0, (found + ROW_UNROLL - 1) // ROW_UNROLL)
    def _(step):
        results = []
        for i in range(ROW_UNROLL):
            at = step * ROW_UNROLL + i
            query = queries[jnp.minimum(list_row[at], row_local - 1)]
            pages = [held[list_block[at], page] for page in range(MAX_PAGES)]
            results.append(attend_row(query, pages, list_length[at]))
        for i, result in enumerate(results):
            rows[list_row[step * ROW_UNROLL + i]] = result

    if last:
        for h in range(query_heads):
            out[:, h * HD : (h + 1) * HD] = rows[:row_local, h, :].astype(out.dtype)
    else:
        out[...] = rows[:row_local]
    for store in stores:
        store.wait()


def settle(dims, routes, own, last, table, row_request, queries, rows, received, blocks):
    row_local, query_heads, _ = queries.shape
    smem = pl.BlockSpec(memory_space=pltpu.SMEM)
    vmem = pl.BlockSpec(memory_space=pltpu.VMEM)
    hbm = pl.BlockSpec(memory_space=pl.ANY)
    count = len(blocks) + (1 if own else 0)
    if last:
        out = jax.ShapeDtypeStruct((row_local, query_heads * HD), jnp.bfloat16)
    else:
        out = jax.ShapeDtypeStruct(rows.shape, rows.dtype)
    return pl.pallas_call(
        functools.partial(settle_kernel, dims, routes, own, last),
        out_shape=[jax.ShapeDtypeStruct(received.shape, received.dtype), out],
        in_specs=[smem, smem, vmem, vmem, hbm] + [hbm] * len(blocks),
        out_specs=[hbm, vmem],
        scratch_shapes=[
            pltpu.VMEM((row_local + 1, query_heads, HD), jnp.float32),
            pltpu.VMEM((count, MAX_PAGES) + received.shape[1:], received.dtype),
            pltpu.SMEM((row_local + ROW_UNROLL,), jnp.int32),
            pltpu.SMEM((row_local + ROW_UNROLL,), jnp.int32),
            pltpu.SMEM((row_local + ROW_UNROLL,), jnp.int32),
            pltpu.SemaphoreType.DMA((count,)),
            pltpu.SemaphoreType.DMA((count,)),
        ],
        input_output_aliases={4: 0},
        compiler_params=pltpu.CompilerParams(vmem_limit_bytes=VMEM_LIMIT),
        cost_estimate=pl.CostEstimate(
            flops=1 << 30, bytes_accessed=4 * sum(b.size for b in blocks), transcendentals=1 << 18
        ),
        name="settle_pages",
    )(table, row_request, queries, rows, received, *blocks)


def multiply_rows(shards, out_weight, attended, sems):
    copies = []
    row_local = shards[0].shape[0]
    for i, shard in enumerate(shards):
        copies.append(pltpu.make_async_copy(shard, attended.at[pl.ds(i * row_local, row_local)], sems.at[i]))
        copies[-1].start()
    for copy in copies:
        copy.wait()
    return jnp.dot(attended[...], out_weight[...], preferred_element_type=jnp.float32)


def project_some_kernel(count, out_weight, *rest):
    out, attended, sems = rest[count:]
    out[...] = multiply_rows(rest[:count], out_weight, attended, sems)


def project_rest_kernel(masks, count, out_weight, some, *rest):
    own, *theirs = rest[count:-3]
    attended, product, sems = rest[-3:]
    me = lax.axis_index("group")
    heads = lax.axis_size("head")
    my_head = lax.axis_index("head")
    row_local = rest[0].shape[0]
    share = own.shape[0]
    product[...] = multiply_rows(rest[:count], out_weight, attended, sems)
    for i, mask in enumerate(masks):
        done = len(masks) - count
        part = some if i < done else product
        at = i if i < done else i - done
        values = part[at * row_local : (at + 1) * row_local]
        row = (me ^ mask) * row_local
        ahead = lax.rem(row // share - my_head + heads, heads)
        place = pl.ds(pl.multiple_of(lax.rem(row, share), row_local), row_local)
        for k, out in enumerate([own, *theirs]):

            @pl.when(ahead == k)
            def _():
                out[place] = values.astype(out.dtype)


def project(gathered, out_weight, heads):
    masks = [mask for mask in gathered if mask % 2 == 0] + [mask for mask in gathered if mask % 2]
    some = len(masks) // 2
    row_local, width = gathered[0].shape
    columns = out_weight.shape[1]
    share = row_local * len(masks) // heads
    vmem = pl.BlockSpec(memory_space=pltpu.VMEM)
    hbm = pl.BlockSpec(memory_space=pl.ANY)

    def call(kernel, name, outs, blocks, extra, scratch):
        rows = row_local * len(blocks)
        return pl.pallas_call(
            kernel,
            out_shape=outs,
            in_specs=[vmem] * (1 + len(extra)) + [hbm] * len(blocks),
            out_specs=[vmem] * len(outs),
            scratch_shapes=[
                pltpu.VMEM((rows, width), jnp.bfloat16),
                *scratch,
                pltpu.SemaphoreType.DMA((len(blocks),)),
            ],
            compiler_params=pltpu.CompilerParams(vmem_limit_bytes=VMEM_LIMIT),
            cost_estimate=pl.CostEstimate(
                flops=2 * rows * width * columns, bytes_accessed=2 * out_weight.size, transcendentals=0
            ),
            name=name,
        )(out_weight, *extra, *blocks)

    out_weight = pltpu.with_memory_space_constraint(out_weight, pltpu.VMEM)
    first = [gathered[mask] for mask in masks[:some]]
    last = [gathered[mask] for mask in masks[some:]]
    (done,) = call(
        functools.partial(project_some_kernel, some), "project_some_rows",
        [jax.ShapeDtypeStruct((some * row_local, columns), jnp.float32)], first, [], [],
    )
    theirs = jax.ShapeDtypeStruct((share, columns), jnp.bfloat16)
    return call(
        functools.partial(project_rest_kernel, masks, len(last)), "project_rows",
        [jax.ShapeDtypeStruct((share, columns), jnp.float32)] + [theirs] * (heads - 1), last, [done],
        [pltpu.VMEM((len(last) * row_local, columns), jnp.float32)],
    )


def local(kv_pool, lengths, prefill_of, decode_of, row_request, queries, out_weight):
    row_local, query_width = queries.shape
    query_heads = queries.reshape(row_local, query_width // HD, HD)
    heads = lax.axis_size("head")

    dims = factors(lax.axis_size("group"))
    routes = page_rounds(dims)
    table = packed(lengths, prefill_of, decode_of, math.prod(dims))
    kv_pool = pltpu.with_memory_space_constraint(kv_pool, pltpu.HBM)
    early = prepare(dims, routes[:EARLY], table, kv_pool, False)
    received, *late = prepare(dims, routes[EARLY:], table, kv_pool, True, early[:1])
    arrived = [send_by(block, route, dims) for block, route in zip([*early, *late], routes)]
    rows = jnp.zeros(query_heads.shape, jnp.float32)
    for first in range(0, len(routes), WAVE):
        wave = slice(first, first + WAVE)
        last = first + WAVE >= len(routes)
        received, rows = settle(
            dims, routes[wave], first == 0, last, table, row_request, query_heads, rows, received, arrived[wave]
        )

    own, *theirs = project(gather_shards(rows), out_weight, heads)
    for ahead_by, part in enumerate(theirs, 1):
        pairs = [(h, (h + ahead_by) % heads) for h in range(heads)]
        own = own + lax.ppermute(part, "head", pairs).astype(jnp.float32)
    return (received, own.astype(jnp.bfloat16))


def solution(mesh):
    in_specs = (
        P("group", None, "head"),
        P(),
        P(),
        P(),
        P(),
        P("group", "head"),
        P("head", "group"),
    )
    assert mesh.shape["group"] & (mesh.shape["group"] - 1) == 0
    out_specs = (P("group", None, "head"), P("head", "group"))
    return jax.shard_map(local, mesh=mesh, in_specs=in_specs, out_specs=out_specs, check_vma=False)
```

```python
import functools
import math

import jax
import jax.numpy as jnp
from jax import lax
from jax.experimental import pallas as pl
from jax.experimental.pallas import tpu as pltpu
from jax.sharding import PartitionSpec as P

HD = 128
MAX_PAGES = 2
WAVE = 3
ROW_UNROLL = 4
EARLY = 2
VMEM_LIMIT = 20 * 1024 * 1024


def factors(groups):
    near = math.gcd(groups, 4)
    return groups // near, near


def uniform(step, swap, dims):
    return tuple(((z + step) % dims[0], swap) for z in range(dims[0]))


def page_rounds(dims):
    far, near = dims
    half = max(near // 2, 1)
    same, other = range(half), range(half, near)
    if far == 4:
        rounds = [((2, n), (0, n), (3, n), (1, n)) for n in same]
        rounds += [((3, n), (1, n), (2, n), (0, n)) for n in same if n]
        rounds += [((3, 0), (2, 0), (1, 0), (0, 0))]
        rounds += [((0, n), (2, n), (1, n), (3, n)) for n in same if n]
        rounds += [((1, n), (3, n), (0, n), (2, n)) for n in same]
    else:
        rounds = [uniform(z, n, dims) for z in range(far) for n in same if z or n]
    rounds += [uniform(z, n, dims) for n in other for z in (1, 0)]
    return rounds + [uniform(z, n, dims) for n in other for z in range(2, far)]


def reverse(route):
    sources = {to: (z, swap) for z, (to, swap) in enumerate(route)}
    return tuple(sources[z] for z in range(len(route)))


def routed(me, route, dims):
    near = dims[1]
    z = me // near
    to, swap = jnp.int32(route[0][0]), jnp.int32(route[0][1])
    for place in range(1, dims[0]):
        to = jnp.where(z == place, route[place][0], to)
        swap = jnp.where(z == place, route[place][1], swap)
    return to * near + (me % near ^ swap)


def send_by(array, route, dims):
    far, near = dims
    pairs = [
        (z * near + n, route[z][0] * near + (n ^ route[z][1])) for z in range(far) for n in range(near)
    ]
    return lax.ppermute(array, "group", pairs)


def swap(array, mask):
    groups = lax.axis_size("group")
    return lax.ppermute(array, "group", [(s, s ^ mask) for s in range(groups)])


def gather_shards(shard):
    held = {0: shard}
    mask = lax.axis_size("group") // 2
    while mask:
        held.update({done | mask: swap(array, mask) for done, array in held.items()})
        mask //= 2
    return held


def packed(lengths, prefill_of, decode_of, groups):
    bits = (groups - 1).bit_length()
    return (lengths << 2 * bits) | (prefill_of << bits) | decode_of


def unpacked(entry, groups):
    bits = (groups - 1).bit_length()
    mask = (1 << bits) - 1
    return entry >> 2 * bits, (entry >> bits) & mask, entry & mask


def prepare_kernel(dims, routes, own, table_hbm, pool, *rest):
    table, held, zero_page, start_of, count_of, table_sem, in_sems, out_sems = rest[-8:]
    received = rest[-8 - len(routes) - own : -8 - len(routes)]
    sends = rest[-8 - len(routes) : -8]
    me = lax.axis_index("group")
    groups = lax.axis_size("group")
    page_size = pool.shape[1]
    copy = pltpu.make_async_copy(table_hbm, table, table_sem)
    copy.start()
    for d in range(groups + 1):
        start_of[d] = 0
        count_of[d] = 0
    zero_page[...] = jnp.zeros_like(zero_page)
    copy.wait()

    def visit(r, running):
        length, home, destination = unpacked(table[r], groups)
        mine = home == me
        count = (length + page_size - 1) // page_size
        to = jnp.where(mine, destination, groups)
        start_of[to] = running
        count_of[to] = count
        return running + jnp.where(mine, count, 0)

    lax.fori_loop(0, table.shape[0], visit, jnp.int32(0), unroll=8)
    targets = [(routed(me, route, dims), send, 0) for route, send in zip(routes, sends)]
    if own:
        targets.append((me, received[0], me * MAX_PAGES))

    def each(do):
        for i, (to, target, base) in enumerate(targets):
            for page in range(MAX_PAGES):
                there = page < count_of[to]
                source = pool.at[jnp.where(there, start_of[to] + page, 0)]
                buffer, place = held.at[i, page], target.at[base + page]
                sem = out_sems.at[i, page]
                do(there, (source, buffer, in_sems.at[i, page]), (buffer, place, sem), (zero_page, place, sem))

    def fetch(there, load, store, blank):
        @pl.when(there)
        def _():
            pltpu.make_async_copy(*load).start()

        @pl.when(jnp.logical_not(there))
        def _():
            pltpu.make_async_copy(*blank).start()

    def forward(there, load, store, blank):
        @pl.when(there)
        def _():
            pltpu.make_async_copy(*load).wait()
            pltpu.make_async_copy(*store).start()

    def finish(there, load, store, blank):
        pltpu.make_async_copy(*blank).wait()

    each(fetch)
    each(forward)
    each(finish)


def prepare(dims, routes, table, pool, own, after=()):
    groups = lax.axis_size("group")
    page = pool.shape[1:]
    blocks = len(routes) + (1 if own else 0)
    hbm = pl.BlockSpec(memory_space=pl.ANY)
    block = jax.ShapeDtypeStruct((MAX_PAGES,) + page, pool.dtype)
    outs = [jax.ShapeDtypeStruct((groups * MAX_PAGES,) + page, pool.dtype)] * own + [block] * len(routes)
    operands = [table, pool, *after]
    return pl.pallas_call(
        functools.partial(prepare_kernel, dims, routes, own),
        out_shape=outs,
        in_specs=[hbm] * len(operands),
        out_specs=[hbm] * len(outs),
        scratch_shapes=[
            pltpu.SMEM(table.shape, jnp.int32),
            pltpu.VMEM((blocks, MAX_PAGES) + page, pool.dtype),
            pltpu.VMEM(page, pool.dtype),
            pltpu.SMEM((groups + 1,), jnp.int32),
            pltpu.SMEM((groups + 1,), jnp.int32),
            pltpu.SemaphoreType.DMA,
            pltpu.SemaphoreType.DMA((blocks, MAX_PAGES)),
            pltpu.SemaphoreType.DMA((blocks, MAX_PAGES)),
        ],
        compiler_params=pltpu.CompilerParams(vmem_limit_bytes=VMEM_LIMIT),
        cost_estimate=pl.CostEstimate(
            flops=0, bytes_accessed=4 * blocks * MAX_PAGES * math.prod(page), transcendentals=0
        ),
        name="outgoing_pages",
    )(*operands)


def attend_row(query, pages, length):
    first, second = pages
    kv_heads = first.shape[1] // (2 * HD)
    share = query.shape[0] // kv_heads
    scores = []
    for h in range(kv_heads):
        columns = slice(2 * h * HD, (2 * h + 1) * HD)
        keys = jnp.concatenate([first[:, columns], second[:, columns]], axis=0)
        every = lax.dot_general(
            query, keys, (((1,), (1,)), ((), ())), preferred_element_type=jnp.float32
        )
        scores.append(every[h * share : (h + 1) * share])
    score = jnp.concatenate(scores, axis=0) * (1.0 / math.sqrt(HD))
    live = lax.broadcasted_iota(jnp.int32, score.shape, 1) < length
    masked = jnp.where(live, score, -1e30)
    highest = jnp.max(masked, axis=1, keepdims=True)
    weights = jnp.where(live, jnp.exp(masked - highest), 0.0)
    totals = jnp.sum(weights, axis=1, keepdims=True)
    rounded = weights.astype(jnp.bfloat16)
    mixtures = []
    for h in range(kv_heads):
        columns = slice((2 * h + 1) * HD, (2 * h + 2) * HD)
        values = jnp.concatenate([first[:, columns], second[:, columns]], axis=0)
        every = jnp.dot(rounded, values, preferred_element_type=jnp.float32)
        mixtures.append(every[h * share : (h + 1) * share])
    return jnp.concatenate(mixtures, axis=0) / totals


def settle_kernel(dims, routes, own, last, table, row_request, queries, rows_in, received_in, *rest):
    blocks = rest[: len(routes)]
    received, out, rows, held, list_row, list_block, list_length, in_sems, out_sems = rest[len(routes) :]
    me = lax.axis_index("group")
    row_local, query_heads, _ = queries.shape
    mine = pl.ds(me * MAX_PAGES, MAX_PAGES)
    origins = [routed(me, reverse(route), dims) for route in routes]
    places = [pl.ds(origin * MAX_PAGES, MAX_PAGES) for origin in origins]
    sources = list(blocks) + ([received_in.at[mine]] if own else [])
    origins += [me] if own else []
    loads = [pltpu.make_async_copy(s, held.at[i], in_sems.at[i]) for i, s in enumerate(sources)]
    stores = [
        pltpu.make_async_copy(held.at[i], received.at[place], out_sems.at[i]) for i, place in enumerate(places)
    ]
    for load in loads:
        load.start()

    found = jnp.int32(0)
    for b in range(row_local):
        length, home, _ = unpacked(table[row_request[me * row_local + b]], math.prod(dims))
        block, match = jnp.int32(0), jnp.int32(0)
        for i, origin in enumerate(origins):
            block = jnp.where(home == origin, i, block)
            match = jnp.where(home == origin, 1, match)
        list_row[found] = b
        list_block[found] = block
        list_length[found] = length
        found = found + match
    for i in range(ROW_UNROLL):
        list_row[found + i] = row_local
        list_block[found + i] = 0
        list_length[found + i] = 1
    rows[:row_local] = rows_in[...]
    for load in loads:
        load.wait()
    for store in stores:
        store.start()

    @pl.loop(0, (found + ROW_UNROLL - 1) // ROW_UNROLL)
    def _(step):
        results = []
        for i in range(ROW_UNROLL):
            at = step * ROW_UNROLL + i
            query = queries[jnp.minimum(list_row[at], row_local - 1)]
            pages = [held[list_block[at], page] for page in range(MAX_PAGES)]
            results.append(attend_row(query, pages, list_length[at]))
        for i, result in enumerate(results):
            rows[list_row[step * ROW_UNROLL + i]] = result

    if last:
        for h in range(query_heads):
            out[:, h * HD : (h + 1) * HD] = rows[:row_local, h, :].astype(out.dtype)
    else:
        out[...] = rows[:row_local]
    for store in stores:
        store.wait()


def settle(dims, routes, own, last, table, row_request, queries, rows, received, blocks):
    row_local, query_heads, _ = queries.shape
    smem = pl.BlockSpec(memory_space=pltpu.SMEM)
    vmem = pl.BlockSpec(memory_space=pltpu.VMEM)
    hbm = pl.BlockSpec(memory_space=pl.ANY)
    count = len(blocks) + (1 if own else 0)
    if last:
        out = jax.ShapeDtypeStruct((row_local, query_heads * HD), jnp.bfloat16)
    else:
        out = jax.ShapeDtypeStruct(rows.shape, rows.dtype)
    return pl.pallas_call(
        functools.partial(settle_kernel, dims, routes, own, last),
        out_shape=[jax.ShapeDtypeStruct(received.shape, received.dtype), out],
        in_specs=[smem, smem, vmem, vmem, hbm] + [hbm] * len(blocks),
        out_specs=[hbm, vmem],
        scratch_shapes=[
            pltpu.VMEM((row_local + 1, query_heads, HD), jnp.float32),
            pltpu.VMEM((count, MAX_PAGES) + received.shape[1:], received.dtype),
            pltpu.SMEM((row_local + ROW_UNROLL,), jnp.int32),
            pltpu.SMEM((row_local + ROW_UNROLL,), jnp.int32),
            pltpu.SMEM((row_local + ROW_UNROLL,), jnp.int32),
            pltpu.SemaphoreType.DMA((count,)),
            pltpu.SemaphoreType.DMA((count,)),
        ],
        input_output_aliases={4: 0},
        compiler_params=pltpu.CompilerParams(vmem_limit_bytes=VMEM_LIMIT),
        cost_estimate=pl.CostEstimate(
            flops=1 << 30, bytes_accessed=4 * sum(b.size for b in blocks), transcendentals=1 << 18
        ),
        name="settle_pages",
    )(table, row_request, queries, rows, received, *blocks)


def multiply_rows(shards, out_weight, attended, sems):
    copies = []
    row_local = shards[0].shape[0]
    for i, shard in enumerate(shards):
        copies.append(pltpu.make_async_copy(shard, attended.at[pl.ds(i * row_local, row_local)], sems.at[i]))
        copies[-1].start()
    for copy in copies:
        copy.wait()
    return jnp.dot(attended[...], out_weight[...], preferred_element_type=jnp.float32)


def project_some_kernel(count, out_weight, *rest):
    out, attended, sems = rest[count:]
    out[...] = multiply_rows(rest[:count], out_weight, attended, sems)


def project_rest_kernel(masks, count, out_weight, some, *rest):
    own, *theirs = rest[count:-3]
    attended, product, sems = rest[-3:]
    me = lax.axis_index("group")
    heads = lax.axis_size("head")
    my_head = lax.axis_index("head")
    row_local = rest[0].shape[0]
    share = own.shape[0]
    product[...] = multiply_rows(rest[:count], out_weight, attended, sems)
    for i, mask in enumerate(masks):
        done = len(masks) - count
        part = some if i < done else product
        at = i if i < done else i - done
        values = part[at * row_local : (at + 1) * row_local]
        row = (me ^ mask) * row_local
        ahead = lax.rem(row // share - my_head + heads, heads)
        place = pl.ds(pl.multiple_of(lax.rem(row, share), row_local), row_local)
        for k, out in enumerate([own, *theirs]):

            @pl.when(ahead == k)
            def _():
                out[place] = values.astype(out.dtype)


def project(gathered, out_weight, heads):
    masks = [mask for mask in gathered if mask % 2 == 0] + [mask for mask in gathered if mask % 2]
    some = len(masks) // 2
    row_local, width = gathered[0].shape
    columns = out_weight.shape[1]
    share = row_local * len(masks) // heads
    vmem = pl.BlockSpec(memory_space=pltpu.VMEM)
    hbm = pl.BlockSpec(memory_space=pl.ANY)

    def call(kernel, name, outs, blocks, extra, scratch):
        rows = row_local * len(blocks)
        return pl.pallas_call(
            kernel,
            out_shape=outs,
            in_specs=[vmem] * (1 + len(extra)) + [hbm] * len(blocks),
            out_specs=[vmem] * len(outs),
            scratch_shapes=[
                pltpu.VMEM((rows, width), jnp.bfloat16),
                *scratch,
                pltpu.SemaphoreType.DMA((len(blocks),)),
            ],
            compiler_params=pltpu.CompilerParams(vmem_limit_bytes=VMEM_LIMIT),
            cost_estimate=pl.CostEstimate(
                flops=2 * rows * width * columns, bytes_accessed=2 * out_weight.size, transcendentals=0
            ),
            name=name,
        )(out_weight, *extra, *blocks)

    out_weight = pltpu.with_memory_space_constraint(out_weight, pltpu.VMEM)
    first = [gathered[mask] for mask in masks[:some]]
    last = [gathered[mask] for mask in masks[some:]]
    (done,) = call(
        functools.partial(project_some_kernel, some), "project_some_rows",
        [jax.ShapeDtypeStruct((some * row_local, columns), jnp.float32)], first, [], [],
    )
    theirs = jax.ShapeDtypeStruct((share, columns), jnp.bfloat16)
    return call(
        functools.partial(project_rest_kernel, masks, len(last)), "project_rows",
        [jax.ShapeDtypeStruct((share, columns), jnp.float32)] + [theirs] * (heads - 1), last, [done],
        [pltpu.VMEM((len(last) * row_local, columns), jnp.float32)],
    )


def local(kv_pool, lengths, prefill_of, decode_of, row_request, queries, out_weight):
    row_local, query_width = queries.shape
    query_heads = queries.reshape(row_local, query_width // HD, HD)
    heads = lax.axis_size("head")

    dims = factors(lax.axis_size("group"))
    routes = page_rounds(dims)
    table = packed(lengths, prefill_of, decode_of, math.prod(dims))
    kv_pool = pltpu.with_memory_space_constraint(kv_pool, pltpu.HBM)
    early = prepare(dims, routes[:EARLY], table, kv_pool, False)
    received, *late = prepare(dims, routes[EARLY:], table, kv_pool, True, early[:1])
    arrived = [send_by(block, route, dims) for block, route in zip([*early, *late], routes)]
    rows = jnp.zeros(query_heads.shape, jnp.float32)
    for first in range(0, len(routes), WAVE):
        wave = slice(first, first + WAVE)
        last = first + WAVE >= len(routes)
        received, rows = settle(
            dims, routes[wave], first == 0, last, table, row_request, query_heads, rows, received, arrived[wave]
        )

    own, *theirs = project(gather_shards(rows), out_weight, heads)
    for ahead_by, part in enumerate(theirs, 1):
        pairs = [(h, (h + ahead_by) % heads) for h in range(heads)]
        own = own + lax.ppermute(part, "head", pairs).astype(jnp.float32)
    return (received, own.astype(jnp.bfloat16))


def solution(mesh):
    in_specs = (
        P("group", None, "head"),
        P(),
        P(),
        P(),
        P(),
        P("group", "head"),
        P("head", "group"),
    )
    assert mesh.shape["group"] & (mesh.shape["group"] - 1) == 0
    out_specs = (P("group", None, "head"), P("head", "group"))
    return jax.shard_map(local, mesh=mesh, in_specs=in_specs, out_specs=out_specs, check_vma=False)
```

```python
import functools
import math

import jax
import jax.numpy as jnp
from jax import lax
from jax.experimental import pallas as pl
from jax.experimental.pallas import tpu as pltpu
from jax.sharding import PartitionSpec as P

HD = 128
MAX_PAGES = 2
WAVE = 3
ROW_UNROLL = 4
EARLY = 2
VMEM_LIMIT = 20 * 1024 * 1024


def factors(groups):
    near = math.gcd(groups, 4)
    return groups // near, near


def uniform(step, swap, dims):
    return tuple(((z + step) % dims[0], swap) for z in range(dims[0]))


def page_rounds(dims):
    far, near = dims
    half = max(near // 2, 1)
    order = []
    for low in range(0, near, half):
        swaps = range(low, min(low + half, near))
        opening = [(1, n) for n in swaps] if low == 0 else [(z, n) for n in swaps for z in (1, 0)]
        rest = [(z, n) for n in swaps for z in range(far - 1, 1, -1)]
        order += opening + ([(0, n) for n in swaps if n] if low == 0 else []) + rest
    return [uniform(z, n, dims) for z, n in order]


def reverse(route):
    sources = {to: (z, swap) for z, (to, swap) in enumerate(route)}
    return tuple(sources[z] for z in range(len(route)))


def routed(me, route, dims):
    near = dims[1]
    z = me // near
    to, swap = jnp.int32(route[0][0]), jnp.int32(route[0][1])
    for place in range(1, dims[0]):
        to = jnp.where(z == place, route[place][0], to)
        swap = jnp.where(z == place, route[place][1], swap)
    return to * near + (me % near ^ swap)


def send_by(array, route, dims):
    far, near = dims
    pairs = [
        (z * near + n, route[z][0] * near + (n ^ route[z][1])) for z in range(far) for n in range(near)
    ]
    return lax.ppermute(array, "group", pairs)


def swap(array, mask):
    groups = lax.axis_size("group")
    return lax.ppermute(array, "group", [(s, s ^ mask) for s in range(groups)])


def gather_shards(shard):
    held = {0: shard}
    mask = lax.axis_size("group") // 2
    while mask:
        held.update({done | mask: swap(array, mask) for done, array in held.items()})
        mask //= 2
    return held


def packed(lengths, prefill_of, decode_of, groups):
    bits = (groups - 1).bit_length()
    return (lengths << 2 * bits) | (prefill_of << bits) | decode_of


def unpacked(entry, groups):
    bits = (groups - 1).bit_length()
    mask = (1 << bits) - 1
    return entry >> 2 * bits, (entry >> bits) & mask, entry & mask


def prepare_kernel(dims, routes, own, table_hbm, pool, *rest):
    table, held, zero_page, start_of, count_of, table_sem, in_sems, out_sems = rest[-8:]
    received = rest[-8 - len(routes) - own : -8 - len(routes)]
    sends = rest[-8 - len(routes) : -8]
    me = lax.axis_index("group")
    groups = lax.axis_size("group")
    page_size = pool.shape[1]
    copy = pltpu.make_async_copy(table_hbm, table, table_sem)
    copy.start()
    for d in range(groups + 1):
        start_of[d] = 0
        count_of[d] = 0
    zero_page[...] = jnp.zeros_like(zero_page)
    copy.wait()

    def visit(r, running):
        length, home, destination = unpacked(table[r], groups)
        mine = home == me
        count = (length + page_size - 1) // page_size
        to = jnp.where(mine, destination, groups)
        start_of[to] = running
        count_of[to] = count
        return running + jnp.where(mine, count, 0)

    lax.fori_loop(0, table.shape[0], visit, jnp.int32(0), unroll=8)
    targets = [(routed(me, route, dims), send, 0) for route, send in zip(routes, sends)]
    if own:
        targets.append((me, received[0], me * MAX_PAGES))

    def each(do):
        for i, (to, target, base) in enumerate(targets):
            for page in range(MAX_PAGES):
                there = page < count_of[to]
                source = pool.at[jnp.where(there, start_of[to] + page, 0)]
                buffer, place = held.at[i, page], target.at[base + page]
                sem = out_sems.at[i, page]
                do(there, (source, buffer, in_sems.at[i, page]), (buffer, place, sem), (zero_page, place, sem))

    def fetch(there, load, store, blank):
        @pl.when(there)
        def _():
            pltpu.make_async_copy(*load).start()

        @pl.when(jnp.logical_not(there))
        def _():
            pltpu.make_async_copy(*blank).start()

    def forward(there, load, store, blank):
        @pl.when(there)
        def _():
            pltpu.make_async_copy(*load).wait()
            pltpu.make_async_copy(*store).start()

    def finish(there, load, store, blank):
        pltpu.make_async_copy(*blank).wait()

    each(fetch)
    each(forward)
    each(finish)


def prepare(dims, routes, table, pool, own, after=()):
    groups = lax.axis_size("group")
    page = pool.shape[1:]
    blocks = len(routes) + (1 if own else 0)
    hbm = pl.BlockSpec(memory_space=pl.ANY)
    block = jax.ShapeDtypeStruct((MAX_PAGES,) + page, pool.dtype)
    outs = [jax.ShapeDtypeStruct((groups * MAX_PAGES,) + page, pool.dtype)] * own + [block] * len(routes)
    operands = [table, pool, *after]
    return pl.pallas_call(
        functools.partial(prepare_kernel, dims, routes, own),
        out_shape=outs,
        in_specs=[hbm] * len(operands),
        out_specs=[hbm] * len(outs),
        scratch_shapes=[
            pltpu.SMEM(table.shape, jnp.int32),
            pltpu.VMEM((blocks, MAX_PAGES) + page, pool.dtype),
            pltpu.VMEM(page, pool.dtype),
            pltpu.SMEM((groups + 1,), jnp.int32),
            pltpu.SMEM((groups + 1,), jnp.int32),
            pltpu.SemaphoreType.DMA,
            pltpu.SemaphoreType.DMA((blocks, MAX_PAGES)),
            pltpu.SemaphoreType.DMA((blocks, MAX_PAGES)),
        ],
        compiler_params=pltpu.CompilerParams(vmem_limit_bytes=VMEM_LIMIT),
        cost_estimate=pl.CostEstimate(
            flops=0, bytes_accessed=4 * blocks * MAX_PAGES * math.prod(page), transcendentals=0
        ),
        name="outgoing_pages",
    )(*operands)


def attend_row(query, pages, length):
    first, second = pages
    kv_heads = first.shape[1] // (2 * HD)
    share = query.shape[0] // kv_heads
    scores = []
    for h in range(kv_heads):
        columns = slice(2 * h * HD, (2 * h + 1) * HD)
        keys = jnp.concatenate([first[:, columns], second[:, columns]], axis=0)
        every = lax.dot_general(
            query, keys, (((1,), (1,)), ((), ())), preferred_element_type=jnp.float32
        )
        scores.append(every[h * share : (h + 1) * share])
    score = jnp.concatenate(scores, axis=0) * (1.0 / math.sqrt(HD))
    live = lax.broadcasted_iota(jnp.int32, score.shape, 1) < length
    masked = jnp.where(live, score, -1e30)
    highest = jnp.max(masked, axis=1, keepdims=True)
    weights = jnp.where(live, jnp.exp(masked - highest), 0.0)
    totals = jnp.sum(weights, axis=1, keepdims=True)
    rounded = weights.astype(jnp.bfloat16)
    mixtures = []
    for h in range(kv_heads):
        columns = slice((2 * h + 1) * HD, (2 * h + 2) * HD)
        values = jnp.concatenate([first[:, columns], second[:, columns]], axis=0)
        every = jnp.dot(rounded, values, preferred_element_type=jnp.float32)
        mixtures.append(every[h * share : (h + 1) * share])
    return jnp.concatenate(mixtures, axis=0) / totals


def settle_kernel(dims, routes, own, last, table, row_request, queries, rows_in, received_in, *rest):
    blocks = rest[: len(routes)]
    received, out, rows, held, list_row, list_block, list_length, in_sems, out_sems = rest[len(routes) :]
    me = lax.axis_index("group")
    row_local, query_heads, _ = queries.shape
    mine = pl.ds(me * MAX_PAGES, MAX_PAGES)
    origins = [routed(me, reverse(route), dims) for route in routes]
    places = [pl.ds(origin * MAX_PAGES, MAX_PAGES) for origin in origins]
    sources = list(blocks) + ([received_in.at[mine]] if own else [])
    origins += [me] if own else []
    loads = [pltpu.make_async_copy(s, held.at[i], in_sems.at[i]) for i, s in enumerate(sources)]
    stores = [
        pltpu.make_async_copy(held.at[i], received.at[place], out_sems.at[i]) for i, place in enumerate(places)
    ]
    for load in loads:
        load.start()

    found = jnp.int32(0)
    for b in range(row_local):
        length, home, _ = unpacked(table[row_request[me * row_local + b]], math.prod(dims))
        block, match = jnp.int32(0), jnp.int32(0)
        for i, origin in enumerate(origins):
            block = jnp.where(home == origin, i, block)
            match = jnp.where(home == origin, 1, match)
        list_row[found] = b
        list_block[found] = block
        list_length[found] = length
        found = found + match
    for i in range(ROW_UNROLL):
        list_row[found + i] = row_local
        list_block[found + i] = 0
        list_length[found + i] = 1
    rows[:row_local] = rows_in[...]
    for load in loads:
        load.wait()
    for store in stores:
        store.start()

    @pl.loop(0, (found + ROW_UNROLL - 1) // ROW_UNROLL)
    def _(step):
        results = []
        for i in range(ROW_UNROLL):
            at = step * ROW_UNROLL + i
            query = queries[jnp.minimum(list_row[at], row_local - 1)]
            pages = [held[list_block[at], page] for page in range(MAX_PAGES)]
            results.append(attend_row(query, pages, list_length[at]))
        for i, result in enumerate(results):
            rows[list_row[step * ROW_UNROLL + i]] = result

    if last:
        for h in range(query_heads):
            out[:, h * HD : (h + 1) * HD] = rows[:row_local, h, :].astype(out.dtype)
    else:
        out[...] = rows[:row_local]
    for store in stores:
        store.wait()


def settle(dims, routes, own, last, table, row_request, queries, rows, received, blocks):
    row_local, query_heads, _ = queries.shape
    smem = pl.BlockSpec(memory_space=pltpu.SMEM)
    vmem = pl.BlockSpec(memory_space=pltpu.VMEM)
    hbm = pl.BlockSpec(memory_space=pl.ANY)
    count = len(blocks) + (1 if own else 0)
    if last:
        out = jax.ShapeDtypeStruct((row_local, query_heads * HD), jnp.bfloat16)
    else:
        out = jax.ShapeDtypeStruct(rows.shape, rows.dtype)
    return pl.pallas_call(
        functools.partial(settle_kernel, dims, routes, own, last),
        out_shape=[jax.ShapeDtypeStruct(received.shape, received.dtype), out],
        in_specs=[smem, smem, vmem, vmem, hbm] + [hbm] * len(blocks),
        out_specs=[hbm, vmem],
        scratch_shapes=[
            pltpu.VMEM((row_local + 1, query_heads, HD), jnp.float32),
            pltpu.VMEM((count, MAX_PAGES) + received.shape[1:], received.dtype),
            pltpu.SMEM((row_local + ROW_UNROLL,), jnp.int32),
            pltpu.SMEM((row_local + ROW_UNROLL,), jnp.int32),
            pltpu.SMEM((row_local + ROW_UNROLL,), jnp.int32),
            pltpu.SemaphoreType.DMA((count,)),
            pltpu.SemaphoreType.DMA((count,)),
        ],
        input_output_aliases={4: 0},
        compiler_params=pltpu.CompilerParams(vmem_limit_bytes=VMEM_LIMIT),
        cost_estimate=pl.CostEstimate(
            flops=1 << 30, bytes_accessed=4 * sum(b.size for b in blocks), transcendentals=1 << 18
        ),
        name="settle_pages",
    )(table, row_request, queries, rows, received, *blocks)


def multiply_rows(shards, out_weight, attended, sems):
    copies = []
    row_local = shards[0].shape[0]
    for i, shard in enumerate(shards):
        copies.append(pltpu.make_async_copy(shard, attended.at[pl.ds(i * row_local, row_local)], sems.at[i]))
        copies[-1].start()
    for copy in copies:
        copy.wait()
    return jnp.dot(attended[...], out_weight[...], preferred_element_type=jnp.float32)


def project_some_kernel(count, out_weight, *rest):
    out, attended, sems = rest[count:]
    out[...] = multiply_rows(rest[:count], out_weight, attended, sems)


def project_rest_kernel(masks, count, out_weight, some, *rest):
    own, *theirs = rest[count:-3]
    attended, product, sems = rest[-3:]
    me = lax.axis_index("group")
    heads = lax.axis_size("head")
    my_head = lax.axis_index("head")
    row_local = rest[0].shape[0]
    share = own.shape[0]
    product[...] = multiply_rows(rest[:count], out_weight, attended, sems)
    for i, mask in enumerate(masks):
        done = len(masks) - count
        part = some if i < done else product
        at = i if i < done else i - done
        values = part[at * row_local : (at + 1) * row_local]
        row = (me ^ mask) * row_local
        ahead = lax.rem(row // share - my_head + heads, heads)
        place = pl.ds(pl.multiple_of(lax.rem(row, share), row_local), row_local)
        for k, out in enumerate([own, *theirs]):

            @pl.when(ahead == k)
            def _():
                out[place] = values.astype(out.dtype)


def project(gathered, out_weight, heads):
    masks = [mask for mask in gathered if mask % 2 == 0] + [mask for mask in gathered if mask % 2]
    some = len(masks) // 2
    row_local, width = gathered[0].shape
    columns = out_weight.shape[1]
    share = row_local * len(masks) // heads
    vmem = pl.BlockSpec(memory_space=pltpu.VMEM)
    hbm = pl.BlockSpec(memory_space=pl.ANY)

    def call(kernel, name, outs, blocks, extra, scratch):
        rows = row_local * len(blocks)
        return pl.pallas_call(
            kernel,
            out_shape=outs,
            in_specs=[vmem] * (1 + len(extra)) + [hbm] * len(blocks),
            out_specs=[vmem] * len(outs),
            scratch_shapes=[
                pltpu.VMEM((rows, width), jnp.bfloat16),
                *scratch,
                pltpu.SemaphoreType.DMA((len(blocks),)),
            ],
            compiler_params=pltpu.CompilerParams(vmem_limit_bytes=VMEM_LIMIT),
            cost_estimate=pl.CostEstimate(
                flops=2 * rows * width * columns, bytes_accessed=2 * out_weight.size, transcendentals=0
            ),
            name=name,
        )(out_weight, *extra, *blocks)

    out_weight = pltpu.with_memory_space_constraint(out_weight, pltpu.VMEM)
    first = [gathered[mask] for mask in masks[:some]]
    last = [gathered[mask] for mask in masks[some:]]
    (done,) = call(
        functools.partial(project_some_kernel, some), "project_some_rows",
        [jax.ShapeDtypeStruct((some * row_local, columns), jnp.float32)], first, [], [],
    )
    theirs = jax.ShapeDtypeStruct((share, columns), jnp.bfloat16)
    return call(
        functools.partial(project_rest_kernel, masks, len(last)), "project_rows",
        [jax.ShapeDtypeStruct((share, columns), jnp.float32)] + [theirs] * (heads - 1), last, [done],
        [pltpu.VMEM((len(last) * row_local, columns), jnp.float32)],
    )


def local(kv_pool, lengths, prefill_of, decode_of, row_request, queries, out_weight):
    row_local, query_width = queries.shape
    query_heads = queries.reshape(row_local, query_width // HD, HD)
    heads = lax.axis_size("head")

    dims = factors(lax.axis_size("group"))
    routes = page_rounds(dims)
    table = packed(lengths, prefill_of, decode_of, math.prod(dims))
    kv_pool = pltpu.with_memory_space_constraint(kv_pool, pltpu.HBM)
    early = prepare(dims, routes[:EARLY], table, kv_pool, False)
    received, *late = prepare(dims, routes[EARLY:], table, kv_pool, True, early[:1])
    arrived = [send_by(block, route, dims) for block, route in zip([*early, *late], routes)]
    rows = jnp.zeros(query_heads.shape, jnp.float32)
    for first in range(0, len(routes), WAVE):
        wave = slice(first, first + WAVE)
        last = first + WAVE >= len(routes)
        received, rows = settle(
            dims, routes[wave], first == 0, last, table, row_request, query_heads, rows, received, arrived[wave]
        )

    own, *theirs = project(gather_shards(rows), out_weight, heads)
    for ahead_by, part in enumerate(theirs, 1):
        pairs = [(h, (h + ahead_by) % heads) for h in range(heads)]
        own = own + lax.ppermute(part, "head", pairs).astype(jnp.float32)
    return (received, own.astype(jnp.bfloat16))


def solution(mesh):
    in_specs = (
        P("group", None, "head"),
        P(),
        P(),
        P(),
        P(),
        P("group", "head"),
        P("head", "group"),
    )
    assert mesh.shape["group"] & (mesh.shape["group"] - 1) == 0
    out_specs = (P("group", None, "head"), P("head", "group"))
    return jax.shard_map(local, mesh=mesh, in_specs=in_specs, out_specs=out_specs, check_vma=False)
```

```python
import functools
import math

import jax
import jax.numpy as jnp
from jax import lax
from jax.experimental import pallas as pl
from jax.experimental.pallas import tpu as pltpu
from jax.sharding import PartitionSpec as P

HD = 128
MAX_PAGES = 2
WAVE = 3
ROW_UNROLL = 4
EARLY = 1
VMEM_LIMIT = 20 * 1024 * 1024


def factors(groups):
    near = math.gcd(groups, 4)
    return groups // near, near


def uniform(step, swap, dims):
    return tuple(((z + step) % dims[0], swap) for z in range(dims[0]))


def page_sendings(dims):
    far, near = dims
    half = max(near // 2, 1)
    steps, sendings = range(1, far), []
    for low in range(0, near, half):
        here = [[(0, n)] for n in range(low, min(low + half, near)) if n]
        pairs = [[(z, n) for n in range(low, min(low + half, near))] for z in steps]
        sendings += pairs[:1] + here + pairs[1:]
    sendings[-1:] = [[round_] for round_ in sendings[-1]]
    return [[uniform(z, n, dims) for z, n in several] for several in sendings]


def reverse(route):
    sources = {to: (z, swap) for z, (to, swap) in enumerate(route)}
    return tuple(sources[z] for z in range(len(route)))


def routed(me, route, dims):
    near = dims[1]
    z = me // near
    to, swap = jnp.int32(route[0][0]), jnp.int32(route[0][1])
    for place in range(1, dims[0]):
        to = jnp.where(z == place, route[place][0], to)
        swap = jnp.where(z == place, route[place][1], swap)
    return to * near + (me % near ^ swap)


def send_by(array, route, dims):
    far, near = dims
    pairs = [
        (z * near + n, route[z][0] * near + (n ^ route[z][1])) for z in range(far) for n in range(near)
    ]
    return lax.ppermute(array, "group", pairs)


def swap(array, mask):
    groups = lax.axis_size("group")
    return lax.ppermute(array, "group", [(s, s ^ mask) for s in range(groups)])


def gather_shards(shard):
    held = {0: shard}
    mask = lax.axis_size("group") // 2
    while mask:
        held.update({done | mask: swap(array, mask) for done, array in held.items()})
        mask //= 2
    return held


def packed(lengths, prefill_of, decode_of, groups):
    bits = (groups - 1).bit_length()
    return (lengths << 2 * bits) | (prefill_of << bits) | decode_of


def unpacked(entry, groups):
    bits = (groups - 1).bit_length()
    mask = (1 << bits) - 1
    return entry >> 2 * bits, (entry >> bits) & mask, entry & mask


def prepare_kernel(dims, sendings, own, table_hbm, pool, *rest):
    table, held, zero_page, start_of, count_of, table_sem, in_sems, out_sems = rest[-8:]
    received = rest[-8 - len(sendings) - own : -8 - len(sendings)]
    sends = rest[-8 - len(sendings) : -8]
    me = lax.axis_index("group")
    groups = lax.axis_size("group")
    page_size = pool.shape[1]
    copy = pltpu.make_async_copy(table_hbm, table, table_sem)
    copy.start()
    for d in range(groups + 1):
        start_of[d] = 0
        count_of[d] = 0
    zero_page[...] = jnp.zeros_like(zero_page)
    copy.wait()

    def visit(r, running):
        length, home, destination = unpacked(table[r], groups)
        mine = home == me
        count = (length + page_size - 1) // page_size
        to = jnp.where(mine, destination, groups)
        start_of[to] = running
        count_of[to] = count
        return running + jnp.where(mine, count, 0)

    lax.fori_loop(0, table.shape[0], visit, jnp.int32(0), unroll=8)
    targets = [
        (routed(me, route, dims), send, i * MAX_PAGES)
        for several, send in zip(sendings, sends)
        for i, route in enumerate(several)
    ]
    if own:
        targets.append((me, received[0], me * MAX_PAGES))

    def each(do):
        for i, (to, target, base) in enumerate(targets):
            for page in range(MAX_PAGES):
                there = page < count_of[to]
                source = pool.at[jnp.where(there, start_of[to] + page, 0)]
                buffer, place = held.at[i, page], target.at[base + page]
                sem = out_sems.at[i, page]
                do(there, (source, buffer, in_sems.at[i, page]), (buffer, place, sem), (zero_page, place, sem))

    def fetch(there, load, store, blank):
        @pl.when(there)
        def _():
            pltpu.make_async_copy(*load).start()

        @pl.when(jnp.logical_not(there))
        def _():
            pltpu.make_async_copy(*blank).start()

    def forward(there, load, store, blank):
        @pl.when(there)
        def _():
            pltpu.make_async_copy(*load).wait()
            pltpu.make_async_copy(*store).start()

    def finish(there, load, store, blank):
        pltpu.make_async_copy(*blank).wait()

    each(fetch)
    each(forward)
    each(finish)


def prepare(dims, sendings, table, pool, own, after=()):
    groups = math.prod(dims)
    page = pool.shape[1:]
    blocks = sum(len(several) for several in sendings) + (1 if own else 0)
    hbm = pl.BlockSpec(memory_space=pl.ANY)
    outs = [jax.ShapeDtypeStruct((groups * MAX_PAGES,) + page, pool.dtype)] * own
    outs += [jax.ShapeDtypeStruct((len(several) * MAX_PAGES,) + page, pool.dtype) for several in sendings]
    operands = [table, pool, *after]
    return pl.pallas_call(
        functools.partial(prepare_kernel, dims, sendings, own),
        out_shape=outs,
        in_specs=[hbm] * len(operands),
        out_specs=[hbm] * len(outs),
        scratch_shapes=[
            pltpu.SMEM(table.shape, jnp.int32),
            pltpu.VMEM((blocks, MAX_PAGES) + page, pool.dtype),
            pltpu.VMEM(page, pool.dtype),
            pltpu.SMEM((groups + 1,), jnp.int32),
            pltpu.SMEM((groups + 1,), jnp.int32),
            pltpu.SemaphoreType.DMA,
            pltpu.SemaphoreType.DMA((blocks, MAX_PAGES)),
            pltpu.SemaphoreType.DMA((blocks, MAX_PAGES)),
        ],
        compiler_params=pltpu.CompilerParams(vmem_limit_bytes=VMEM_LIMIT),
        cost_estimate=pl.CostEstimate(
            flops=0, bytes_accessed=4 * blocks * MAX_PAGES * math.prod(page), transcendentals=0
        ),
        name="outgoing_pages",
    )(*operands)


def attend_row(query, pages, length):
    first, second = pages
    kv_heads = first.shape[1] // (2 * HD)
    share = query.shape[0] // kv_heads
    scores = []
    for h in range(kv_heads):
        columns = slice(2 * h * HD, (2 * h + 1) * HD)
        keys = jnp.concatenate([first[:, columns], second[:, columns]], axis=0)
        every = lax.dot_general(
            query, keys, (((1,), (1,)), ((), ())), preferred_element_type=jnp.float32
        )
        scores.append(every[h * share : (h + 1) * share])
    score = jnp.concatenate(scores, axis=0) * (1.0 / math.sqrt(HD))
    live = lax.broadcasted_iota(jnp.int32, score.shape, 1) < length
    masked = jnp.where(live, score, -1e30)
    highest = jnp.max(masked, axis=1, keepdims=True)
    weights = jnp.where(live, jnp.exp(masked - highest), 0.0)
    totals = jnp.sum(weights, axis=1, keepdims=True)
    rounded = weights.astype(jnp.bfloat16)
    mixtures = []
    for h in range(kv_heads):
        columns = slice((2 * h + 1) * HD, (2 * h + 2) * HD)
        values = jnp.concatenate([first[:, columns], second[:, columns]], axis=0)
        every = jnp.dot(rounded, values, preferred_element_type=jnp.float32)
        mixtures.append(every[h * share : (h + 1) * share])
    return jnp.concatenate(mixtures, axis=0) / totals


def settle_kernel(dims, routes, own, last, table, row_request, queries, rows_in, received_in, *rest):
    blocks = rest[: len(routes)]
    received, out, rows, held, list_row, list_block, list_length, in_sems, out_sems = rest[len(routes) :]
    me = lax.axis_index("group")
    row_local, query_heads, _ = queries.shape
    mine = pl.ds(me * MAX_PAGES, MAX_PAGES)
    origins = [routed(me, reverse(route), dims) for route in routes]
    places = [pl.ds(origin * MAX_PAGES, MAX_PAGES) for origin in origins]
    sources = list(blocks) + ([received_in.at[mine]] if own else [])
    origins += [me] if own else []
    loads = [pltpu.make_async_copy(s, held.at[i], in_sems.at[i]) for i, s in enumerate(sources)]
    stores = [
        pltpu.make_async_copy(held.at[i], received.at[place], out_sems.at[i]) for i, place in enumerate(places)
    ]
    for load in loads:
        load.start()

    found = jnp.int32(0)
    for b in range(row_local):
        length, home, _ = unpacked(table[row_request[me * row_local + b]], math.prod(dims))
        block, match = jnp.int32(0), jnp.int32(0)
        for i, origin in enumerate(origins):
            block = jnp.where(home == origin, i, block)
            match = jnp.where(home == origin, 1, match)
        list_row[found] = b
        list_block[found] = block
        list_length[found] = length
        found = found + match
    for i in range(ROW_UNROLL):
        list_row[found + i] = row_local
        list_block[found + i] = 0
        list_length[found + i] = 1
    rows[:row_local] = rows_in[...]
    for load in loads:
        load.wait()
    for store in stores:
        store.start()

    @pl.loop(0, (found + ROW_UNROLL - 1) // ROW_UNROLL)
    def _(step):
        results = []
        for i in range(ROW_UNROLL):
            at = step * ROW_UNROLL + i
            query = queries[jnp.minimum(list_row[at], row_local - 1)]
            pages = [held[list_block[at], page] for page in range(MAX_PAGES)]
            results.append(attend_row(query, pages, list_length[at]))
        for i, result in enumerate(results):
            rows[list_row[step * ROW_UNROLL + i]] = result

    if last:
        for h in range(query_heads):
            out[:, h * HD : (h + 1) * HD] = rows[:row_local, h, :].astype(out.dtype)
    else:
        out[...] = rows[:row_local]
    for store in stores:
        store.wait()


def settle(dims, routes, own, last, table, row_request, queries, rows, received, blocks):
    row_local, query_heads, _ = queries.shape
    smem = pl.BlockSpec(memory_space=pltpu.SMEM)
    vmem = pl.BlockSpec(memory_space=pltpu.VMEM)
    hbm = pl.BlockSpec(memory_space=pl.ANY)
    count = len(blocks) + (1 if own else 0)
    if last:
        out = jax.ShapeDtypeStruct((row_local, query_heads * HD), jnp.bfloat16)
    else:
        out = jax.ShapeDtypeStruct(rows.shape, rows.dtype)
    return pl.pallas_call(
        functools.partial(settle_kernel, dims, routes, own, last),
        out_shape=[jax.ShapeDtypeStruct(received.shape, received.dtype), out],
        in_specs=[smem, smem, vmem, vmem, hbm] + [hbm] * len(blocks),
        out_specs=[hbm, vmem],
        scratch_shapes=[
            pltpu.VMEM((row_local + 1, query_heads, HD), jnp.float32),
            pltpu.VMEM((count, MAX_PAGES) + received.shape[1:], received.dtype),
            pltpu.SMEM((row_local + ROW_UNROLL,), jnp.int32),
            pltpu.SMEM((row_local + ROW_UNROLL,), jnp.int32),
            pltpu.SMEM((row_local + ROW_UNROLL,), jnp.int32),
            pltpu.SemaphoreType.DMA((count,)),
            pltpu.SemaphoreType.DMA((count,)),
        ],
        input_output_aliases={4: 0},
        compiler_params=pltpu.CompilerParams(vmem_limit_bytes=VMEM_LIMIT),
        cost_estimate=pl.CostEstimate(
            flops=1 << 30, bytes_accessed=4 * sum(b.size for b in blocks), transcendentals=1 << 18
        ),
        name="settle_pages",
    )(table, row_request, queries, rows, received, *blocks)


def multiply_rows(shards, out_weight, attended, sems):
    copies = []
    row_local = shards[0].shape[0]
    for i, shard in enumerate(shards):
        copies.append(pltpu.make_async_copy(shard, attended.at[pl.ds(i * row_local, row_local)], sems.at[i]))
        copies[-1].start()
    for copy in copies:
        copy.wait()
    return jnp.dot(attended[...], out_weight[...], preferred_element_type=jnp.float32)


def project_some_kernel(count, out_weight, *rest):
    out, attended, sems = rest[count:]
    out[...] = multiply_rows(rest[:count], out_weight, attended, sems)


def project_rest_kernel(masks, count, out_weight, some, *rest):
    own, *theirs = rest[count:-3]
    attended, product, sems = rest[-3:]
    me = lax.axis_index("group")
    heads = lax.axis_size("head")
    my_head = lax.axis_index("head")
    row_local = rest[0].shape[0]
    share = own.shape[0]
    product[...] = multiply_rows(rest[:count], out_weight, attended, sems)
    for i, mask in enumerate(masks):
        done = len(masks) - count
        part = some if i < done else product
        at = i if i < done else i - done
        values = part[at * row_local : (at + 1) * row_local]
        row = (me ^ mask) * row_local
        ahead = lax.rem(row // share - my_head + heads, heads)
        place = pl.ds(pl.multiple_of(lax.rem(row, share), row_local), row_local)
        for k, out in enumerate([own, *theirs]):

            @pl.when(ahead == k)
            def _():
                out[place] = values.astype(out.dtype)


def project(gathered, out_weight, heads):
    masks = [mask for mask in gathered if mask % 2 == 0] + [mask for mask in gathered if mask % 2]
    some = len(masks) // 2
    row_local, width = gathered[0].shape
    columns = out_weight.shape[1]
    share = row_local * len(masks) // heads
    vmem = pl.BlockSpec(memory_space=pltpu.VMEM)
    hbm = pl.BlockSpec(memory_space=pl.ANY)

    def call(kernel, name, outs, blocks, extra, scratch):
        rows = row_local * len(blocks)
        return pl.pallas_call(
            kernel,
            out_shape=outs,
            in_specs=[vmem] * (1 + len(extra)) + [hbm] * len(blocks),
            out_specs=[vmem] * len(outs),
            scratch_shapes=[
                pltpu.VMEM((rows, width), jnp.bfloat16),
                *scratch,
                pltpu.SemaphoreType.DMA((len(blocks),)),
            ],
            compiler_params=pltpu.CompilerParams(vmem_limit_bytes=VMEM_LIMIT),
            cost_estimate=pl.CostEstimate(
                flops=2 * rows * width * columns, bytes_accessed=2 * out_weight.size, transcendentals=0
            ),
            name=name,
        )(out_weight, *extra, *blocks)

    out_weight = pltpu.with_memory_space_constraint(out_weight, pltpu.VMEM)
    first = [gathered[mask] for mask in masks[:some]]
    last = [gathered[mask] for mask in masks[some:]]
    (done,) = call(
        functools.partial(project_some_kernel, some), "project_some_rows",
        [jax.ShapeDtypeStruct((some * row_local, columns), jnp.float32)], first, [], [],
    )
    theirs = jax.ShapeDtypeStruct((share, columns), jnp.bfloat16)
    return call(
        functools.partial(project_rest_kernel, masks, len(last)), "project_rows",
        [jax.ShapeDtypeStruct((share, columns), jnp.float32)] + [theirs] * (heads - 1), last, [done],
        [pltpu.VMEM((len(last) * row_local, columns), jnp.float32)],
    )


def local(kv_pool, lengths, prefill_of, decode_of, row_request, queries, out_weight):
    row_local, query_width = queries.shape
    query_heads = queries.reshape(row_local, query_width // HD, HD)
    heads = lax.axis_size("head")

    dims = factors(lax.axis_size("group"))
    sendings = page_sendings(dims)
    routes = [route for several in sendings for route in several]
    table = packed(lengths, prefill_of, decode_of, math.prod(dims))
    kv_pool = pltpu.with_memory_space_constraint(kv_pool, pltpu.HBM)
    early = prepare(dims, sendings[:EARLY], table, kv_pool, False)
    received, *late = prepare(dims, sendings[EARLY:], table, kv_pool, True, early[:1])
    arrived = []
    for carried, several in zip([*early, *late], sendings):
        landed = send_by(carried, several[0], dims)
        arrived.append(landed[:MAX_PAGES])
        if len(several) > 1:
            arrived.append(swap(landed[MAX_PAGES:], 1))
    rows = jnp.zeros(query_heads.shape, jnp.float32)
    for first in range(0, len(routes), WAVE):
        wave = slice(first, first + WAVE)
        last = first + WAVE >= len(routes)
        received, rows = settle(
            dims, routes[wave], first == 0, last, table, row_request, query_heads, rows, received, arrived[wave]
        )

    own, *theirs = project(gather_shards(rows), out_weight, heads)
    for ahead_by, part in enumerate(theirs, 1):
        pairs = [(h, (h + ahead_by) % heads) for h in range(heads)]
        own = own + lax.ppermute(part, "head", pairs).astype(jnp.float32)
    return (received, own.astype(jnp.bfloat16))


def solution(mesh):
    in_specs = (
        P("group", None, "head"),
        P(),
        P(),
        P(),
        P(),
        P("group", "head"),
        P("head", "group"),
    )
    assert mesh.shape["group"] & (mesh.shape["group"] - 1) == 0
    out_specs = (P("group", None, "head"), P("head", "group"))
    return jax.shard_map(local, mesh=mesh, in_specs=in_specs, out_specs=out_specs, check_vma=False)
```

```python
import functools
import math

import jax
import jax.numpy as jnp
from jax import lax
from jax.experimental import pallas as pl
from jax.experimental.pallas import tpu as pltpu
from jax.sharding import PartitionSpec as P

HD = 128
MAX_PAGES = 2
WAVE = 3
ROW_UNROLL = 4
EARLY = 2
VMEM_LIMIT = 20 * 1024 * 1024


def factors(groups):
    near = math.gcd(groups, 4)
    return groups // near, near


def uniform(step, swap, dims):
    return tuple(((z + step) % dims[0], swap) for z in range(dims[0]))


def page_rounds(dims):
    far, near = dims
    half = max(near // 2, 1)
    order = []
    for low in range(0, near, half):
        swaps = range(low, min(low + half, near))
        opening = [(1, n) for n in swaps] if low == 0 else [(z, n) for n in swaps for z in (1, 0)]
        rest = [(z, n) for n in swaps for z in range(2, far)]
        order += opening + ([(0, n) for n in swaps if n] if low == 0 else []) + rest
    return [uniform(z, n, dims) for z, n in order]


def reverse(route):
    sources = {to: (z, swap) for z, (to, swap) in enumerate(route)}
    return tuple(sources[z] for z in range(len(route)))


def routed(me, route, dims):
    near = dims[1]
    z = me // near
    to, swap = jnp.int32(route[0][0]), jnp.int32(route[0][1])
    for place in range(1, dims[0]):
        to = jnp.where(z == place, route[place][0], to)
        swap = jnp.where(z == place, route[place][1], swap)
    return to * near + (me % near ^ swap)


def send_by(array, route, dims):
    far, near = dims
    pairs = [
        (z * near + n, route[z][0] * near + (n ^ route[z][1])) for z in range(far) for n in range(near)
    ]
    return lax.ppermute(array, "group", pairs)


def swap(array, mask):
    groups = lax.axis_size("group")
    return lax.ppermute(array, "group", [(s, s ^ mask) for s in range(groups)])


def tied(array, after):
    return lax.optimization_barrier((array, after))[0]


def gather_shards(shard):
    groups = lax.axis_size("group")
    swaps = [1 << i for i in reversed(range(groups.bit_length() - 1))]
    own = {mask: swap(shard, mask) for mask in swaps}
    held = {0: shard, **own}
    if len(swaps) > 3:
        far, near, side = swaps[0], swaps[-3], swaps[-2]
        held[near] = tied(held[near], held[side])
        held[near | side] = swap(held[near], side)
        held[far] = tied(held[far], held[near | side])
    for mask in swaps[1:]:
        for done, array in list(held.items()):
            if done & -done > mask and done | mask not in held:
                held[done | mask] = swap(array, mask)
    return held


def packed(lengths, prefill_of, decode_of, groups):
    bits = (groups - 1).bit_length()
    return (lengths << 2 * bits) | (prefill_of << bits) | decode_of


def unpacked(entry, groups):
    bits = (groups - 1).bit_length()
    mask = (1 << bits) - 1
    return entry >> 2 * bits, (entry >> bits) & mask, entry & mask


def prepare_kernel(dims, routes, own, table_hbm, pool, *rest):
    table, held, zero_page, start_of, count_of, table_sem, in_sems, out_sems = rest[-8:]
    received = rest[-8 - len(routes) - own : -8 - len(routes)]
    sends = rest[-8 - len(routes) : -8]
    me = lax.axis_index("group")
    groups = lax.axis_size("group")
    page_size = pool.shape[1]
    copy = pltpu.make_async_copy(table_hbm, table, table_sem)
    copy.start()
    for d in range(groups + 1):
        start_of[d] = 0
        count_of[d] = 0
    zero_page[...] = jnp.zeros_like(zero_page)
    copy.wait()

    def visit(r, running):
        length, home, destination = unpacked(table[r], groups)
        mine = home == me
        count = (length + page_size - 1) // page_size
        to = jnp.where(mine, destination, groups)
        start_of[to] = running
        count_of[to] = count
        return running + jnp.where(mine, count, 0)

    lax.fori_loop(0, table.shape[0], visit, jnp.int32(0), unroll=8)
    targets = [(routed(me, route, dims), send, 0) for route, send in zip(routes, sends)]
    if own:
        targets.append((me, received[0], me * MAX_PAGES))

    def each(do):
        for i, (to, target, base) in enumerate(targets):
            for page in range(MAX_PAGES):
                there = page < count_of[to]
                source = pool.at[jnp.where(there, start_of[to] + page, 0)]
                buffer, place = held.at[i, page], target.at[base + page]
                sem = out_sems.at[i, page]
                do(there, (source, buffer, in_sems.at[i, page]), (buffer, place, sem), (zero_page, place, sem))

    def fetch(there, load, store, blank):
        @pl.when(there)
        def _():
            pltpu.make_async_copy(*load).start()

        @pl.when(jnp.logical_not(there))
        def _():
            pltpu.make_async_copy(*blank).start()

    def forward(there, load, store, blank):
        @pl.when(there)
        def _():
            pltpu.make_async_copy(*load).wait()
            pltpu.make_async_copy(*store).start()

    def finish(there, load, store, blank):
        pltpu.make_async_copy(*blank).wait()

    each(fetch)
    each(forward)
    each(finish)


def prepare(dims, routes, table, pool, own, after=()):
    groups = lax.axis_size("group")
    page = pool.shape[1:]
    blocks = len(routes) + (1 if own else 0)
    hbm = pl.BlockSpec(memory_space=pl.ANY)
    block = jax.ShapeDtypeStruct((MAX_PAGES,) + page, pool.dtype)
    outs = [jax.ShapeDtypeStruct((groups * MAX_PAGES,) + page, pool.dtype)] * own + [block] * len(routes)
    operands = [table, pool, *after]
    return pl.pallas_call(
        functools.partial(prepare_kernel, dims, routes, own),
        out_shape=outs,
        in_specs=[hbm] * len(operands),
        out_specs=[hbm] * len(outs),
        scratch_shapes=[
            pltpu.SMEM(table.shape, jnp.int32),
            pltpu.VMEM((blocks, MAX_PAGES) + page, pool.dtype),
            pltpu.VMEM(page, pool.dtype),
            pltpu.SMEM((groups + 1,), jnp.int32),
            pltpu.SMEM((groups + 1,), jnp.int32),
            pltpu.SemaphoreType.DMA,
            pltpu.SemaphoreType.DMA((blocks, MAX_PAGES)),
            pltpu.SemaphoreType.DMA((blocks, MAX_PAGES)),
        ],
        compiler_params=pltpu.CompilerParams(vmem_limit_bytes=VMEM_LIMIT),
        cost_estimate=pl.CostEstimate(
            flops=0, bytes_accessed=4 * blocks * MAX_PAGES * math.prod(page), transcendentals=0
        ),
        name="outgoing_pages",
    )(*operands)


def attend_row(query, pages, length):
    first, second = pages
    kv_heads = first.shape[1] // (2 * HD)
    share = query.shape[0] // kv_heads
    scores = []
    for h in range(kv_heads):
        columns = slice(2 * h * HD, (2 * h + 1) * HD)
        keys = jnp.concatenate([first[:, columns], second[:, columns]], axis=0)
        every = lax.dot_general(
            query, keys, (((1,), (1,)), ((), ())), preferred_element_type=jnp.float32
        )
        scores.append(every[h * share : (h + 1) * share])
    score = jnp.concatenate(scores, axis=0) * (1.0 / math.sqrt(HD))
    live = lax.broadcasted_iota(jnp.int32, score.shape, 1) < length
    masked = jnp.where(live, score, -1e30)
    highest = jnp.max(masked, axis=1, keepdims=True)
    weights = jnp.where(live, jnp.exp(masked - highest), 0.0)
    totals = jnp.sum(weights, axis=1, keepdims=True)
    rounded = weights.astype(jnp.bfloat16)
    mixtures = []
    for h in range(kv_heads):
        columns = slice((2 * h + 1) * HD, (2 * h + 2) * HD)
        values = jnp.concatenate([first[:, columns], second[:, columns]], axis=0)
        every = jnp.dot(rounded, values, preferred_element_type=jnp.float32)
        mixtures.append(every[h * share : (h + 1) * share])
    return jnp.concatenate(mixtures, axis=0) / totals


def settle_kernel(dims, routes, own, last, table, row_request, queries, rows_in, received_in, *rest):
    blocks = rest[: len(routes)]
    received, out, rows, held, list_row, list_block, list_length, in_sems, out_sems = rest[len(routes) :]
    me = lax.axis_index("group")
    row_local, query_heads, _ = queries.shape
    mine = pl.ds(me * MAX_PAGES, MAX_PAGES)
    origins = [routed(me, reverse(route), dims) for route in routes]
    places = [pl.ds(origin * MAX_PAGES, MAX_PAGES) for origin in origins]
    sources = list(blocks) + ([received_in.at[mine]] if own else [])
    origins += [me] if own else []
    loads = [pltpu.make_async_copy(s, held.at[i], in_sems.at[i]) for i, s in enumerate(sources)]
    stores = [
        pltpu.make_async_copy(held.at[i], received.at[place], out_sems.at[i]) for i, place in enumerate(places)
    ]
    for load in loads:
        load.start()

    found = jnp.int32(0)
    for b in range(row_local):
        length, home, _ = unpacked(table[row_request[me * row_local + b]], math.prod(dims))
        block, match = jnp.int32(0), jnp.int32(0)
        for i, origin in enumerate(origins):
            block = jnp.where(home == origin, i, block)
            match = jnp.where(home == origin, 1, match)
        list_row[found] = b
        list_block[found] = block
        list_length[found] = length
        found = found + match
    for i in range(ROW_UNROLL):
        list_row[found + i] = row_local
        list_block[found + i] = 0
        list_length[found + i] = 1
    rows[:row_local] = rows_in[...]
    for load in loads:
        load.wait()
    for store in stores:
        store.start()

    @pl.loop(0, (found + ROW_UNROLL - 1) // ROW_UNROLL)
    def _(step):
        results = []
        for i in range(ROW_UNROLL):
            at = step * ROW_UNROLL + i
            query = queries[jnp.minimum(list_row[at], row_local - 1)]
            pages = [held[list_block[at], page] for page in range(MAX_PAGES)]
            results.append(attend_row(query, pages, list_length[at]))
        for i, result in enumerate(results):
            rows[list_row[step * ROW_UNROLL + i]] = result

    if last:
        for h in range(query_heads):
            out[:, h * HD : (h + 1) * HD] = rows[:row_local, h, :].astype(out.dtype)
    else:
        out[...] = rows[:row_local]
    for store in stores:
        store.wait()


def settle(dims, routes, own, last, table, row_request, queries, rows, received, blocks):
    row_local, query_heads, _ = queries.shape
    smem = pl.BlockSpec(memory_space=pltpu.SMEM)
    vmem = pl.BlockSpec(memory_space=pltpu.VMEM)
    hbm = pl.BlockSpec(memory_space=pl.ANY)
    count = len(blocks) + (1 if own else 0)
    if last:
        out = jax.ShapeDtypeStruct((row_local, query_heads * HD), jnp.bfloat16)
    else:
        out = jax.ShapeDtypeStruct(rows.shape, rows.dtype)
    return pl.pallas_call(
        functools.partial(settle_kernel, dims, routes, own, last),
        out_shape=[jax.ShapeDtypeStruct(received.shape, received.dtype), out],
        in_specs=[smem, smem, vmem, vmem, hbm] + [hbm] * len(blocks),
        out_specs=[hbm, vmem],
        scratch_shapes=[
            pltpu.VMEM((row_local + 1, query_heads, HD), jnp.float32),
            pltpu.VMEM((count, MAX_PAGES) + received.shape[1:], received.dtype),
            pltpu.SMEM((row_local + ROW_UNROLL,), jnp.int32),
            pltpu.SMEM((row_local + ROW_UNROLL,), jnp.int32),
            pltpu.SMEM((row_local + ROW_UNROLL,), jnp.int32),
            pltpu.SemaphoreType.DMA((count,)),
            pltpu.SemaphoreType.DMA((count,)),
        ],
        input_output_aliases={4: 0},
        compiler_params=pltpu.CompilerParams(vmem_limit_bytes=VMEM_LIMIT),
        cost_estimate=pl.CostEstimate(
            flops=1 << 30, bytes_accessed=4 * sum(b.size for b in blocks), transcendentals=1 << 18
        ),
        name="settle_pages",
    )(table, row_request, queries, rows, received, *blocks)


def multiply_rows(shards, out_weight, attended, sems):
    copies = []
    row_local = shards[0].shape[0]
    for i, shard in enumerate(shards):
        copies.append(pltpu.make_async_copy(shard, attended.at[pl.ds(i * row_local, row_local)], sems.at[i]))
        copies[-1].start()
    for copy in copies:
        copy.wait()
    return jnp.dot(attended[...], out_weight[...], preferred_element_type=jnp.float32)


def project_some_kernel(count, out_weight, *rest):
    out, attended, sems = rest[count:]
    out[...] = multiply_rows(rest[:count], out_weight, attended, sems)


def project_rest_kernel(masks, count, out_weight, some, *rest):
    own, *theirs = rest[count:-3]
    attended, product, sems = rest[-3:]
    me = lax.axis_index("group")
    heads = lax.axis_size("head")
    my_head = lax.axis_index("head")
    row_local = rest[0].shape[0]
    share = own.shape[0]
    product[...] = multiply_rows(rest[:count], out_weight, attended, sems)
    for i, mask in enumerate(masks):
        done = len(masks) - count
        part = some if i < done else product
        at = i if i < done else i - done
        values = part[at * row_local : (at + 1) * row_local]
        row = (me ^ mask) * row_local
        ahead = lax.rem(row // share - my_head + heads, heads)
        place = pl.ds(pl.multiple_of(lax.rem(row, share), row_local), row_local)
        for k, out in enumerate([own, *theirs]):

            @pl.when(ahead == k)
            def _():
                out[place] = values.astype(out.dtype)


def project(gathered, out_weight, heads):
    masks = [mask for mask in gathered if mask % 2 == 0] + [mask for mask in gathered if mask % 2]
    some = len(masks) // 2
    row_local, width = gathered[0].shape
    columns = out_weight.shape[1]
    share = row_local * len(masks) // heads
    vmem = pl.BlockSpec(memory_space=pltpu.VMEM)
    hbm = pl.BlockSpec(memory_space=pl.ANY)

    def call(kernel, name, outs, blocks, extra, scratch):
        rows = row_local * len(blocks)
        return pl.pallas_call(
            kernel,
            out_shape=outs,
            in_specs=[vmem] * (1 + len(extra)) + [hbm] * len(blocks),
            out_specs=[vmem] * len(outs),
            scratch_shapes=[
                pltpu.VMEM((rows, width), jnp.bfloat16),
                *scratch,
                pltpu.SemaphoreType.DMA((len(blocks),)),
            ],
            compiler_params=pltpu.CompilerParams(vmem_limit_bytes=VMEM_LIMIT),
            cost_estimate=pl.CostEstimate(
                flops=2 * rows * width * columns, bytes_accessed=2 * out_weight.size, transcendentals=0
            ),
            name=name,
        )(out_weight, *extra, *blocks)

    out_weight = pltpu.with_memory_space_constraint(out_weight, pltpu.VMEM)
    first = [gathered[mask] for mask in masks[:some]]
    last = [gathered[mask] for mask in masks[some:]]
    (done,) = call(
        functools.partial(project_some_kernel, some), "project_some_rows",
        [jax.ShapeDtypeStruct((some * row_local, columns), jnp.float32)], first, [], [],
    )
    theirs = jax.ShapeDtypeStruct((share, columns), jnp.bfloat16)
    return call(
        functools.partial(project_rest_kernel, masks, len(last)), "project_rows",
        [jax.ShapeDtypeStruct((share, columns), jnp.float32)] + [theirs] * (heads - 1), last, [done],
        [pltpu.VMEM((len(last) * row_local, columns), jnp.float32)],
    )


def local(kv_pool, lengths, prefill_of, decode_of, row_request, queries, out_weight):
    row_local, query_width = queries.shape
    query_heads = queries.reshape(row_local, query_width // HD, HD)
    heads = lax.axis_size("head")

    dims = factors(lax.axis_size("group"))
    routes = page_rounds(dims)
    table = packed(lengths, prefill_of, decode_of, math.prod(dims))
    kv_pool = pltpu.with_memory_space_constraint(kv_pool, pltpu.HBM)
    early = prepare(dims, routes[:EARLY], table, kv_pool, False)
    received, *late = prepare(dims, routes[EARLY:], table, kv_pool, True, early[:1])
    arrived = [send_by(block, route, dims) for block, route in zip([*early, *late], routes)]
    rows = jnp.zeros(query_heads.shape, jnp.float32)
    for first in range(0, len(routes), WAVE):
        wave = slice(first, first + WAVE)
        last = first + WAVE >= len(routes)
        received, rows = settle(
            dims, routes[wave], first == 0, last, table, row_request, query_heads, rows, received, arrived[wave]
        )

    own, *theirs = project(gather_shards(rows), out_weight, heads)
    for ahead_by, part in enumerate(theirs, 1):
        pairs = [(h, (h + ahead_by) % heads) for h in range(heads)]
        own = own + lax.ppermute(part, "head", pairs).astype(jnp.float32)
    return (received, own.astype(jnp.bfloat16))


def solution(mesh):
    in_specs = (
        P("group", None, "head"),
        P(),
        P(),
        P(),
        P(),
        P("group", "head"),
        P("head", "group"),
    )
    assert mesh.shape["group"] & (mesh.shape["group"] - 1) == 0
    out_specs = (P("group", None, "head"), P("head", "group"))
    return jax.shard_map(local, mesh=mesh, in_specs=in_specs, out_specs=out_specs, check_vma=False)
```

```python
import functools
import math

import jax
import jax.numpy as jnp
from jax import lax
from jax.experimental import pallas as pl
from jax.experimental.pallas import tpu as pltpu
from jax.sharding import PartitionSpec as P

HD = 128
MAX_PAGES = 2
WAVE = 3
ROW_UNROLL = 4
EARLY = 2
VMEM_LIMIT = 20 * 1024 * 1024


def factors(groups):
    near = math.gcd(groups, 4)
    return groups // near, near


def uniform(step, swap, dims):
    return tuple(((z + step) % dims[0], swap) for z in range(dims[0]))


def page_rounds(dims):
    far, near = dims
    half = max(near // 2, 1)
    order = []
    for low in range(0, near, half):
        swaps = range(low, min(low + half, near))
        opening = [(1, n) for n in swaps] if low == 0 else [(z, n) for n in swaps for z in (1, 0)]
        rest = [(z, n) for z in range(2, far) for n in swaps]
        order += opening + ([(0, n) for n in swaps if n] if low == 0 else []) + rest
    return [uniform(z, n, dims) for z, n in order]


def reverse(route):
    sources = {to: (z, swap) for z, (to, swap) in enumerate(route)}
    return tuple(sources[z] for z in range(len(route)))


def routed(me, route, dims):
    near = dims[1]
    z = me // near
    to, swap = jnp.int32(route[0][0]), jnp.int32(route[0][1])
    for place in range(1, dims[0]):
        to = jnp.where(z == place, route[place][0], to)
        swap = jnp.where(z == place, route[place][1], swap)
    return to * near + (me % near ^ swap)


def send_by(array, route, dims):
    far, near = dims
    pairs = [
        (z * near + n, route[z][0] * near + (n ^ route[z][1])) for z in range(far) for n in range(near)
    ]
    return lax.ppermute(array, "group", pairs)


def swap(array, mask):
    groups = lax.axis_size("group")
    return lax.ppermute(array, "group", [(s, s ^ mask) for s in range(groups)])


def gather_shards(shard):
    held = {0: shard}
    mask = lax.axis_size("group") // 2
    while mask:
        held.update({done | mask: swap(array, mask) for done, array in held.items()})
        mask //= 2
    return held


def packed(lengths, prefill_of, decode_of, groups):
    bits = (groups - 1).bit_length()
    return (lengths << 2 * bits) | (prefill_of << bits) | decode_of


def unpacked(entry, groups):
    bits = (groups - 1).bit_length()
    mask = (1 << bits) - 1
    return entry >> 2 * bits, (entry >> bits) & mask, entry & mask


def prepare_kernel(dims, routes, own, table_hbm, pool, *rest):
    table, held, zero_page, start_of, count_of, table_sem, in_sems, out_sem = rest[-8:]
    received = rest[-8 - len(routes) - own : -8 - len(routes)]
    sends = rest[-8 - len(routes) : -8]
    me = lax.axis_index("group")
    groups = lax.axis_size("group")
    page_size = pool.shape[1]
    copy = pltpu.make_async_copy(table_hbm, table, table_sem)
    copy.start()
    for d in range(groups + 1):
        start_of[d] = 0
        count_of[d] = 0
    zero_page[...] = jnp.zeros_like(zero_page)
    copy.wait()

    def visit(r, running):
        length, home, destination = unpacked(table[r], groups)
        mine = home == me
        count = (length + page_size - 1) // page_size
        to = jnp.where(mine, destination, groups)
        start_of[to] = running
        count_of[to] = count
        return running + jnp.where(mine, count, 0)

    lax.fori_loop(0, table.shape[0], visit, jnp.int32(0), unroll=8)
    targets = [(routed(me, route, dims), send, 0) for route, send in zip(routes, sends)]
    if own:
        targets.append((me, received[0], me * MAX_PAGES))

    def each(do):
        for i, (to, target, base) in enumerate(targets):
            for page in range(MAX_PAGES):
                there = page < count_of[to]
                source = pool.at[jnp.where(there, start_of[to] + page, 0)]
                buffer, place = held.at[i, page], target.at[base + page]
                do(there, (source, buffer, in_sems.at[i, page]), (buffer, place, out_sem), (zero_page, place, out_sem))

    def fetch(there, load, store, blank):
        @pl.when(there)
        def _():
            pltpu.make_async_copy(*load).start()

        @pl.when(jnp.logical_not(there))
        def _():
            pltpu.make_async_copy(*blank).start()

    def forward(there, load, store, blank):
        @pl.when(there)
        def _():
            pltpu.make_async_copy(*load).wait()
            pltpu.make_async_copy(*store).start()

    def finish(there, load, store, blank):
        pltpu.make_async_copy(*blank).wait()

    each(fetch)
    each(forward)
    each(finish)


def prepare(dims, routes, table, pool, own, after=()):
    groups = lax.axis_size("group")
    page = pool.shape[1:]
    blocks = len(routes) + (1 if own else 0)
    hbm = pl.BlockSpec(memory_space=pl.ANY)
    block = jax.ShapeDtypeStruct((MAX_PAGES,) + page, pool.dtype)
    outs = [jax.ShapeDtypeStruct((groups * MAX_PAGES,) + page, pool.dtype)] * own + [block] * len(routes)
    operands = [table, pool, *after]
    return pl.pallas_call(
        functools.partial(prepare_kernel, dims, routes, own),
        out_shape=outs,
        in_specs=[hbm] * len(operands),
        out_specs=[hbm] * len(outs),
        scratch_shapes=[
            pltpu.SMEM(table.shape, jnp.int32),
            pltpu.VMEM((blocks, MAX_PAGES) + page, pool.dtype),
            pltpu.VMEM(page, pool.dtype),
            pltpu.SMEM((groups + 1,), jnp.int32),
            pltpu.SMEM((groups + 1,), jnp.int32),
            pltpu.SemaphoreType.DMA,
            pltpu.SemaphoreType.DMA((blocks, MAX_PAGES)),
            pltpu.SemaphoreType.DMA,
        ],
        compiler_params=pltpu.CompilerParams(vmem_limit_bytes=VMEM_LIMIT),
        cost_estimate=pl.CostEstimate(
            flops=0, bytes_accessed=4 * blocks * MAX_PAGES * math.prod(page), transcendentals=0
        ),
        name="outgoing_pages",
    )(*operands)


def attend_row(query, pages, length):
    first, second = pages
    kv_heads = first.shape[1] // (2 * HD)
    share = query.shape[0] // kv_heads
    scores = []
    for h in range(kv_heads):
        columns = slice(2 * h * HD, (2 * h + 1) * HD)
        keys = jnp.concatenate([first[:, columns], second[:, columns]], axis=0)
        every = lax.dot_general(
            query, keys, (((1,), (1,)), ((), ())), preferred_element_type=jnp.float32
        )
        scores.append(every[h * share : (h + 1) * share])
    score = jnp.concatenate(scores, axis=0) * (1.0 / math.sqrt(HD))
    live = lax.broadcasted_iota(jnp.int32, score.shape, 1) < length
    masked = jnp.where(live, score, -1e30)
    highest = jnp.max(masked, axis=1, keepdims=True)
    weights = jnp.where(live, jnp.exp(masked - highest), 0.0)
    totals = jnp.sum(weights, axis=1, keepdims=True)
    rounded = weights.astype(jnp.bfloat16)
    mixtures = []
    for h in range(kv_heads):
        columns = slice((2 * h + 1) * HD, (2 * h + 2) * HD)
        values = jnp.concatenate([first[:, columns], second[:, columns]], axis=0)
        every = jnp.dot(rounded, values, preferred_element_type=jnp.float32)
        mixtures.append(every[h * share : (h + 1) * share])
    return jnp.concatenate(mixtures, axis=0) / totals


def settle_kernel(dims, routes, own, last, table, row_request, queries, rows_in, received_in, *rest):
    blocks = rest[: len(routes)]
    received, out, rows, held, list_row, list_block, list_length, in_sems, out_sems = rest[len(routes) :]
    me = lax.axis_index("group")
    row_local, query_heads, _ = queries.shape
    mine = pl.ds(me * MAX_PAGES, MAX_PAGES)
    origins = [routed(me, reverse(route), dims) for route in routes]
    places = [pl.ds(origin * MAX_PAGES, MAX_PAGES) for origin in origins]
    sources = list(blocks) + ([received_in.at[mine]] if own else [])
    origins += [me] if own else []
    loads = [pltpu.make_async_copy(s, held.at[i], in_sems.at[i]) for i, s in enumerate(sources)]
    stores = [
        pltpu.make_async_copy(held.at[i], received.at[place], out_sems.at[i]) for i, place in enumerate(places)
    ]
    for load in loads:
        load.start()

    found = jnp.int32(0)
    for b in range(row_local):
        length, home, _ = unpacked(table[row_request[me * row_local + b]], math.prod(dims))
        block, match = jnp.int32(0), jnp.int32(0)
        for i, origin in enumerate(origins):
            block = jnp.where(home == origin, i, block)
            match = jnp.where(home == origin, 1, match)
        list_row[found] = b
        list_block[found] = block
        list_length[found] = length
        found = found + match
    for i in range(ROW_UNROLL):
        list_row[found + i] = row_local
        list_block[found + i] = 0
        list_length[found + i] = 1
    rows[:row_local] = rows_in[...]
    for load in loads:
        load.wait()
    for store in stores:
        store.start()

    @pl.loop(0, (found + ROW_UNROLL - 1) // ROW_UNROLL)
    def _(step):
        results = []
        for i in range(ROW_UNROLL):
            at = step * ROW_UNROLL + i
            query = queries[jnp.minimum(list_row[at], row_local - 1)]
            pages = [held[list_block[at], page] for page in range(MAX_PAGES)]
            results.append(attend_row(query, pages, list_length[at]))
        for i, result in enumerate(results):
            rows[list_row[step * ROW_UNROLL + i]] = result

    if last:
        for h in range(query_heads):
            out[:, h * HD : (h + 1) * HD] = rows[:row_local, h, :].astype(out.dtype)
    else:
        out[...] = rows[:row_local]
    for store in stores:
        store.wait()


def settle(dims, routes, own, last, table, row_request, queries, rows, received, blocks):
    row_local, query_heads, _ = queries.shape
    smem = pl.BlockSpec(memory_space=pltpu.SMEM)
    vmem = pl.BlockSpec(memory_space=pltpu.VMEM)
    hbm = pl.BlockSpec(memory_space=pl.ANY)
    count = len(blocks) + (1 if own else 0)
    if last:
        out = jax.ShapeDtypeStruct((row_local, query_heads * HD), jnp.bfloat16)
    else:
        out = jax.ShapeDtypeStruct(rows.shape, rows.dtype)
    return pl.pallas_call(
        functools.partial(settle_kernel, dims, routes, own, last),
        out_shape=[jax.ShapeDtypeStruct(received.shape, received.dtype), out],
        in_specs=[smem, smem, vmem, vmem, hbm] + [hbm] * len(blocks),
        out_specs=[hbm, vmem],
        scratch_shapes=[
            pltpu.VMEM((row_local + 1, query_heads, HD), jnp.float32),
            pltpu.VMEM((count, MAX_PAGES) + received.shape[1:], received.dtype),
            pltpu.SMEM((row_local + ROW_UNROLL,), jnp.int32),
            pltpu.SMEM((row_local + ROW_UNROLL,), jnp.int32),
            pltpu.SMEM((row_local + ROW_UNROLL,), jnp.int32),
            pltpu.SemaphoreType.DMA((count,)),
            pltpu.SemaphoreType.DMA((count,)),
        ],
        input_output_aliases={4: 0},
        compiler_params=pltpu.CompilerParams(vmem_limit_bytes=VMEM_LIMIT),
        cost_estimate=pl.CostEstimate(
            flops=1 << 30, bytes_accessed=4 * sum(b.size for b in blocks), transcendentals=1 << 18
        ),
        name="settle_pages",
    )(table, row_request, queries, rows, received, *blocks)


def multiply_rows(shards, out_weight, attended, sems):
    copies = []
    row_local = shards[0].shape[0]
    for i, shard in enumerate(shards):
        copies.append(pltpu.make_async_copy(shard, attended.at[pl.ds(i * row_local, row_local)], sems.at[i]))
        copies[-1].start()
    for copy in copies:
        copy.wait()
    return jnp.dot(attended[...], out_weight[...], preferred_element_type=jnp.float32)


def project_some_kernel(count, out_weight, *rest):
    out, attended, sems = rest[count:]
    out[...] = multiply_rows(rest[:count], out_weight, attended, sems)


def project_rest_kernel(masks, count, out_weight, some, *rest):
    own, *theirs = rest[count:-3]
    attended, product, sems = rest[-3:]
    me = lax.axis_index("group")
    heads = lax.axis_size("head")
    my_head = lax.axis_index("head")
    row_local = rest[0].shape[0]
    share = own.shape[0]
    product[...] = multiply_rows(rest[:count], out_weight, attended, sems)
    for i, mask in enumerate(masks):
        done = len(masks) - count
        part = some if i < done else product
        at = i if i < done else i - done
        values = part[at * row_local : (at + 1) * row_local]
        row = (me ^ mask) * row_local
        ahead = lax.rem(row // share - my_head + heads, heads)
        place = pl.ds(pl.multiple_of(lax.rem(row, share), row_local), row_local)
        for k, out in enumerate([own, *theirs]):

            @pl.when(ahead == k)
            def _():
                out[place] = values.astype(out.dtype)


def project(gathered, out_weight, heads):
    masks = [mask for mask in gathered if mask % 2 == 0] + [mask for mask in gathered if mask % 2]
    some = len(masks) // 2
    row_local, width = gathered[0].shape
    columns = out_weight.shape[1]
    share = row_local * len(masks) // heads
    vmem = pl.BlockSpec(memory_space=pltpu.VMEM)
    hbm = pl.BlockSpec(memory_space=pl.ANY)

    def call(kernel, name, outs, blocks, extra, scratch):
        rows = row_local * len(blocks)
        return pl.pallas_call(
            kernel,
            out_shape=outs,
            in_specs=[vmem] * (1 + len(extra)) + [hbm] * len(blocks),
            out_specs=[vmem] * len(outs),
            scratch_shapes=[
                pltpu.VMEM((rows, width), jnp.bfloat16),
                *scratch,
                pltpu.SemaphoreType.DMA((len(blocks),)),
            ],
            compiler_params=pltpu.CompilerParams(vmem_limit_bytes=VMEM_LIMIT),
            cost_estimate=pl.CostEstimate(
                flops=2 * rows * width * columns, bytes_accessed=2 * out_weight.size, transcendentals=0
            ),
            name=name,
        )(out_weight, *extra, *blocks)

    out_weight = pltpu.with_memory_space_constraint(out_weight, pltpu.VMEM)
    first = [gathered[mask] for mask in masks[:some]]
    last = [gathered[mask] for mask in masks[some:]]
    (done,) = call(
        functools.partial(project_some_kernel, some), "project_some_rows",
        [jax.ShapeDtypeStruct((some * row_local, columns), jnp.float32)], first, [], [],
    )
    theirs = jax.ShapeDtypeStruct((share, columns), jnp.bfloat16)
    return call(
        functools.partial(project_rest_kernel, masks, len(last)), "project_rows",
        [jax.ShapeDtypeStruct((share, columns), jnp.float32)] + [theirs] * (heads - 1), last, [done],
        [pltpu.VMEM((len(last) * row_local, columns), jnp.float32)],
    )


def local(kv_pool, lengths, prefill_of, decode_of, row_request, queries, out_weight):
    row_local, query_width = queries.shape
    query_heads = queries.reshape(row_local, query_width // HD, HD)
    heads = lax.axis_size("head")

    dims = factors(lax.axis_size("group"))
    routes = page_rounds(dims)
    table = packed(lengths, prefill_of, decode_of, math.prod(dims))
    kv_pool = pltpu.with_memory_space_constraint(kv_pool, pltpu.HBM)
    early = prepare(dims, routes[:EARLY], table, kv_pool, False)
    received, *late = prepare(dims, routes[EARLY:], table, kv_pool, True, early[:1])
    arrived = [send_by(block, route, dims) for block, route in zip([*early, *late], routes)]
    rows = jnp.zeros(query_heads.shape, jnp.float32)
    for first in range(0, len(routes), WAVE):
        wave = slice(first, first + WAVE)
        last = first + WAVE >= len(routes)
        received, rows = settle(
            dims, routes[wave], first == 0, last, table, row_request, query_heads, rows, received, arrived[wave]
        )

    own, *theirs = project(gather_shards(rows), out_weight, heads)
    for ahead_by, part in enumerate(theirs, 1):
        pairs = [(h, (h + ahead_by) % heads) for h in range(heads)]
        own = own + lax.ppermute(part, "head", pairs).astype(jnp.float32)
    return (received, own.astype(jnp.bfloat16))


def solution(mesh):
    in_specs = (
        P("group", None, "head"),
        P(),
        P(),
        P(),
        P(),
        P("group", "head"),
        P("head", "group"),
    )
    assert mesh.shape["group"] & (mesh.shape["group"] - 1) == 0
    out_specs = (P("group", None, "head"), P("head", "group"))
    return jax.shard_map(local, mesh=mesh, in_specs=in_specs, out_specs=out_specs, check_vma=False)
```

```python
import functools
import math

import jax
import jax.numpy as jnp
from jax import lax
from jax.experimental import pallas as pl
from jax.experimental.pallas import tpu as pltpu
from jax.sharding import PartitionSpec as P

HD = 128
MAX_PAGES = 2
WAVE = 3
ROW_UNROLL = 4
EARLY = 2
VMEM_LIMIT = 20 * 1024 * 1024


def factors(groups):
    near = math.gcd(groups, 4)
    return groups // near, near


def uniform(step, swap, dims):
    return tuple(((z + step) % dims[0], swap) for z in range(dims[0]))


def page_rounds(dims):
    far, near = dims
    half = max(near // 2, 1)
    order = []
    for low in range(0, near, half):
        swaps = range(low, min(low + half, near))
        opening = [(1, n) for n in swaps] if low == 0 else [(z, n) for z in (1, 0) for n in swaps]
        rest = [(z, n) for z in range(2, far) for n in swaps]
        order += opening + ([(0, n) for n in swaps if n] if low == 0 else []) + rest
    return [uniform(z, n, dims) for z, n in order]


def reverse(route):
    sources = {to: (z, swap) for z, (to, swap) in enumerate(route)}
    return tuple(sources[z] for z in range(len(route)))


def routed(me, route, dims):
    near = dims[1]
    z = me // near
    to, swap = jnp.int32(route[0][0]), jnp.int32(route[0][1])
    for place in range(1, dims[0]):
        to = jnp.where(z == place, route[place][0], to)
        swap = jnp.where(z == place, route[place][1], swap)
    return to * near + (me % near ^ swap)


def send_by(array, route, dims):
    far, near = dims
    pairs = [
        (z * near + n, route[z][0] * near + (n ^ route[z][1])) for z in range(far) for n in range(near)
    ]
    return lax.ppermute(array, "group", pairs)


def swap(array, mask):
    groups = lax.axis_size("group")
    return lax.ppermute(array, "group", [(s, s ^ mask) for s in range(groups)])


def gather_shards(shard):
    held = {0: shard}
    mask = lax.axis_size("group") // 2
    while mask:
        held.update({done | mask: swap(array, mask) for done, array in held.items()})
        mask //= 2
    return held


def packed(lengths, prefill_of, decode_of, groups):
    bits = (groups - 1).bit_length()
    return (lengths << 2 * bits) | (prefill_of << bits) | decode_of


def unpacked(entry, groups):
    bits = (groups - 1).bit_length()
    mask = (1 << bits) - 1
    return entry >> 2 * bits, (entry >> bits) & mask, entry & mask


def prepare_kernel(dims, routes, own, table_hbm, pool, *rest):
    table, held, zero_page, start_of, count_of, table_sem, in_sems, out_sem = rest[-8:]
    received = rest[-8 - len(routes) - own : -8 - len(routes)]
    sends = rest[-8 - len(routes) : -8]
    me = lax.axis_index("group")
    groups = lax.axis_size("group")
    page_size = pool.shape[1]
    copy = pltpu.make_async_copy(table_hbm, table, table_sem)
    copy.start()
    for d in range(groups + 1):
        start_of[d] = 0
        count_of[d] = 0
    zero_page[...] = jnp.zeros_like(zero_page)
    copy.wait()

    def visit(r, running):
        length, home, destination = unpacked(table[r], groups)
        mine = home == me
        count = (length + page_size - 1) // page_size
        to = jnp.where(mine, destination, groups)
        start_of[to] = running
        count_of[to] = count
        return running + jnp.where(mine, count, 0)

    lax.fori_loop(0, table.shape[0], visit, jnp.int32(0), unroll=8)
    targets = [(routed(me, route, dims), send, 0) for route, send in zip(routes, sends)]
    if own:
        targets.append((me, received[0], me * MAX_PAGES))

    def each(do):
        for i, (to, target, base) in enumerate(targets):
            for page in range(MAX_PAGES):
                there = page < count_of[to]
                source = pool.at[jnp.where(there, start_of[to] + page, 0)]
                buffer, place = held.at[i, page], target.at[base + page]
                do(there, (source, buffer, in_sems.at[i, page]), (buffer, place, out_sem), (zero_page, place, out_sem))

    def fetch(there, load, store, blank):
        @pl.when(there)
        def _():
            pltpu.make_async_copy(*load).start()

        @pl.when(jnp.logical_not(there))
        def _():
            pltpu.make_async_copy(*blank).start()

    def forward(there, load, store, blank):
        @pl.when(there)
        def _():
            pltpu.make_async_copy(*load).wait()
            pltpu.make_async_copy(*store).start()

    def finish(there, load, store, blank):
        pltpu.make_async_copy(*blank).wait()

    each(fetch)
    each(forward)
    each(finish)


def prepare(dims, routes, table, pool, own, after=()):
    groups = lax.axis_size("group")
    page = pool.shape[1:]
    blocks = len(routes) + (1 if own else 0)
    hbm = pl.BlockSpec(memory_space=pl.ANY)
    block = jax.ShapeDtypeStruct((MAX_PAGES,) + page, pool.dtype)
    outs = [jax.ShapeDtypeStruct((groups * MAX_PAGES,) + page, pool.dtype)] * own + [block] * len(routes)
    operands = [table, pool, *after]
    return pl.pallas_call(
        functools.partial(prepare_kernel, dims, routes, own),
        out_shape=outs,
        in_specs=[hbm] * len(operands),
        out_specs=[hbm] * len(outs),
        scratch_shapes=[
            pltpu.SMEM(table.shape, jnp.int32),
            pltpu.VMEM((blocks, MAX_PAGES) + page, pool.dtype),
            pltpu.VMEM(page, pool.dtype),
            pltpu.SMEM((groups + 1,), jnp.int32),
            pltpu.SMEM((groups + 1,), jnp.int32),
            pltpu.SemaphoreType.DMA,
            pltpu.SemaphoreType.DMA((blocks, MAX_PAGES)),
            pltpu.SemaphoreType.DMA,
        ],
        compiler_params=pltpu.CompilerParams(vmem_limit_bytes=VMEM_LIMIT),
        cost_estimate=pl.CostEstimate(
            flops=0, bytes_accessed=4 * blocks * MAX_PAGES * math.prod(page), transcendentals=0
        ),
        name="outgoing_pages",
    )(*operands)


def attend_row(query, pages, length):
    first, second = pages
    kv_heads = first.shape[1] // (2 * HD)
    share = query.shape[0] // kv_heads
    scores = []
    for h in range(kv_heads):
        columns = slice(2 * h * HD, (2 * h + 1) * HD)
        keys = jnp.concatenate([first[:, columns], second[:, columns]], axis=0)
        every = lax.dot_general(
            query, keys, (((1,), (1,)), ((), ())), preferred_element_type=jnp.float32
        )
        scores.append(every[h * share : (h + 1) * share])
    score = jnp.concatenate(scores, axis=0) * (1.0 / math.sqrt(HD))
    live = lax.broadcasted_iota(jnp.int32, score.shape, 1) < length
    masked = jnp.where(live, score, -1e30)
    highest = jnp.max(masked, axis=1, keepdims=True)
    weights = jnp.where(live, jnp.exp(masked - highest), 0.0)
    totals = jnp.sum(weights, axis=1, keepdims=True)
    rounded = weights.astype(jnp.bfloat16)
    mixtures = []
    for h in range(kv_heads):
        columns = slice((2 * h + 1) * HD, (2 * h + 2) * HD)
        values = jnp.concatenate([first[:, columns], second[:, columns]], axis=0)
        every = jnp.dot(rounded, values, preferred_element_type=jnp.float32)
        mixtures.append(every[h * share : (h + 1) * share])
    return jnp.concatenate(mixtures, axis=0) / totals


def settle_kernel(dims, routes, own, last, table, row_request, queries, rows_in, received_in, *rest):
    blocks = rest[: len(routes)]
    received, out, rows, held, list_row, list_block, list_length, in_sems, out_sems = rest[len(routes) :]
    me = lax.axis_index("group")
    row_local, query_heads, _ = queries.shape
    mine = pl.ds(me * MAX_PAGES, MAX_PAGES)
    origins = [routed(me, reverse(route), dims) for route in routes]
    places = [pl.ds(origin * MAX_PAGES, MAX_PAGES) for origin in origins]
    sources = list(blocks) + ([received_in.at[mine]] if own else [])
    origins += [me] if own else []
    loads = [pltpu.make_async_copy(s, held.at[i], in_sems.at[i]) for i, s in enumerate(sources)]
    stores = [
        pltpu.make_async_copy(held.at[i], received.at[place], out_sems.at[i]) for i, place in enumerate(places)
    ]
    for load in loads:
        load.start()

    found = jnp.int32(0)
    for b in range(row_local):
        length, home, _ = unpacked(table[row_request[me * row_local + b]], math.prod(dims))
        block, match = jnp.int32(0), jnp.int32(0)
        for i, origin in enumerate(origins):
            block = jnp.where(home == origin, i, block)
            match = jnp.where(home == origin, 1, match)
        list_row[found] = b
        list_block[found] = block
        list_length[found] = length
        found = found + match
    for i in range(ROW_UNROLL):
        list_row[found + i] = row_local
        list_block[found + i] = 0
        list_length[found + i] = 1
    rows[:row_local] = rows_in[...]
    for load in loads:
        load.wait()
    for store in stores:
        store.start()

    @pl.loop(0, (found + ROW_UNROLL - 1) // ROW_UNROLL)
    def _(step):
        results = []
        for i in range(ROW_UNROLL):
            at = step * ROW_UNROLL + i
            query = queries[jnp.minimum(list_row[at], row_local - 1)]
            pages = [held[list_block[at], page] for page in range(MAX_PAGES)]
            results.append(attend_row(query, pages, list_length[at]))
        for i, result in enumerate(results):
            rows[list_row[step * ROW_UNROLL + i]] = result

    if last:
        for h in range(query_heads):
            out[:, h * HD : (h + 1) * HD] = rows[:row_local, h, :].astype(out.dtype)
    else:
        out[...] = rows[:row_local]
    for store in stores:
        store.wait()


def settle(dims, routes, own, last, table, row_request, queries, rows, received, blocks):
    row_local, query_heads, _ = queries.shape
    smem = pl.BlockSpec(memory_space=pltpu.SMEM)
    vmem = pl.BlockSpec(memory_space=pltpu.VMEM)
    hbm = pl.BlockSpec(memory_space=pl.ANY)
    count = len(blocks) + (1 if own else 0)
    if last:
        out = jax.ShapeDtypeStruct((row_local, query_heads * HD), jnp.bfloat16)
    else:
        out = jax.ShapeDtypeStruct(rows.shape, rows.dtype)
    return pl.pallas_call(
        functools.partial(settle_kernel, dims, routes, own, last),
        out_shape=[jax.ShapeDtypeStruct(received.shape, received.dtype), out],
        in_specs=[smem, smem, vmem, vmem, hbm] + [hbm] * len(blocks),
        out_specs=[hbm, vmem],
        scratch_shapes=[
            pltpu.VMEM((row_local + 1, query_heads, HD), jnp.float32),
            pltpu.VMEM((count, MAX_PAGES) + received.shape[1:], received.dtype),
            pltpu.SMEM((row_local + ROW_UNROLL,), jnp.int32),
            pltpu.SMEM((row_local + ROW_UNROLL,), jnp.int32),
            pltpu.SMEM((row_local + ROW_UNROLL,), jnp.int32),
            pltpu.SemaphoreType.DMA((count,)),
            pltpu.SemaphoreType.DMA((count,)),
        ],
        input_output_aliases={4: 0},
        compiler_params=pltpu.CompilerParams(vmem_limit_bytes=VMEM_LIMIT),
        cost_estimate=pl.CostEstimate(
            flops=1 << 30, bytes_accessed=4 * sum(b.size for b in blocks), transcendentals=1 << 18
        ),
        name="settle_pages",
    )(table, row_request, queries, rows, received, *blocks)


def multiply_rows(shards, out_weight, attended, sems):
    copies = []
    row_local = shards[0].shape[0]
    for i, shard in enumerate(shards):
        copies.append(pltpu.make_async_copy(shard, attended.at[pl.ds(i * row_local, row_local)], sems.at[i]))
        copies[-1].start()
    for copy in copies:
        copy.wait()
    return jnp.dot(attended[...], out_weight[...], preferred_element_type=jnp.float32)


def project_some_kernel(count, out_weight, *rest):
    out, attended, sems = rest[count:]
    out[...] = multiply_rows(rest[:count], out_weight, attended, sems)


def project_rest_kernel(masks, count, out_weight, some, *rest):
    own, *theirs = rest[count:-3]
    attended, product, sems = rest[-3:]
    me = lax.axis_index("group")
    heads = lax.axis_size("head")
    my_head = lax.axis_index("head")
    row_local = rest[0].shape[0]
    share = own.shape[0]
    product[...] = multiply_rows(rest[:count], out_weight, attended, sems)
    for i, mask in enumerate(masks):
        done = len(masks) - count
        part = some if i < done else product
        at = i if i < done else i - done
        values = part[at * row_local : (at + 1) * row_local]
        row = (me ^ mask) * row_local
        ahead = lax.rem(row // share - my_head + heads, heads)
        place = pl.ds(pl.multiple_of(lax.rem(row, share), row_local), row_local)
        for k, out in enumerate([own, *theirs]):

            @pl.when(ahead == k)
            def _():
                out[place] = values.astype(out.dtype)


def project(gathered, out_weight, heads):
    masks = [mask for mask in gathered if mask % 2 == 0] + [mask for mask in gathered if mask % 2]
    some = len(masks) // 2
    row_local, width = gathered[0].shape
    columns = out_weight.shape[1]
    share = row_local * len(masks) // heads
    vmem = pl.BlockSpec(memory_space=pltpu.VMEM)
    hbm = pl.BlockSpec(memory_space=pl.ANY)

    def call(kernel, name, outs, blocks, extra, scratch):
        rows = row_local * len(blocks)
        return pl.pallas_call(
            kernel,
            out_shape=outs,
            in_specs=[vmem] * (1 + len(extra)) + [hbm] * len(blocks),
            out_specs=[vmem] * len(outs),
            scratch_shapes=[
                pltpu.VMEM((rows, width), jnp.bfloat16),
                *scratch,
                pltpu.SemaphoreType.DMA((len(blocks),)),
            ],
            compiler_params=pltpu.CompilerParams(vmem_limit_bytes=VMEM_LIMIT),
            cost_estimate=pl.CostEstimate(
                flops=2 * rows * width * columns, bytes_accessed=2 * out_weight.size, transcendentals=0
            ),
            name=name,
        )(out_weight, *extra, *blocks)

    out_weight = pltpu.with_memory_space_constraint(out_weight, pltpu.VMEM)
    first = [gathered[mask] for mask in masks[:some]]
    last = [gathered[mask] for mask in masks[some:]]
    (done,) = call(
        functools.partial(project_some_kernel, some), "project_some_rows",
        [jax.ShapeDtypeStruct((some * row_local, columns), jnp.float32)], first, [], [],
    )
    theirs = jax.ShapeDtypeStruct((share, columns), jnp.bfloat16)
    return call(
        functools.partial(project_rest_kernel, masks, len(last)), "project_rows",
        [jax.ShapeDtypeStruct((share, columns), jnp.float32)] + [theirs] * (heads - 1), last, [done],
        [pltpu.VMEM((len(last) * row_local, columns), jnp.float32)],
    )


def local(kv_pool, lengths, prefill_of, decode_of, row_request, queries, out_weight):
    row_local, query_width = queries.shape
    query_heads = queries.reshape(row_local, query_width // HD, HD)
    heads = lax.axis_size("head")

    dims = factors(lax.axis_size("group"))
    routes = page_rounds(dims)
    table = packed(lengths, prefill_of, decode_of, math.prod(dims))
    kv_pool = pltpu.with_memory_space_constraint(kv_pool, pltpu.HBM)
    early = prepare(dims, routes[:EARLY], table, kv_pool, False)
    received, *late = prepare(dims, routes[EARLY:], table, kv_pool, True, early[:1])
    arrived = [send_by(block, route, dims) for block, route in zip([*early, *late], routes)]
    rows = jnp.zeros(query_heads.shape, jnp.float32)
    for first in range(0, len(routes), WAVE):
        wave = slice(first, first + WAVE)
        last = first + WAVE >= len(routes)
        received, rows = settle(
            dims, routes[wave], first == 0, last, table, row_request, query_heads, rows, received, arrived[wave]
        )

    own, *theirs = project(gather_shards(rows), out_weight, heads)
    for ahead_by, part in enumerate(theirs, 1):
        pairs = [(h, (h + ahead_by) % heads) for h in range(heads)]
        own = own + lax.ppermute(part, "head", pairs).astype(jnp.float32)
    return (received, own.astype(jnp.bfloat16))


def solution(mesh):
    in_specs = (
        P("group", None, "head"),
        P(),
        P(),
        P(),
        P(),
        P("group", "head"),
        P("head", "group"),
    )
    assert mesh.shape["group"] & (mesh.shape["group"] - 1) == 0
    out_specs = (P("group", None, "head"), P("head", "group"))
    return jax.shard_map(local, mesh=mesh, in_specs=in_specs, out_specs=out_specs, check_vma=False)
```
